32 devices in a mesh: dp: 8 (over z, core), fsdp: 4 (over y, x).
Axes of the slice: x: 2, y: 2, z: 4, core: 2. Of those that a mesh axis runs over, the one named last changes fastest.
Arguments:
- units: bfloat16 [32, 1024, 1024], P(None, ('dp', 'fsdp')), may hold values from -6 to 6
- encoder: bfloat16 [32, 256, 1024], P(None, ('dp', 'fsdp')), may hold values from -6 to 6
- cotangent: bfloat16 [32, 1024, 1024], P(None, ('dp', 'fsdp')), may hold values from -6 to 6
- deal: int32 [32], replicated, may hold values from 0 to 31, each once
- lengths: int32 [32], replicated, may hold values from 256 to 1024, as said below
- enc_counts: int32 [32], replicated, may hold values from 128 to 256, as said below
- self_qkv: bfloat16 [3, 1024, 1024], P(None, ('dp', 'fsdp')), may hold values from -0.1875 to 0.1875
- self_out: bfloat16 [1024, 1024], P(('dp', 'fsdp')), may hold values from -1.5 to 1.5
- cross_qkv: bfloat16 [3, 1024, 1024], P(None, ('dp', 'fsdp')), may hold values from -0.1875 to 0.1875
- cross_out: bfloat16 [1024, 1024], P(('dp', 'fsdp')), may hold values from -1.5 to 1.5
- ffn_up: bfloat16 [1024, 4096], P(('dp', 'fsdp')), may hold values from -0.1875 to 0.1875
- ffn_down: bfloat16 [4096, 1024], P(('dp', 'fsdp')), may hold values from -0.125 to 0.125
- biases: bfloat16 [6, 1024], P(None, ('dp', 'fsdp')), may hold values from -1.75 to 1.75
- ffn_bias_up: bfloat16 [4096], P(('dp', 'fsdp')), may hold values from -1.75 to 1.75
- ffn_bias_down: bfloat16 [1024], P(('dp', 'fsdp')), may hold values from -1.75 to 1.75
- norm_gain: bfloat16 [3, 1024], P(None, ('dp', 'fsdp')), may hold values from 0.5 to 1.5
- norm_shift: bfloat16 [3, 1024], P(None, ('dp', 'fsdp')), may hold values from -1.75 to 1.75
Outputs:
- output: bfloat16 [32, 1024, 1024], P(None, ('dp', 'fsdp'))
- grad_units: bfloat16 [32, 1024, 1024], P(None, ('dp', 'fsdp'))
- grad_encoder: bfloat16 [32, 256, 1024], P(None, ('dp', 'fsdp'))
- grad_self_qkv: float32 [3, 1024, 1024], P(None, ('dp', 'fsdp'))
- grad_self_out: float32 [1024, 1024], P(('dp', 'fsdp'))
- grad_cross_qkv: float32 [3, 1024, 1024], P(None, ('dp', 'fsdp'))
- grad_cross_out: float32 [1024, 1024], P(('dp', 'fsdp'))
- grad_ffn_up: float32 [1024, 4096], P(('dp', 'fsdp'))
- grad_ffn_down: float32 [4096, 1024], P(('dp', 'fsdp'))
- grad_biases: float32 [6, 1024], P(None, ('dp', 'fsdp'))
- grad_ffn_bias_up: float32 [4096], P(('dp', 'fsdp'))
- grad_ffn_bias_down: float32 [1024], P(('dp', 'fsdp'))
- grad_norm_gain: float32 [3, 1024], P(None, ('dp', 'fsdp'))
- grad_norm_shift: float32 [3, 1024], P(None, ('dp', 'fsdp'))
The draws below stay inside these ranges and needn't reach their ends.
Inputs may be any that keep to these rules, and one draw needn't show every extreme that they name: `deal`: every sequence number appears exactly once. `lengths`: each sequence has at least 256 tokens, and some sequence fills all 1024 slots. `enc_counts`: each sequence has at least 128 encoder states, and some sequence fills all 256 slots.
All inputs are finite; a program needn't handle non-finite values.
Results may differ from the reference program's by a relative error of at most 0.02.
Values may be sent and summed in bfloat16 or wider, within the bound.
A program may use at most 384 MiB of HBM per device.

```python
import jax
import jax.numpy as jnp
from jax import lax

D = 1024
FF = 4096
HD = 64
LEN = 1024
ENC = 256
SEQS = 32


def draw_lengths(key, part):
    key = jax.random.fold_in(key, 11)
    first, second = jax.random.split(key)
    drawn = jax.random.randint(first, (SEQS,), LEN // 4, LEN + 1, dtype=jnp.int32)
    chosen = jax.random.randint(second, (), 0, SEQS, dtype=jnp.int32)
    return jnp.where(jnp.arange(SEQS, dtype=jnp.int32) == chosen, LEN, drawn).astype(jnp.int32)


def draw_enc_counts(key, part):
    key = jax.random.fold_in(key, 23)
    first, second = jax.random.split(key)
    drawn = jax.random.randint(first, (SEQS,), ENC // 2, ENC + 1, dtype=jnp.int32)
    chosen = jax.random.randint(second, (), 0, SEQS, dtype=jnp.int32)
    return jnp.where(jnp.arange(SEQS, dtype=jnp.int32) == chosen, ENC, drawn).astype(jnp.int32)


def level_of(own_key, dims, cuts, low, largest):
    level = 1.0
    for dim, shards_of in cuts:
        draws = jax.random.uniform(jax.random.fold_in(jax.random.fold_in(own_key, 6), dim), (shards_of,), jnp.float32, low / len(cuts), largest / len(cuts))
        level = level * jnp.repeat(jnp.exp(draws), dims[dim] // shards_of).reshape((-1,) + (1,) * (len(dims) - 1 - dim))
    return level


def normal_values(own_key, dims, scale, limit, cuts=(), held_as=jnp.bfloat16):
    values = jax.random.normal(own_key, dims, jnp.float32) * scale
    if len(cuts) > 0:
        values = level_of(own_key, dims, cuts, -0.22, 0.18) * values
    return jnp.clip(values, min=-limit, max=limit).astype(held_as)


def setup_inputs(seed: int = 0) -> dict:
    key_list = jax.random.split(jax.random.key(seed), 18)
    return {
        "units": normal_values(key_list[0], (SEQS, LEN, D), 1.0, 6.0, ((1, 32),)),
        "encoder": normal_values(key_list[1], (SEQS, ENC, D), 1.0, 6.0, ((1, 32),)),
        "cotangent": normal_values(key_list[2], (SEQS, LEN, D), 1.0, 6.0, ((1, 32),)),
        "deal": jax.random.permutation(key_list[3], SEQS).astype(jnp.int32),
        "lengths": draw_lengths(jax.random.fold_in(key_list[17], 71), 0),
        "enc_counts": draw_enc_counts(jax.random.fold_in(key_list[17], 71), 0),
        "self_qkv": normal_values(key_list[6], (3, D, D), D ** -0.5, 0.1875, ((1, 32),)),
        "self_out": normal_values(key_list[7], (D, D), (D // 64) ** -0.5, 1.5, ((0, 32),)),
        "cross_qkv": normal_values(key_list[8], (3, D, D), D ** -0.5, 0.1875, ((1, 32),)),
        "cross_out": normal_values(key_list[9], (D, D), (D // 64) ** -0.5, 1.5, ((0, 32),)),
        "ffn_up": normal_values(key_list[10], (D, FF), D ** -0.5, 0.1875, ((0, 32),)),
        "ffn_down": normal_values(key_list[11], (FF, D), (FF // 2) ** -0.5, 0.125, ((0, 32),)),
        "biases": normal_values(key_list[12], (6, D), 0.3, 1.75, ((1, 32),)),
        "ffn_bias_up": normal_values(key_list[13], (FF,), 0.3, 1.75, ((0, 32),)),
        "ffn_bias_down": normal_values(key_list[14], (D,), 0.3, 1.75, ((0, 32),)),
        "norm_gain": jnp.clip(1.0 + 0.1 * jax.random.normal(key_list[15], (3, D), jnp.float32), 0.5, 1.5).astype(jnp.bfloat16),
        "norm_shift": normal_values(key_list[16], (3, D), 0.3, 1.75, ((1, 32),)),
    }


@jax.custom_vjp
def low(v):
    return lax.optimization_barrier(v.astype(jnp.bfloat16)).astype(jnp.float32)

@jax.custom_vjp
def low_back(v):
    return v

def low_keep(v):
    return (low(v), None)

def low_pass(kept, grad):
    return (grad,)

def back_keep(v):
    return (v, None)

def back_low(kept, grad):
    return (low(grad),)
low.defvjp(low_keep, low_pass)
low_back.defvjp(back_keep, back_low)
EPSILON = 1e-05
SCALE = 0.125
NEGATIVE = -1e+30
HIGH = lax.Precision.HIGHEST

def matmul(left, right):
    return jnp.dot(left, right, precision=HIGH)

def layer_norm(value, gain, shift):
    mean = lax.optimization_barrier(jnp.mean(value, axis=-1, keepdims=True))
    centred = value - mean
    spread = lax.optimization_barrier(jnp.mean(centred * centred, axis=-1, keepdims=True))
    return centred * lax.rsqrt(spread + EPSILON) * gain + shift

def attend(query, keys, values, allowed):
    rows, width = query.shape
    heads = width // HD
    query3 = query.reshape(rows, heads, HD)
    keys3 = keys.reshape(keys.shape[0], heads, HD)
    values3 = values.reshape(values.shape[0], heads, HD)
    scores = jnp.einsum('qhd,khd->hqk', query3, keys3, precision=HIGH)
    scores = low_back(scores)
    scores = jnp.where(allowed[None], scores, NEGATIVE)
    top = lax.optimization_barrier(jnp.max(scores, axis=-1, keepdims=True))
    weights = jnp.exp(scores - top)
    probs = weights / lax.optimization_barrier(jnp.sum(weights, axis=-1, keepdims=True))
    mixed = jnp.einsum('hqk,khd->qhd', low(probs), values3, precision=HIGH)
    return mixed.reshape(rows, width)

def one_sequence(params, states, memory, length, count):
    self_qkv, self_out, cross_qkv, cross_out, ffn_up, ffn_down, biases, bias_up, bias_down, gains, shifts = params
    positions = jnp.arange(LEN, dtype=jnp.int32)
    enc_positions = jnp.arange(ENC, dtype=jnp.int32)
    valid = (positions < length).astype(jnp.float32)[:, None]
    causal = (positions[None, :] <= positions[:, None]) & (positions[None, :] < length)
    across = jnp.broadcast_to(enc_positions[None, :] < count, (LEN, ENC))
    normed = low(layer_norm(states, gains[0], shifts[0]))
    query = low(low_back((matmul(normed, self_qkv[0]) + biases[0]) * SCALE))
    keys = low(low_back(matmul(normed, self_qkv[1])))
    values = low(low_back(matmul(normed, self_qkv[2]) + biases[1]))
    mixed = low(low_back(attend(query, keys, values, causal)))
    first = states + low_back(matmul(mixed, self_out) + biases[2])
    normed = low(layer_norm(first, gains[1], shifts[1]))
    query = low(low_back((matmul(normed, cross_qkv[0]) + biases[3]) * SCALE))
    keys = low(low_back(matmul(memory, cross_qkv[1])))
    values = low(low_back(matmul(memory, cross_qkv[2]) + biases[4]))
    mixed = low(low_back(attend(query, keys, values, across)))
    second = first + low_back(matmul(mixed, cross_out) + biases[5])
    normed = low(layer_norm(second, gains[2], shifts[2]))
    hidden = low(jax.nn.gelu(low_back(matmul(normed, ffn_up) + bias_up), approximate=True))
    result = second + low_back(matmul(hidden, ffn_down) + bias_down)
    return result * valid

def reference(units, encoder, cotangent, deal, lengths, enc_counts, self_qkv, self_out, cross_qkv, cross_out, ffn_up, ffn_down, biases, ffn_bias_up, ffn_bias_down, norm_gain, norm_shift):
    params = (self_qkv.astype(jnp.float32), self_out.astype(jnp.float32), cross_qkv.astype(jnp.float32), cross_out.astype(jnp.float32), ffn_up.astype(jnp.float32), ffn_down.astype(jnp.float32), biases.astype(jnp.float32), ffn_bias_up.astype(jnp.float32), ffn_bias_down.astype(jnp.float32), norm_gain.astype(jnp.float32), norm_shift.astype(jnp.float32))
    inverse = jnp.zeros((SEQS,), jnp.int32).at[deal.astype(jnp.int32)].set(jnp.arange(SEQS, dtype=jnp.int32))
    seq_lengths = jnp.take(lengths, inverse).astype(jnp.int32)
    seq_counts = jnp.take(enc_counts, inverse).astype(jnp.int32)
    states = units.astype(jnp.float32)
    memory = encoder.astype(jnp.float32)
    checked = jax.checkpoint(one_sequence)

    def forward(weights, inputs, states_enc):

        def step(item):
            return checked(weights, item[0], item[1], item[2], item[3])
        return lax.map(step, (inputs, states_enc, seq_lengths, seq_counts))
    outputs, pullback = jax.vjp(forward, params, states, memory)
    grads, grad_states, grad_memory = pullback(cotangent.astype(jnp.float32))
    return (outputs.astype(jnp.bfloat16), grad_states.astype(jnp.bfloat16), grad_memory.astype(jnp.bfloat16), grads[0], grads[1], grads[2], grads[3], grads[4], grads[5], grads[6], grads[7], grads[8], grads[9], grads[10])
```

```python
import functools

import jax
import jax.numpy as jnp
from jax import lax
from jax.experimental import pallas as pl
from jax.experimental.pallas import tpu as pltpu
from jax.sharding import PartitionSpec as P

HD = 64
MESH = pl.DeviceIdType.MESH
ANY = pl.BlockSpec(memory_space=pl.ANY)


def ring_place(f, ring):
    half = ring // 2
    upper, rest = f // half, f % half
    return upper * half + rest + upper * (half - 1 - 2 * rest)


def position(depth, ring):
    d, f = lax.axis_index("dp"), lax.axis_index("fsdp")
    return d // 2, d % 2, ring_place(f, ring), f


def greet(z, c, right, left, depth, f):
    barrier = pltpu.get_barrier_semaphore()

    def hail(d, g):
        pl.semaphore_signal(barrier, inc=1, device_id=(d, g), device_id_type=MESH)

    for s in range(1, depth):
        hail((z + s) % depth * 2 + c, f)
    hail(z * 2 + c, right)
    hail(z * 2 + c, left)
    hail(z * 2 + 1 - c, f)
    pl.semaphore_wait(barrier, depth + 2)


def gather_kernel(depth, ring, units, n_in, *refs):
    shards, fulls = refs[:n_in], refs[n_in : 2 * n_in]
    local_sem, z_send, z_recv, r_send, r_recv, c_send, c_recv = refs[2 * n_in :]
    half = ring // 2
    z, c, place, f = position(depth, ring)
    right = ring_place((place + 1) % ring, ring)
    left = ring_place((place + ring - 1) % ring, ring)
    greet(z, c, right, left, depth, f)

    def own(u):
        which, lead, rows, cols = units[u]
        return shards[which].at[lead, rows, cols]

    def chunk(u, zs, cc, g):
        which, lead, rows, cols = units[u]
        return fulls[which].at[lead, zs, cc, g, rows, cols]

    def remote(src, dst, send, recv, d, g):
        return pltpu.make_async_remote_copy(
            src_ref=src, dst_ref=dst, send_sem=send, recv_sem=recv,
            device_id=(d, g), device_id_type=MESH,
        )

    def kept(u):
        return pltpu.make_async_copy(own(u), chunk(u, z, c, f), local_sem.at[u])

    def z_out(u, s):
        return remote(own(u), chunk(u, z, c, f), z_send.at[u, s], z_recv.at[u, s],
                      (z + s) % depth * 2 + c, f)

    def z_in(u, s):
        src = (z + depth - s) % depth
        return remote(own(u), chunk(u, src, c, f), z_send.at[u, s], z_recv.at[u, s],
                      (z + s) % depth * 2 + c, f)

    all_z, low_z, high_z = slice(0, depth), slice(0, depth // 2), slice(depth // 2, depth)

    def zs_of(t, way):
        return all_z if t < half else (low_z, high_z)[way]

    def ring_copy(u, t, way, incoming):
        back = t - 1 + incoming
        origin = (place + ring - back) % ring if way == 0 else (place + back) % ring
        piece = chunk(u, zs_of(t, way), c, ring_place(origin, ring))
        return remote(piece, piece, r_send.at[u, t - 1, way], r_recv.at[u, t - 1, way],
                      z * 2 + c, (right, left)[way])

    def core_copy(u, origin, slot, cc):
        piece = chunk(u, all_z, cc, ring_place(origin % ring, ring))
        return remote(piece, piece, c_send.at[u, slot], c_recv.at[u, slot], z * 2 + 1 - c, f)

    def start_z(u):
        kept(u).start()
        for s in range(1, depth):
            z_out(u, s).start()

    def end_z(u):
        kept(u).wait()
        for s in range(1, depth):
            z_in(u, s).wait_recv()

    def start_ring(u, t):
        for way in range(2):
            ring_copy(u, t, way, 0).start()

    def end_ring(u, t):
        for way in range(2):
            ring_copy(u, t, way, 1).wait_recv()

    def sets_after(t):
        if t == 0:
            return [0]
        return [t] if t == half else [ring - t, t]

    def start_core(u, t):
        for shift in sets_after(t):
            core_copy(u, place + shift, shift, c).start()

    count = len(units)
    ahead = 2
    for u in range(min(ahead, count)):
        start_z(u)
    for i in range(count + half):
        if i + ahead < count:
            start_z(i + ahead)
        if i < count:
            end_z(i)
            start_ring(i, 1)
            start_core(i, 0)
        for t in range(1, half + 1):
            u = i - t
            if 0 <= u < count:
                end_ring(u, t)
                if t < half:
                    start_ring(u, t + 1)
                start_core(u, t)
    for u in range(count):
        for s in range(1, depth):
            z_out(u, s).wait_send()
        for t in range(1, half + 1):
            for way in range(2):
                ring_copy(u, t, way, 0).wait_send()
        for shift in range(ring):
            core_copy(u, place + shift, shift, c).wait_send()
            core_copy(u, place + shift, shift, 1 - c).wait_recv()


def gather_weights(mesh, shards, units, ident):
    depth, ring = mesh.shape["dp"] // 2, mesh.shape["fsdp"]
    n = len(units)
    half = ring // 2
    dma = pltpu.SemaphoreType.DMA
    return pl.pallas_call(
        functools.partial(gather_kernel, depth, ring, units, len(shards)),
        out_shape=[
            jax.ShapeDtypeStruct((a.shape[0], depth, 2, ring) + a.shape[1:], a.dtype)
            for a in shards
        ],
        in_specs=[ANY] * len(shards),
        out_specs=[ANY] * len(shards),
        scratch_shapes=[
            dma((n,)),
            dma((n, depth)),
            dma((n, depth)),
            dma((n, half, 2)),
            dma((n, half, 2)),
            dma((n, ring)),
            dma((n, ring)),
        ],
        compiler_params=pltpu.CompilerParams(collective_id=ident, has_side_effects=True),
        cost_estimate=pl.CostEstimate(flops=120_000_000_000, bytes_accessed=2 * 33_554_432, transcendentals=0),
        name="gather_weights",
    )(*shards)


def scatter_kernel(depth, ring, units, n_in, *refs):
    fulls, outs = refs[:n_in], refs[n_in : 2 * n_in]
    mine, theirs, rhalf, rfull, zbuf = refs[2 * n_in : 2 * n_in + 5]
    l_sem, c_send, c_recv, r_send, r_recv, z_send, z_recv = refs[2 * n_in + 5 :]
    half = ring // 2
    hz = depth // 2
    z, c, place, f = position(depth, ring)
    right = ring_place((place + 1) % ring, ring)
    left = ring_place((place + ring - 1) % ring, ring)
    greet(z, c, right, left, depth, f)
    count = len(units)

    def chunk(u, cc):
        which, lead, rows, cols = units[u]
        return fulls[which].at[lead, slice(0, depth), cc, slice(0, ring), rows, cols]

    def remote(src, dst, send, recv, d, g):
        return pltpu.make_async_remote_copy(
            src_ref=src, dst_ref=dst, send_sem=send, recv_sem=recv,
            device_id=(d, g), device_id_type=MESH,
        )

    def load(u):
        return pltpu.make_async_copy(chunk(u, c), mine.at[u], l_sem.at[u])

    def core(u):
        return remote(chunk(u, 1 - c), theirs.at[u], c_send.at[u], c_recv.at[u], z * 2 + 1 - c, f)

    def dest(t, way):
        ahead = half - t + 1
        return ring_place((place + ahead) % ring if way == 0 else (place + ring - ahead) % ring, ring)

    def ring_copy(u, t, way):
        g = dest(t, way)
        if t == 1:
            src = mine.at[u, slice(0, hz) if way == 0 else slice(hz, depth), g]
            dst = rhalf.at[u, way]
        else:
            src = mine.at[u, slice(0, depth), g]
            dst = rfull.at[u, t - 2, way]
        return remote(src, dst, r_send.at[u, t - 1, way], r_recv.at[u, t - 1, way],
                      z * 2 + c, (right, left)[way])

    def z_copy(u, s):
        to = (z + s) % depth
        return remote(mine.at[u, to, f], zbuf.at[u, s - 1], z_send.at[u, s], z_recv.at[u, s],
                      to * 2 + c, f)

    def first_sum(u):
        core(u).wait_recv()
        load(u).wait()

        def body(i, carry):
            a, g = i // ring, i % ring
            mine[u, a, g] = (
                mine[u, a, g].astype(jnp.float32) + theirs[u, a, g].astype(jnp.float32)
            ).astype(mine.dtype)
            return carry

        lax.fori_loop(0, depth * ring, body, 0)
        for way in range(2):
            ring_copy(u, 1, way).start()

    def next_sum(u, t):
        for way in range(2):
            ring_copy(u, t, way).wait_recv()
        if t < half:
            for way in range(2):
                g = dest(t + 1, way)
                low = hz * way if t == 1 else 0
                many = hz if t == 1 else depth
                src = rhalf.at[u, way] if t == 1 else rfull.at[u, t - 2, way]

                def body(i, carry, g=g, low=low, src=src):
                    mine[u, low + i, g] = (
                        mine[u, low + i, g].astype(jnp.float32) + src[i].astype(jnp.float32)
                    ).astype(mine.dtype)
                    return carry

                lax.fori_loop(0, many, body, 0)
                ring_copy(u, t + 1, way).start()
        else:
            one, two = rfull.at[u, t - 2, 0], rfull.at[u, t - 2, 1]

            def body(i, carry):
                mine[u, i, f] = (
                    mine[u, i, f].astype(jnp.float32)
                    + one[i].astype(jnp.float32)
                    + two[i].astype(jnp.float32)
                ).astype(mine.dtype)
                return carry

            lax.fori_loop(0, depth, body, 0)
            for s in range(1, depth):
                z_copy(u, s).start()

    def last_sum(u):
        for s in range(1, depth):
            z_copy(u, s).wait_recv()
        which, lead, rows, cols = units[u]
        total = mine[u, z, f].astype(jnp.float32)
        for s in range(1, depth):
            total = total + zbuf[u, s - 1].astype(jnp.float32)
        outs[which][lead, rows, cols] = total

    for u in range(count):
        core(u).start()
        load(u).start()
    for i in range(count + half + 1):
        if i < count:
            first_sum(i)
        for t in range(1, half + 1):
            u = i - t
            if 0 <= u < count:
                next_sum(u, t)
        u = i - half - 1
        if 0 <= u < count:
            last_sum(u)
    for u in range(count):
        core(u).wait_send()
        for t in range(1, half + 1):
            for way in range(2):
                ring_copy(u, t, way).wait_send()
        for s in range(1, depth):
            z_copy(u, s).wait_send()


def scatter_grads(mesh, fulls, units, ident):
    depth, ring = mesh.shape["dp"] // 2, mesh.shape["fsdp"]
    n = len(units)
    half = ring // 2
    hz = depth // 2
    dma = pltpu.SemaphoreType.DMA
    low = fulls[0].dtype
    rows = fulls[0].shape[-2]
    cols = fulls[0].shape[-1]
    vm = pl.BlockSpec(memory_space=pltpu.VMEM)
    return pl.pallas_call(
        functools.partial(scatter_kernel, depth, ring, units, len(fulls)),
        out_shape=[jax.ShapeDtypeStruct((a.shape[0],) + a.shape[4:], jnp.float32) for a in fulls],
        in_specs=[ANY] * len(fulls),
        out_specs=[vm] * len(fulls),
        scratch_shapes=[
            pltpu.VMEM((n, depth, ring, rows, cols), low),
            pltpu.VMEM((n, depth, ring, rows, cols), low),
            pltpu.VMEM((n, 2, hz, rows, cols), low),
            pltpu.VMEM((n, half - 1, 2, depth, rows, cols), low),
            pltpu.VMEM((n, depth - 1, rows, cols), low),
            dma((n,)),
            dma((n,)),
            dma((n,)),
            dma((n, half, 2)),
            dma((n, half, 2)),
            dma((n, depth)),
            dma((n, depth)),
        ],
        compiler_params=pltpu.CompilerParams(
            collective_id=ident, has_side_effects=True, vmem_limit_bytes=60 * 2**20
        ),
        name="scatter_grads",
    )(*fulls)


def units_of(shards):
    base = shards[0].shape[1]
    wide = shards[0].shape[2]
    found = []
    for which, (lead, rows, cols) in enumerate(a.shape for a in shards):
        for l in range(lead):
            for r in range(rows // base):
                for k in range(cols // wide):
                    found.append((which, l, slice(r * base, (r + 1) * base), slice(k * wide, (k + 1) * wide)))
    return tuple(found)


def packed(parts):
    flat = jnp.concatenate([p.reshape(-1) for p in parts])
    size = -(-flat.shape[0] // 2048) * 2048
    return jnp.pad(flat, (0, size - flat.shape[0])).reshape(1, size // 128, 128)


def unpacked(flat, shapes):
    parts, at = [], 0
    for shape in shapes:
        size = 1
        for d in shape:
            size *= d
        part = flat[:, at : at + size].reshape((-1,) + shape)
        parts.append(jnp.moveaxis(part, 0, -2).reshape(shape[:-1] + (-1,)))
        at += size
    return parts


EPSILON = 1e-05
SCALE = 0.125
NEGATIVE = -1e30


def layer_norm(value, gain, shift):
    mean = jnp.mean(value, axis=-1, keepdims=True)
    centred = value - mean
    spread = jnp.mean(centred * centred, axis=-1, keepdims=True)
    return centred * lax.rsqrt(spread + EPSILON) * gain + shift


def smooth_gate(value):
    return jax.nn.gelu(value, approximate=True)


def product(left, right):
    return jnp.dot(left, right, preferred_element_type=jnp.float32)


def product_tn(left, right):
    return lax.dot_general(
        left, right, (((0,), (0,)), ((), ())), preferred_element_type=jnp.float32
    )


def product_nt(left, right):
    return lax.dot_general(
        left, right, (((1,), (1,)), ((), ())), preferred_element_type=jnp.float32
    )


def column_sum(value):
    return jnp.sum(value.astype(jnp.float32), axis=0)


def attend_forward(query, keys, values, allowed):
    rows, width = query.shape
    heads = width // HD
    block = min(512, rows)
    keys3 = keys.reshape(keys.shape[0], heads, HD)
    values3 = values.reshape(values.shape[0], heads, HD)

    def one_block(start):
        query3 = lax.dynamic_slice_in_dim(query, start, block, 0).reshape(block, heads, HD)
        scores = jnp.einsum("qhd,khd->hqk", query3, keys3, preferred_element_type=jnp.float32)
        scores = jnp.where(allowed(start, block)[None], scores, NEGATIVE)
        top = jnp.max(scores, axis=-1, keepdims=True)
        weights = jnp.exp(scores - top)
        total = jnp.sum(weights, axis=-1, keepdims=True)
        probs = (weights / total).astype(jnp.bfloat16)
        mixed = jnp.einsum("hqk,khd->qhd", probs, values3, preferred_element_type=jnp.float32)
        return (mixed.reshape(block, width), top + jnp.log(total))

    starts = jnp.arange(rows // block, dtype=jnp.int32) * block
    mixed, summary = lax.map(one_block, starts)
    return (mixed.reshape(rows, width).astype(jnp.bfloat16), summary)


def attend_backward(query, keys, values, summary, grad_mixed, allowed):
    rows, width = query.shape
    heads = width // HD
    block = min(512, rows)
    count = keys.shape[0]
    keys3 = keys.reshape(count, heads, HD)
    values3 = values.reshape(count, heads, HD)

    def one_block(carry, item):
        grad_keys, grad_values = carry
        start, logsum = item
        query3 = lax.dynamic_slice_in_dim(query, start, block, 0).reshape(block, heads, HD)
        grad3 = lax.dynamic_slice_in_dim(grad_mixed, start, block, 0).reshape(block, heads, HD)
        scores = jnp.einsum("qhd,khd->hqk", query3, keys3, preferred_element_type=jnp.float32)
        scores = jnp.where(allowed(start, block)[None], scores, NEGATIVE)
        probs = jnp.exp(scores - logsum)
        grad_values = grad_values + jnp.einsum(
            "hqk,qhd->khd", probs.astype(jnp.bfloat16), grad3, preferred_element_type=jnp.float32
        )
        grad_probs = jnp.einsum("qhd,khd->hqk", grad3, values3, preferred_element_type=jnp.float32)
        inner = jnp.sum(probs * grad_probs, axis=-1, keepdims=True)
        grad_scores = (probs * (grad_probs - inner)).astype(jnp.bfloat16)
        grad_query = jnp.einsum(
            "hqk,khd->qhd", grad_scores, keys3, preferred_element_type=jnp.float32
        )
        grad_keys = grad_keys + jnp.einsum(
            "hqk,qhd->khd", grad_scores, query3, preferred_element_type=jnp.float32
        )
        return ((grad_keys, grad_values), grad_query.reshape(block, width))

    empty = jnp.zeros((count, heads, HD), jnp.float32)
    starts = jnp.arange(rows // block, dtype=jnp.int32) * block
    (grad_keys, grad_values), grad_query = lax.scan(one_block, (empty, empty), (starts, summary))
    return (
        grad_query.reshape(rows, width).astype(jnp.bfloat16),
        grad_keys.reshape(count, width).astype(jnp.bfloat16),
        grad_values.reshape(count, width).astype(jnp.bfloat16),
    )


def per_device(
    mesh,
    units,
    encoder,
    cotangent,
    deal,
    lengths,
    enc_counts,
    self_qkv,
    self_out,
    cross_qkv,
    cross_out,
    ffn_up,
    ffn_down,
    biases,
    ffn_bias_up,
    ffn_bias_down,
    norm_gain,
    norm_shift,
):
    slots = deal.shape[0]
    inverse = jnp.zeros((slots,), jnp.int32).at[deal].set(jnp.arange(slots, dtype=jnp.int32))
    dealt_units = jnp.take(units, deal, axis=0)
    dealt_enc = jnp.take(encoder, deal, axis=0)
    dealt_cot = jnp.take(cotangent, deal, axis=0)
    arrived, enc_arrived, cot_arrived = (
        lax.all_to_all(dealt_units, ("dp", "fsdp"), split_axis=0, concat_axis=1, tiled=True),
        lax.all_to_all(dealt_enc, ("dp", "fsdp"), split_axis=0, concat_axis=1, tiled=True),
        lax.all_to_all(dealt_cot, ("dp", "fsdp"), split_axis=0, concat_axis=1, tiled=True),
    )
    place = lax.axis_index(("dp", "fsdp"))
    length = lax.dynamic_index_in_dim(lengths, place, keepdims=False)
    enc_count = lax.dynamic_index_in_dim(enc_counts, place, keepdims=False)
    states = arrived[0].astype(jnp.float32)
    memory = enc_arrived[0]
    rows = states.shape[0]
    positions = jnp.arange(rows, dtype=jnp.int32)
    enc_positions = jnp.arange(memory.shape[0], dtype=jnp.int32)
    valid = (positions < length).astype(jnp.float32)[:, None]
    grad_out = cot_arrived[0].astype(jnp.float32) * valid

    def causal(start, block):
        query_rows = start + jnp.arange(block, dtype=jnp.int32)
        return (positions[None, :] <= query_rows[:, None]) & (positions[None, :] < length)

    def across(start, block):
        return jnp.broadcast_to(enc_positions[None, :] < enc_count, (block, enc_positions.shape[0]))

    big = [self_qkv, self_out[None], cross_qkv, cross_out[None], ffn_up[None], ffn_down[None]]
    units_list = units_of(big)
    small = (biases, ffn_bias_up, ffn_bias_down, norm_gain, norm_shift)
    little = packed(small)
    little_unit = ((len(big), 0, slice(0, little.shape[1]), slice(0, 128)),)
    gathered = gather_weights(mesh, big + [little], little_unit + units_list, 0)
    s_qkv, s_out, c_qkv, c_out, w_up, w_down = (
        g.reshape(g.shape[0], -1, g.shape[-1]) for g in gathered[:6]
    )
    s_out, c_out, w_up, w_down = s_out[0], c_out[0], w_up[0], w_down[0]
    weights = [None] * 6 + unpacked(gathered[6].reshape(slots, -1), [p.shape for p in small])
    bias_rows = weights[6].astype(jnp.float32)
    bias_up = weights[7].astype(jnp.float32)
    bias_down = weights[8].astype(jnp.float32)
    gains = weights[9].astype(jnp.float32)
    shifts = weights[10].astype(jnp.float32)
    normed0 = layer_norm(states, gains[0], shifts[0]).astype(jnp.bfloat16)
    query0 = ((product(normed0, s_qkv[0]) + bias_rows[0]) * SCALE).astype(jnp.bfloat16)
    keys0 = product(normed0, s_qkv[1]).astype(jnp.bfloat16)
    values0 = (product(normed0, s_qkv[2]) + bias_rows[1]).astype(jnp.bfloat16)
    mixed0, summary0 = attend_forward(query0, keys0, values0, causal)
    first = states + (product(mixed0, s_out) + bias_rows[2])
    normed1 = layer_norm(first, gains[1], shifts[1]).astype(jnp.bfloat16)
    query1 = ((product(normed1, c_qkv[0]) + bias_rows[3]) * SCALE).astype(jnp.bfloat16)
    keys1 = product(memory, c_qkv[1]).astype(jnp.bfloat16)
    values1 = (product(memory, c_qkv[2]) + bias_rows[4]).astype(jnp.bfloat16)
    mixed1, summary1 = attend_forward(query1, keys1, values1, across)
    second = first + (product(mixed1, c_out) + bias_rows[5])
    normed2 = layer_norm(second, gains[2], shifts[2]).astype(jnp.bfloat16)
    before = product(normed2, w_up) + bias_up
    activated, pull_gate = jax.vjp(smooth_gate, before)
    hidden = activated.astype(jnp.bfloat16)
    result = (second + (product(hidden, w_down) + bias_down)) * valid
    branch = grad_out.astype(jnp.bfloat16)
    grad_down = product_tn(hidden, branch)
    grad_bias_down = column_sum(branch)
    grad_hidden = product_nt(branch, w_down)
    grad_before = pull_gate(grad_hidden)[0].astype(jnp.bfloat16)
    grad_up = product_tn(normed2, grad_before)
    grad_bias_up = column_sum(grad_before)
    _, pull_two = jax.vjp(layer_norm, second, gains[2], shifts[2])
    grad_from, grad_gain_two, grad_shift_two = pull_two(product_nt(grad_before, w_up))
    grad_second = grad_out + grad_from
    branch = grad_second.astype(jnp.bfloat16)
    grad_cross_out = product_tn(mixed1, branch)
    grad_bias_five = column_sum(branch)
    grad_mixed = product_nt(branch, c_out).astype(jnp.bfloat16)
    grad_query, grad_keys, grad_values = attend_backward(
        query1, keys1, values1, summary1, grad_mixed, across
    )
    grad_cross_query = product_tn(normed1, grad_query) * SCALE
    grad_bias_three = column_sum(grad_query) * SCALE
    grad_cross_keys = product_tn(memory, grad_keys)
    grad_cross_values = product_tn(memory, grad_values)
    grad_bias_four = column_sum(grad_values)
    grad_memory = product_nt(grad_keys, c_qkv[1]) + product_nt(grad_values, c_qkv[2])
    _, pull_one = jax.vjp(layer_norm, first, gains[1], shifts[1])
    grad_from, grad_gain_one, grad_shift_one = pull_one(product_nt(grad_query, c_qkv[0]) * SCALE)
    grad_first = grad_second + grad_from
    branch = grad_first.astype(jnp.bfloat16)
    grad_self_out = product_tn(mixed0, branch)
    grad_bias_two = column_sum(branch)
    grad_mixed = product_nt(branch, s_out).astype(jnp.bfloat16)
    grad_query, grad_keys, grad_values = attend_backward(
        query0, keys0, values0, summary0, grad_mixed, causal
    )
    grad_self_query = product_tn(normed0, grad_query) * SCALE
    grad_bias_zero = column_sum(grad_query) * SCALE
    grad_self_keys = product_tn(normed0, grad_keys)
    grad_self_values = product_tn(normed0, grad_values)
    grad_bias_one = column_sum(grad_values)
    grad_normed = (
        product_nt(grad_query, s_qkv[0]) * SCALE
        + product_nt(grad_keys, s_qkv[1])
        + product_nt(grad_values, s_qkv[2])
    )
    _, pull_zero = jax.vjp(layer_norm, states, gains[0], shifts[0])
    grad_from, grad_gain_zero, grad_shift_zero = pull_zero(grad_normed)
    grad_states = grad_first + grad_from
    grad_self_qkv = jnp.stack([grad_self_query, grad_self_keys, grad_self_values])
    grad_cross_qkv = jnp.stack([grad_cross_query, grad_cross_keys, grad_cross_values])
    grad_biases = jnp.stack(
        [
            grad_bias_zero,
            grad_bias_one,
            grad_bias_two,
            grad_bias_three,
            grad_bias_four,
            grad_bias_five,
        ]
    )
    grad_gains = jnp.stack([grad_gain_zero, grad_gain_one, grad_gain_two])
    grad_shifts = jnp.stack([grad_shift_zero, grad_shift_one, grad_shift_two])
    low = jnp.bfloat16
    depth, ring = mesh.shape["dp"] // 2, mesh.shape["fsdp"]

    def cut(g):
        g = g if g.ndim == 3 else g[None]
        return g.astype(low).reshape(g.shape[0], depth, 2, ring, -1, g.shape[-1])

    big_grads = [cut(g) for g in (grad_self_qkv, grad_self_out, grad_cross_qkv, grad_cross_out, grad_up, grad_down)]
    sums = scatter_grads(mesh, big_grads, units_list, 1)
    small_grads = (grad_biases, grad_bias_up, grad_bias_down, grad_gains, grad_shifts)
    terms = jnp.concatenate(
        [
            jnp.moveaxis(g.reshape(g.shape[:-1] + (slots, -1)), -2, 0).reshape(slots, -1)
            for g in small_grads
        ],
        axis=1,
    )
    terms = lax.all_to_all(terms, ("dp", "fsdp"), split_axis=0, concat_axis=0, tiled=True)
    flat = jnp.sum(terms, axis=0)
    small_sums, at = [], 0
    for p in small:
        small_sums.append(flat[at : at + p.size].reshape(p.shape))
        at += p.size
    summed = (sums[0], sums[1][0], sums[2], sums[3][0], sums[4][0], sums[5][0], *small_sums)
    leaving = result.astype(jnp.bfloat16)[None]
    grad_leaving = grad_states.astype(jnp.bfloat16)[None]
    grad_enc_leaving = grad_memory.astype(jnp.bfloat16)[None]
    returned, grad_returned, grad_enc_returned = (
        lax.all_to_all(leaving, ("dp", "fsdp"), split_axis=1, concat_axis=0, tiled=True),
        lax.all_to_all(grad_leaving, ("dp", "fsdp"), split_axis=1, concat_axis=0, tiled=True),
        lax.all_to_all(grad_enc_leaving, ("dp", "fsdp"), split_axis=1, concat_axis=0, tiled=True),
    )
    returned = jnp.take(returned, inverse, axis=0)
    grad_returned = jnp.take(grad_returned, inverse, axis=0)
    grad_enc_returned = jnp.take(grad_enc_returned, inverse, axis=0)
    return (
        returned,
        grad_returned,
        grad_enc_returned,
        summed[0],
        summed[1],
        summed[2],
        summed[3],
        summed[4],
        summed[5],
        summed[6],
        summed[7],
        summed[8],
        summed[9],
        summed[10],
    )


def solution(mesh):
    placed = (
        P(None, ("dp", "fsdp"), None),
        P(None, ("dp", "fsdp"), None),
        P(None, ("dp", "fsdp"), None),
        P(),
        P(),
        P(),
        P(None, ("dp", "fsdp"), None),
        P(("dp", "fsdp"), None),
        P(None, ("dp", "fsdp"), None),
        P(("dp", "fsdp"), None),
        P(("dp", "fsdp"), None),
        P(("dp", "fsdp"), None),
        P(None, ("dp", "fsdp")),
        P(("dp", "fsdp")),
        P(("dp", "fsdp")),
        P(None, ("dp", "fsdp")),
        P(None, ("dp", "fsdp")),
    )
    return jax.shard_map(
        functools.partial(per_device, mesh),
        mesh=mesh,
        in_specs=placed,
        out_specs=(
            P(None, ("dp", "fsdp"), None),
            P(None, ("dp", "fsdp"), None),
            P(None, ("dp", "fsdp"), None),
            P(None, ("dp", "fsdp"), None),
            P(("dp", "fsdp"), None),
            P(None, ("dp", "fsdp"), None),
            P(("dp", "fsdp"), None),
            P(("dp", "fsdp"), None),
            P(("dp", "fsdp"), None),
            P(None, ("dp", "fsdp")),
            P(("dp", "fsdp")),
            P(("dp", "fsdp")),
            P(None, ("dp", "fsdp")),
            P(None, ("dp", "fsdp")),
        ),
        check_vma=False,
    )
```

```python
import functools

import jax
import jax.numpy as jnp
from jax import lax
from jax.experimental import pallas as pl
from jax.experimental.pallas import tpu as pltpu
from jax.sharding import PartitionSpec as P

HD = 64
EPSILON = 1e-05
SCALE = 0.125
NEGATIVE = -1e30
MESH = pl.DeviceIdType.MESH
ANY = pl.BlockSpec(memory_space=pl.ANY)


def ring_place(f, ring):
    half = ring // 2
    upper, rest = f // half, f % half
    return upper * half + rest + upper * (half - 1 - 2 * rest)


def position(depth, ring):
    d, f = lax.axis_index("dp"), lax.axis_index("fsdp")
    return d // 2, d % 2, ring_place(f, ring), f


def greet(z, c, right, left, depth, f):
    barrier = pltpu.get_barrier_semaphore()

    def hail(d, g):
        pl.semaphore_signal(barrier, inc=1, device_id=(d, g), device_id_type=MESH)

    for s in range(1, depth):
        hail((z + s) % depth * 2 + c, f)
    hail(z * 2 + c, right)
    hail(z * 2 + c, left)
    hail(z * 2 + 1 - c, f)
    pl.semaphore_wait(barrier, depth + 2)


def gather_kernel(depth, ring, units, n_in, *refs):
    shards, fulls = refs[:n_in], refs[n_in : 2 * n_in]
    local_sem, z_send, z_recv, r_send, r_recv, c_send, c_recv = refs[2 * n_in :]
    half = ring // 2
    z, c, place, f = position(depth, ring)
    right = ring_place((place + 1) % ring, ring)
    left = ring_place((place + ring - 1) % ring, ring)
    greet(z, c, right, left, depth, f)

    def own(u):
        which, lead, rows, cols = units[u]
        return shards[which].at[lead, rows, cols]

    def chunk(u, zs, cc, g):
        which, lead, rows, cols = units[u]
        return fulls[which].at[lead, zs, cc, g, rows, cols]

    def remote(src, dst, send, recv, d, g):
        return pltpu.make_async_remote_copy(
            src_ref=src, dst_ref=dst, send_sem=send, recv_sem=recv,
            device_id=(d, g), device_id_type=MESH,
        )

    def kept(u):
        return pltpu.make_async_copy(own(u), chunk(u, z, c, f), local_sem.at[u])

    def z_out(u, s):
        return remote(own(u), chunk(u, z, c, f), z_send.at[u, s], z_recv.at[u, s],
                      (z + s) % depth * 2 + c, f)

    def z_in(u, s):
        src = (z + depth - s) % depth
        return remote(own(u), chunk(u, src, c, f), z_send.at[u, s], z_recv.at[u, s],
                      (z + s) % depth * 2 + c, f)

    all_z, low_z, high_z = slice(0, depth), slice(0, depth // 2), slice(depth // 2, depth)

    def zs_of(t, way):
        return all_z if t < half else (low_z, high_z)[way]

    def ring_copy(u, t, way, incoming):
        back = t - 1 + incoming
        origin = (place + ring - back) % ring if way == 0 else (place + back) % ring
        piece = chunk(u, zs_of(t, way), c, ring_place(origin, ring))
        return remote(piece, piece, r_send.at[u, t - 1, way], r_recv.at[u, t - 1, way],
                      z * 2 + c, (right, left)[way])

    def core_copy(u, origin, slot, cc):
        piece = chunk(u, all_z, cc, ring_place(origin % ring, ring))
        return remote(piece, piece, c_send.at[u, slot], c_recv.at[u, slot], z * 2 + 1 - c, f)

    def start_z(u):
        kept(u).start()
        for s in range(1, depth):
            z_out(u, s).start()

    def end_z(u):
        kept(u).wait()
        for s in range(1, depth):
            z_in(u, s).wait_recv()

    def start_ring(u, t):
        for way in range(2):
            ring_copy(u, t, way, 0).start()

    def end_ring(u, t):
        for way in range(2):
            ring_copy(u, t, way, 1).wait_recv()

    def sets_after(t):
        if t == 0:
            return [0]
        return [t] if t == half else [ring - t, t]

    def start_core(u, t):
        for shift in sets_after(t):
            core_copy(u, place + shift, shift, c).start()

    count = len(units)
    ahead = 2
    for u in range(min(ahead, count)):
        start_z(u)
    for i in range(count + half):
        if i + ahead < count:
            start_z(i + ahead)
        if i < count:
            end_z(i)
            start_ring(i, 1)
            start_core(i, 0)
        for t in range(1, half + 1):
            u = i - t
            if 0 <= u < count:
                end_ring(u, t)
                if t < half:
                    start_ring(u, t + 1)
                start_core(u, t)
    for u in range(count):
        for s in range(1, depth):
            z_out(u, s).wait_send()
        for t in range(1, half + 1):
            for way in range(2):
                ring_copy(u, t, way, 0).wait_send()
        for shift in range(ring):
            core_copy(u, place + shift, shift, c).wait_send()
            core_copy(u, place + shift, shift, 1 - c).wait_recv()


def gather_weights(mesh, shards, units, ident):
    depth, ring = mesh.shape["dp"] // 2, mesh.shape["fsdp"]
    n = len(units)
    half = ring // 2
    dma = pltpu.SemaphoreType.DMA
    return pl.pallas_call(
        functools.partial(gather_kernel, depth, ring, units, len(shards)),
        out_shape=[
            jax.ShapeDtypeStruct((a.shape[0], depth, 2, ring) + a.shape[1:], a.dtype)
            for a in shards
        ],
        in_specs=[ANY] * len(shards),
        out_specs=[ANY] * len(shards),
        scratch_shapes=[
            dma((n,)),
            dma((n, depth)),
            dma((n, depth)),
            dma((n, half, 2)),
            dma((n, half, 2)),
            dma((n, ring)),
            dma((n, ring)),
        ],
        compiler_params=pltpu.CompilerParams(collective_id=ident, has_side_effects=True),
        cost_estimate=pl.CostEstimate(flops=120_000_000_000, bytes_accessed=2 * 33_554_432, transcendentals=0),
        name="gather_weights",
    )(*shards)


def scatter_kernel(depth, ring, units, n_in, *refs):
    fulls, outs = refs[:n_in], refs[n_in : 2 * n_in]
    mine, theirs, rhalf, rfull, zbuf = refs[2 * n_in : 2 * n_in + 5]
    l_sem, c_send, c_recv, r_send, r_recv, z_send, z_recv = refs[2 * n_in + 5 :]
    half = ring // 2
    hz = depth // 2
    z, c, place, f = position(depth, ring)
    right = ring_place((place + 1) % ring, ring)
    left = ring_place((place + ring - 1) % ring, ring)
    greet(z, c, right, left, depth, f)
    count = len(units)

    def chunk(u, cc):
        which, lead, rows, cols = units[u]
        return fulls[which].at[lead, slice(0, depth), cc, slice(0, ring), rows, cols]

    def remote(src, dst, send, recv, d, g):
        return pltpu.make_async_remote_copy(
            src_ref=src, dst_ref=dst, send_sem=send, recv_sem=recv,
            device_id=(d, g), device_id_type=MESH,
        )

    def load(u):
        return pltpu.make_async_copy(chunk(u, c), mine.at[u], l_sem.at[u])

    def core(u):
        return remote(chunk(u, 1 - c), theirs.at[u], c_send.at[u], c_recv.at[u], z * 2 + 1 - c, f)

    def dest(t, way):
        ahead = half - t + 1
        return ring_place((place + ahead) % ring if way == 0 else (place + ring - ahead) % ring, ring)

    def ring_copy(u, t, way):
        g = dest(t, way)
        if t == 1:
            src = mine.at[u, slice(0, hz) if way == 0 else slice(hz, depth), g]
            dst = rhalf.at[u, way]
        else:
            src = mine.at[u, slice(0, depth), g]
            dst = rfull.at[u, t - 2, way]
        return remote(src, dst, r_send.at[u, t - 1, way], r_recv.at[u, t - 1, way],
                      z * 2 + c, (right, left)[way])

    def z_copy(u, s):
        to = (z + s) % depth
        return remote(mine.at[u, to, f], zbuf.at[u, s - 1], z_send.at[u, s], z_recv.at[u, s],
                      to * 2 + c, f)

    def first_sum(u):
        core(u).wait_recv()
        load(u).wait()

        def body(i, carry):
            a, g = i // ring, i % ring
            mine[u, a, g] = (
                mine[u, a, g].astype(jnp.float32) + theirs[u, a, g].astype(jnp.float32)
            ).astype(mine.dtype)
            return carry

        lax.fori_loop(0, depth * ring, body, 0)
        for way in range(2):
            ring_copy(u, 1, way).start()

    def next_sum(u, t):
        for way in range(2):
            ring_copy(u, t, way).wait_recv()
        if t < half:
            for way in range(2):
                g = dest(t + 1, way)
                low = hz * way if t == 1 else 0
                many = hz if t == 1 else depth
                src = rhalf.at[u, way] if t == 1 else rfull.at[u, t - 2, way]

                def body(i, carry, g=g, low=low, src=src):
                    mine[u, low + i, g] = (
                        mine[u, low + i, g].astype(jnp.float32) + src[i].astype(jnp.float32)
                    ).astype(mine.dtype)
                    return carry

                lax.fori_loop(0, many, body, 0)
                ring_copy(u, t + 1, way).start()
        else:
            one, two = rfull.at[u, t - 2, 0], rfull.at[u, t - 2, 1]

            def body(i, carry):
                mine[u, i, f] = (
                    mine[u, i, f].astype(jnp.float32)
                    + one[i].astype(jnp.float32)
                    + two[i].astype(jnp.float32)
                ).astype(mine.dtype)
                return carry

            lax.fori_loop(0, depth, body, 0)
            for s in range(1, depth):
                z_copy(u, s).start()

    def last_sum(u):
        for s in range(1, depth):
            z_copy(u, s).wait_recv()
        which, lead, rows, cols = units[u]
        total = mine[u, z, f].astype(jnp.float32)
        for s in range(1, depth):
            total = total + zbuf[u, s - 1].astype(jnp.float32)
        outs[which][lead, rows, cols] = total

    for u in range(count):
        core(u).start()
        load(u).start()
    for i in range(count + half + 1):
        if i < count:
            first_sum(i)
        for t in range(1, half + 1):
            u = i - t
            if 0 <= u < count:
                next_sum(u, t)
        u = i - half - 1
        if 0 <= u < count:
            last_sum(u)
    for u in range(count):
        core(u).wait_send()
        for t in range(1, half + 1):
            for way in range(2):
                ring_copy(u, t, way).wait_send()
        for s in range(1, depth):
            z_copy(u, s).wait_send()


def scatter_grads(mesh, fulls, units, ident):
    depth, ring = mesh.shape["dp"] // 2, mesh.shape["fsdp"]
    n = len(units)
    half = ring // 2
    hz = depth // 2
    dma = pltpu.SemaphoreType.DMA
    low = fulls[0].dtype
    rows = fulls[0].shape[-2]
    cols = fulls[0].shape[-1]
    vm = pl.BlockSpec(memory_space=pltpu.VMEM)
    return pl.pallas_call(
        functools.partial(scatter_kernel, depth, ring, units, len(fulls)),
        out_shape=[jax.ShapeDtypeStruct((a.shape[0],) + a.shape[4:], jnp.float32) for a in fulls],
        in_specs=[ANY] * len(fulls),
        out_specs=[vm] * len(fulls),
        scratch_shapes=[
            pltpu.VMEM((n, depth, ring, rows, cols), low),
            pltpu.VMEM((n, depth, ring, rows, cols), low),
            pltpu.VMEM((n, 2, hz, rows, cols), low),
            pltpu.VMEM((n, half - 1, 2, depth, rows, cols), low),
            pltpu.VMEM((n, depth - 1, rows, cols), low),
            dma((n,)),
            dma((n,)),
            dma((n,)),
            dma((n, half, 2)),
            dma((n, half, 2)),
            dma((n, depth)),
            dma((n, depth)),
        ],
        compiler_params=pltpu.CompilerParams(
            collective_id=ident, has_side_effects=True, vmem_limit_bytes=60 * 2**20
        ),
        name="scatter_grads",
    )(*fulls)


NN = (((1,), (0,)), ((), ()))
NT = (((1,), (1,)), ((), ()))
TN = (((0,), (0,)), ((), ()))
LOW = jnp.bfloat16
FULL = jnp.float32
SMEM = pl.BlockSpec(memory_space=pltpu.SMEM)
VMEM = pl.BlockSpec(memory_space=pltpu.VMEM)
PAIR = 2 * HD
ROOM = 60 * 2**20


def dot(left, right, how):
    return lax.dot_general(left, right, how, preferred_element_type=FULL)


def calls(kernel, name, flops, moved, **kw):
    return pl.pallas_call(
        kernel,
        name=name,
        compiler_params=pltpu.CompilerParams(vmem_limit_bytes=ROOM),
        cost_estimate=pl.CostEstimate(flops=int(flops), bytes_accessed=int(moved), transcendentals=0),
        **kw,
    )


def whole(shape):
    return pl.BlockSpec(shape, lambda *_: (0,) * len(shape))


def normal(x):
    mean = jnp.mean(x, axis=-1, keepdims=True)
    centred = x - mean
    rstd = lax.rsqrt(jnp.mean(centred * centred, axis=-1, keepdims=True) + EPSILON)
    return centred * rstd, rstd


def normal_back(hat, rstd, grad, gain):
    scaled = grad * gain
    lean = jnp.mean(scaled, axis=-1, keepdims=True)
    tilt = jnp.mean(scaled * hat, axis=-1, keepdims=True)
    back = rstd * (scaled - lean - hat * tilt)
    return back, jnp.sum(grad * hat, axis=0, keepdims=True), jnp.sum(grad, axis=0, keepdims=True)


def add_row(ref, value, first):
    @pl.when(first)
    def _():
        ref[...] = value

    @pl.when(jnp.logical_not(first))
    def _():
        ref[...] += value


GAIN, SHIFT, DOWN = 6, 9, 12


def qkv_kernel(x_ref, w_ref, p_ref, a_ref, o_ref):
    j = pl.program_id(0)

    @pl.when(j == 0)
    def _():
        hat, _ = normal(x_ref[...].astype(FULL))
        a_ref[...] = (hat * p_ref[GAIN : GAIN + 1] + p_ref[SHIFT : SHIFT + 1]).astype(LOW)

    bias = jnp.where(j == 0, p_ref[0:1], jnp.where(j == 2, p_ref[1:2], 0.0))
    scale = jnp.where(j == 0, SCALE, 1.0)
    o_ref[0] = ((dot(a_ref[...], w_ref[0], NN) + bias) * scale).astype(LOW)


def project_qkv(x, w, p):
    rows, width = x.shape
    return calls(
        qkv_kernel,
        "project_qkv",
        6 * rows * width * width,
        2 * (5 * rows * width + 3 * width * width),
        grid=(3,),
        in_specs=[whole(x.shape), pl.BlockSpec((1, width, width), lambda j: (j, 0, 0)), whole(p.shape)],
        out_specs=[whole(x.shape), pl.BlockSpec((1, rows, width), lambda j: (j, 0, 0))],
        out_shape=[
            jax.ShapeDtypeStruct((rows, width), LOW),
            jax.ShapeDtypeStruct((3, rows, width), LOW),
        ],
    )(x, w, p)


def lanes(shape):
    return lax.broadcasted_iota(jnp.int32, shape, len(shape) - 1)


def rows_of(shape):
    return lax.broadcasted_iota(jnp.int32, shape, 0)


def head_mask(head):
    return jnp.where(lanes((1, PAIR)) // HD == head, 1.0, 0.0).astype(LOW)


def attend_kernel(causal, tile, n_ref, q_ref, k_ref, v_ref, o_ref, l_ref):
    h = pl.program_id(0)
    q, k, v = q_ref[0], k_ref[0], v_ref[0]
    queries, count = q.shape[0], k.shape[0]
    lane_k = lanes((count, PAIR))
    shut = jnp.where((lane_k == 0) & (rows_of((count, PAIR)) >= n_ref[0]), NEGATIVE, 0.0).astype(LOW)
    first = jnp.where(lanes((queries, PAIR)) == 0, 1.0, 0.0).astype(LOW)
    ones = jnp.ones((count, PAIR), LOW)
    wide_q = jnp.concatenate([q, first], axis=1)
    spots = lanes((tile, PAIR))
    keys = [jnp.concatenate([k * head_mask(head), shut], axis=1) for head in range(2)]
    values = [jnp.concatenate([v * head_mask(head), ones], axis=1) for head in range(2)]
    for i in range(queries // tile):
        at = slice(i * tile, (i + 1) * tile)
        seen = (i + 1) * tile if causal else count
        mixed = jnp.zeros((tile, PAIR), FULL)

        @pl.when(h == 0)
        def _():
            l_ref[at] = jnp.zeros((tile, PAIR), FULL)

        kept = l_ref[at]
        for head in range(2):
            scores = dot(wide_q[at], keys[head][:seen], NT)
            if causal:
                square = (tile, tile)
                last = jnp.where(lanes(square) <= rows_of(square), scores[:, seen - tile :], NEGATIVE)
                scores = last if seen == tile else jnp.concatenate([scores[:, : seen - tile], last], axis=1)
            top = jnp.max(scores, axis=1, keepdims=True)
            weights = jnp.exp(scores - top).astype(LOW)
            sums = dot(weights, values[head][:seen], NN)
            total = sums[:, PAIR:]
            mixed = mixed + sums[:, :PAIR] / total
            kept = jnp.where(spots == 2 * h + head, top + jnp.log(total), kept)
        o_ref[at] = mixed.astype(LOW)
        l_ref[at] = kept


def attend(length, q, k, v, causal, name):
    rows, width = q[0].shape[1:]
    count = k[0].shape[1]
    tile = 256

    def cut(pair):
        part = pair[1]
        return pl.BlockSpec((1, pair[0].shape[1], PAIR), lambda h: (part, 0, h))

    return calls(
        functools.partial(attend_kernel, causal, tile),
        name,
        4 * 4 * rows * count * width // (2 if causal else 1),
        2 * (2 * rows + 2 * count) * width,
        grid=(width // PAIR,),
        in_specs=[SMEM, cut(q), cut(k), cut(v)],
        out_specs=[pl.BlockSpec((rows, PAIR), lambda h: (0, h)), whole((rows, PAIR))],
        out_shape=[
            jax.ShapeDtypeStruct((rows, width), LOW),
            jax.ShapeDtypeStruct((rows, PAIR), FULL),
        ],
    )(length, q[0], k[0], v[0])


def thirds(x):
    one = x.astype(LOW).astype(FULL)
    two = (x - one).astype(LOW).astype(FULL)
    return one, two, x - one - two


def attend_back_kernel(causal, tile, n_ref, q_ref, k_ref, v_ref, o_ref, g_ref, l_ref, dq_ref, dkv_ref, acc_ref):
    h = pl.program_id(0)
    q, k, v, grad = q_ref[0], k_ref[0], v_ref[0], g_ref[...]
    queries, count = q.shape[0], k.shape[0]
    lane_k, lane_q = lanes((count, PAIR)), lanes((queries, PAIR))
    shut = jnp.where(rows_of((count, PAIR)) >= n_ref[0], NEGATIVE, 0.0)
    open_k = jnp.where(lane_k == 0, shut, jnp.where(lane_k < 4, 1.0, 0.0)).astype(LOW)
    open_v = jnp.where(lane_k < 3, 1.0, 0.0).astype(LOW)
    product = grad.astype(FULL) * o_ref[...].astype(FULL)
    acc_ref[...] = jnp.zeros_like(acc_ref)
    heads = []
    for head in range(2):
        mask = head_mask(head)
        level = jnp.sum(jnp.where(lane_q == 2 * h + head, l_ref[...], 0.0), axis=1, keepdims=True)
        one, two, three = thirds(-level)
        tail = jnp.where(lane_q == 0, 1.0, jnp.where(lane_q == 1, one, jnp.where(lane_q == 2, two, jnp.where(lane_q == 3, three, 0.0))))
        wide_q = jnp.concatenate([q, tail.astype(LOW)], axis=1)
        inner = jnp.sum(jnp.where(lane_q // HD == head, product, 0.0), axis=1, keepdims=True)
        one, two, three = thirds(-inner)
        tail = jnp.where(lane_q == 0, one, jnp.where(lane_q == 1, two, jnp.where(lane_q == 2, three, 0.0)))
        wide_g = jnp.concatenate([grad, tail.astype(LOW)], axis=1)
        heads.append(
            (
                wide_q,
                wide_g,
                jnp.concatenate([k * mask, open_k], axis=1),
                jnp.concatenate([v * mask, open_v], axis=1),
                q * mask,
                grad * mask,
                k * mask,
            )
        )
    for i in range(count // tile):
        at = slice(i * tile, (i + 1) * tile)
        low = i * tile if causal else 0
        grad_k = jnp.zeros((tile, PAIR), FULL)
        grad_v = jnp.zeros((tile, PAIR), FULL)
        for wide_q, wide_g, wide_k, wide_v, q_one, g_one, k_one in heads:
            scores = dot(wide_k[at], wide_q[low:], NT)
            if causal:
                square = (tile, tile)
                near = jnp.where(rows_of(square) <= lanes(square), scores[:, :tile], NEGATIVE)
                scores = near if low + tile == queries else jnp.concatenate([near, scores[:, tile:]], axis=1)
            probs = jnp.exp(scores)
            slope = (probs * dot(wide_v[at], wide_g[low:], NT)).astype(LOW)
            grad_v = grad_v + dot(probs.astype(LOW), g_one[low:], NN)
            grad_k = grad_k + dot(slope, q_one[low:], NN)
            acc_ref[low:] += dot(slope, k_one[at], TN)
        dkv_ref[0, at] = grad_k.astype(LOW)
        dkv_ref[1, at] = grad_v.astype(LOW)
    dq_ref[...] = acc_ref[...].astype(LOW)


def attend_back(length, q, k, v, mixed, grad, level, causal, name):
    rows, width = mixed.shape
    count = k[0].shape[1]
    tile = 256

    def cut(pair):
        part = pair[1]
        return pl.BlockSpec((1, pair[0].shape[1], PAIR), lambda h: (part, 0, h))

    column = pl.BlockSpec((rows, PAIR), lambda h: (0, h))
    return calls(
        functools.partial(attend_back_kernel, causal, tile),
        name,
        4 * 10 * rows * count * width // (2 if causal else 1),
        2 * (4 * rows + 4 * count) * width,
        grid=(width // PAIR,),
        in_specs=[SMEM, cut(q), cut(k), cut(v), column, column, whole((rows, PAIR))],
        out_specs=[column, pl.BlockSpec((2, count, PAIR), lambda h: (0, 0, h))],
        out_shape=[
            jax.ShapeDtypeStruct((rows, width), LOW),
            jax.ShapeDtypeStruct((2, count, width), LOW),
        ],
        scratch_shapes=[pltpu.VMEM((rows, PAIR), FULL)],
    )(length, q[0], k[0], v[0], mixed, grad, level)


def middle_kernel(x_ref, o_ref, wo_ref, wq_ref, p_ref, x1_ref, a_ref, q_ref):
    x1 = x_ref[...].astype(FULL) + (dot(o_ref[...], wo_ref[...], NN) + p_ref[2:3])
    x1_ref[...] = x1
    hat, _ = normal(x1)
    a = (hat * p_ref[GAIN + 1 : GAIN + 2] + p_ref[SHIFT + 1 : SHIFT + 2]).astype(LOW)
    a_ref[...] = a
    q_ref[0] = ((dot(a, wq_ref[0], NN) + p_ref[3:4]) * SCALE).astype(LOW)


def middle(x, mixed, w_out, w_cross, p, tile=256):
    rows, width = x.shape
    part = pl.BlockSpec((tile, width), lambda i: (i, 0))
    return calls(
        middle_kernel,
        "middle",
        4 * rows * width * width,
        12 * rows * width + 4 * width * width,
        grid=(rows // tile,),
        in_specs=[part, part, whole(w_out.shape), whole((1, width, width)), whole(p.shape)],
        out_specs=[part, part, pl.BlockSpec((1, tile, width), lambda i: (0, i, 0))],
        out_shape=[
            jax.ShapeDtypeStruct((rows, width), FULL),
            jax.ShapeDtypeStruct((rows, width), LOW),
            jax.ShapeDtypeStruct((1, rows, width), LOW),
        ],
    )(x, mixed, w_out, w_cross, p)


def memory_kernel(e_ref, w_ref, p_ref, o_ref):
    j = pl.program_id(0)
    o_ref[0] = (dot(e_ref[...], w_ref[0], NN) + jnp.where(j == 1, p_ref[4:5], 0.0)).astype(LOW)


def project_memory(memory, w_cross, p):
    count, width = memory.shape
    return calls(
        memory_kernel,
        "project_memory",
        4 * count * width * width,
        4 * width * width,
        grid=(2,),
        in_specs=[whole(memory.shape), pl.BlockSpec((1, width, width), lambda j: (j + 1, 0, 0)), whole(p.shape)],
        out_specs=pl.BlockSpec((1, count, width), lambda j: (j, 0, 0)),
        out_shape=jax.ShapeDtypeStruct((2, count, width), LOW),
    )(memory, w_cross, p)


CUBIC = 0.044715
ROOT = 0.7978845608028654


def feed_kernel(
    step_cols, n_ref, x1_ref, o_ref, g_ref, wc_hbm, wu_hbm, wd_hbm, p_ref, bu_ref,
    out_ref, r_ref, du_ref, a_ref, g3_ref, dx_ref, g2_ref, do_ref,
    sum_up, sum_down, sum_five, sum_gain, sum_shift,
    wc_ref, wu_ref, wd_ref, slope_ref, sems,
):
    i = pl.program_id(0)
    first = i == 0
    tile, width = x1_ref.shape
    inner = wu_ref.shape[1]
    loads = [
        pltpu.make_async_copy(a, b, sems.at[s])
        for s, (a, b) in enumerate(((wc_hbm, wc_ref), (wu_hbm, wu_ref), (wd_hbm, wd_ref)))
    ]

    @pl.when(first)
    def _():
        for load in loads:
            load.start()
        loads[0].wait()

    valid = jnp.where(i * tile + rows_of((tile, 1)) < n_ref[0], 1.0, 0.0)
    x2 = x1_ref[...] + (dot(o_ref[...], wc_ref[...], NN) + p_ref[5:6])
    hat, rstd = normal(x2)
    gain = p_ref[GAIN + 2 : GAIN + 3]
    a_ref[...] = (hat * gain + p_ref[SHIFT + 2 : SHIFT + 3]).astype(LOW)

    @pl.when(first)
    def _():
        loads[1].wait()
        loads[2].wait()

    total = x2 + p_ref[DOWN : DOWN + 1]
    for j in range(inner // step_cols):
        cols = slice(j * step_cols, (j + 1) * step_cols)
        u = dot(a_ref[...], wu_ref[:, cols], NN) + bu_ref[:, cols]
        square = u * u
        t = jnp.tanh(ROOT * (u * (1.0 + CUBIC * square)))
        half = 0.5 * (1.0 + t)
        r = (u * half).astype(LOW)
        r_ref[:, cols] = r
        slope = half + 0.5 * u * (1.0 - t * t) * (ROOT * (1.0 + 3.0 * CUBIC * square))
        slope_ref[:, cols] = slope.astype(LOW)
        total = total + dot(r, wd_ref[cols, :], NN)
    out_ref[...] = (total * valid).astype(LOW)
    grad_out = g_ref[...].astype(FULL) * valid
    g3 = grad_out.astype(LOW)
    g3_ref[...] = g3
    grad = jnp.zeros((tile, width), FULL)
    for j in range(inner // step_cols):
        cols = slice(j * step_cols, (j + 1) * step_cols)
        du = (dot(g3, wd_ref[cols, :], NT) * slope_ref[:, cols].astype(FULL)).astype(LOW)
        du_ref[:, cols] = du
        line = jnp.sum(du.astype(FULL), axis=0, keepdims=True)

        @pl.when(first)
        def _():
            sum_up[:, cols] = line

        @pl.when(jnp.logical_not(first))
        def _():
            sum_up[:, cols] += line

        grad = grad + dot(du, wu_ref[:, cols], NT)
    back, lines, shifts = normal_back(hat, rstd, grad, gain)
    dx2 = grad_out + back
    dx_ref[...] = dx2
    g2 = dx2.astype(LOW)
    g2_ref[...] = g2
    do_ref[...] = dot(g2, wc_ref[...], NT).astype(LOW)
    add_row(sum_down, jnp.sum(g3.astype(FULL), axis=0, keepdims=True), first)
    add_row(sum_five, jnp.sum(g2.astype(FULL), axis=0, keepdims=True), first)
    add_row(sum_gain, lines, first)
    add_row(sum_shift, shifts, first)


def feed(length, x1, mixed, cotangent, w_cross, w_up, w_down, p, bias_up, tile=256):
    rows, width = x1.shape
    inner = w_up.shape[1]
    part = pl.BlockSpec((tile, width), lambda i: (i, 0))
    broad = pl.BlockSpec((tile, inner), lambda i: (i, 0))
    low = jax.ShapeDtypeStruct((rows, width), LOW)
    wide = jax.ShapeDtypeStruct((rows, inner), LOW)
    line = jax.ShapeDtypeStruct((1, width), FULL)
    return calls(
        functools.partial(feed_kernel, min(1024, inner)),
        "feed",
        2 * rows * width * (4 * inner + 2 * width),
        2 * rows * (9 * width + 2 * inner) + 4 * inner * width,
        grid=(rows // tile,),
        in_specs=[SMEM, part, part, part, ANY, ANY, ANY, whole(p.shape), whole(bias_up.shape)],
        out_specs=[part, broad, broad, part, part, part, part, part, whole((1, inner))] + [whole((1, width))] * 4,
        out_shape=[low, wide, wide, low, low, jax.ShapeDtypeStruct((rows, width), FULL), low, low,
                   jax.ShapeDtypeStruct((1, inner), FULL), line, line, line, line],
        scratch_shapes=[
            pltpu.VMEM(w_cross.shape, LOW),
            pltpu.VMEM(w_up.shape, LOW),
            pltpu.VMEM(w_down.shape, LOW),
            pltpu.VMEM((tile, inner), LOW),
            pltpu.SemaphoreType.DMA((3,)),
        ],
    )(length, x1, mixed, cotangent, w_cross, w_up, w_down, p, bias_up)


def weight_kernel(scale, a_ref, b_ref, o_ref):
    value = dot(a_ref[...], b_ref[...], TN)
    o_ref[...] = (value if scale == 1.0 else value * scale).astype(LOW)


def weight_grad(a, b, name, scale=1.0):
    rows, n = a.shape
    m = b.shape[1]
    block = min(1024, n)
    cols = min(1024, m)
    return calls(
        functools.partial(weight_kernel, scale),
        name,
        2 * rows * n * m,
        2 * (rows * (n + m) + n * m),
        grid=(n // block, m // cols),
        in_specs=[pl.BlockSpec((rows, block), lambda i, j: (0, i)), pl.BlockSpec((rows, cols), lambda i, j: (0, j))],
        out_specs=pl.BlockSpec((block, cols), lambda i, j: (i, j)),
        out_shape=jax.ShapeDtypeStruct((n, m), LOW),
    )(a, b)


def cross_back_kernel(x1_ref, dq_ref, dx2_ref, wq_ref, wo_ref, p_ref, dx_ref, g1_ref, do_ref,
                      sum_q, sum_out, sum_gain, sum_shift):
    first = pl.program_id(0) == 0
    grad = dot(dq_ref[...], wq_ref[0], NT) * SCALE
    hat, rstd = normal(x1_ref[...])
    back, lines, shifts = normal_back(hat, rstd, grad, p_ref[GAIN + 1 : GAIN + 2])
    dx1 = dx2_ref[...] + back
    dx_ref[...] = dx1
    g1 = dx1.astype(LOW)
    g1_ref[...] = g1
    do_ref[...] = dot(g1, wo_ref[...], NT).astype(LOW)
    add_row(sum_q, jnp.sum(dq_ref[...].astype(FULL), axis=0, keepdims=True) * SCALE, first)
    add_row(sum_out, jnp.sum(g1.astype(FULL), axis=0, keepdims=True), first)
    add_row(sum_gain, lines, first)
    add_row(sum_shift, shifts, first)


def cross_back(x1, dq, dx2, w_cross, w_out, p, tile=256):
    rows, width = x1.shape
    part = pl.BlockSpec((tile, width), lambda i: (i, 0))
    low = jax.ShapeDtypeStruct((rows, width), LOW)
    line = jax.ShapeDtypeStruct((1, width), FULL)
    return calls(
        cross_back_kernel,
        "cross_back",
        4 * rows * width * width,
        16 * rows * width + 4 * width * width,
        grid=(rows // tile,),
        in_specs=[part, part, part, whole((1, width, width)), whole(w_out.shape), whole(p.shape)],
        out_specs=[part, part, part] + [whole((1, width))] * 4,
        out_shape=[jax.ShapeDtypeStruct((rows, width), FULL), low, low, line, line, line, line],
    )(x1, dq, dx2, w_cross, w_out, p)


def self_back_kernel(x_ref, dq_ref, dkv_ref, dx1_ref, w_ref, p_ref, dx_ref, sum_q, sum_v, sum_gain, sum_shift):
    first = pl.program_id(0) == 0
    dq = dq_ref[...]
    grad = dot(dq, w_ref[0], NT) * SCALE + dot(dkv_ref[0], w_ref[1], NT) + dot(dkv_ref[1], w_ref[2], NT)
    hat, rstd = normal(x_ref[...].astype(FULL))
    back, lines, shifts = normal_back(hat, rstd, grad, p_ref[GAIN : GAIN + 1])
    dx_ref[...] = (dx1_ref[...] + back).astype(LOW)
    add_row(sum_q, jnp.sum(dq.astype(FULL), axis=0, keepdims=True) * SCALE, first)
    add_row(sum_v, jnp.sum(dkv_ref[1].astype(FULL), axis=0, keepdims=True), first)
    add_row(sum_gain, lines, first)
    add_row(sum_shift, shifts, first)


def self_back(x, dq, dkv, dx1, w, p, tile=256):
    rows, width = x.shape
    part = pl.BlockSpec((tile, width), lambda i: (i, 0))
    line = jax.ShapeDtypeStruct((1, width), FULL)
    return calls(
        self_back_kernel,
        "self_back",
        6 * rows * width * width,
        14 * rows * width + 6 * width * width,
        grid=(rows // tile,),
        in_specs=[part, part, pl.BlockSpec((2, tile, width), lambda i: (0, i, 0)), part, whole(w.shape), whole(p.shape)],
        out_specs=[part] + [whole((1, width))] * 4,
        out_shape=[jax.ShapeDtypeStruct((rows, width), LOW), line, line, line, line],
    )(x, dq, dkv, dx1, w, p)


def qkv_grad_kernel(a_ref, q_ref, b_ref, o_ref):
    j = pl.program_id(0)

    @pl.when(j == 0)
    def _():
        o_ref[0] = (dot(a_ref[...], q_ref[...], TN) * SCALE).astype(LOW)

    @pl.when(j > 0)
    def _():
        o_ref[0] = dot(a_ref[...], b_ref[0], TN).astype(LOW)


def qkv_grad(a, dq, dkv):
    rows, width = a.shape
    return calls(
        qkv_grad_kernel,
        "qkv_grad",
        6 * rows * width * width,
        2 * (4 * rows * width + 3 * width * width),
        grid=(3,),
        in_specs=[
            whole(a.shape),
            whole(dq.shape),
            pl.BlockSpec((1, rows, width), lambda j: (jnp.maximum(j - 1, 0), 0, 0)),
        ],
        out_specs=pl.BlockSpec((1, width, width), lambda j: (j, 0, 0)),
        out_shape=jax.ShapeDtypeStruct((3, width, width), LOW),
    )(a, dq, dkv)


def cross_grad_kernel(a_ref, q_ref, e_ref, b_ref, w_ref, o_ref, de_ref, sum_v, acc_ref):
    j = pl.program_id(0)

    @pl.when(j == 0)
    def _():
        o_ref[0] = (dot(a_ref[...], q_ref[...], TN) * SCALE).astype(LOW)

    @pl.when(j > 0)
    def _():
        o_ref[0] = dot(e_ref[...], b_ref[0], TN).astype(LOW)

    @pl.when(j == 1)
    def _():
        acc_ref[...] = dot(b_ref[0], w_ref[0], NT)

    @pl.when(j == 2)
    def _():
        de_ref[...] = (acc_ref[...] + dot(b_ref[0], w_ref[0], NT)).astype(LOW)
        sum_v[...] = jnp.sum(b_ref[0].astype(FULL), axis=0, keepdims=True)


def cross_grad(a, dq, memory, dkv, w_cross):
    rows, width = a.shape
    count = memory.shape[0]
    return calls(
        cross_grad_kernel,
        "cross_grad",
        2 * rows * width * width + 8 * count * width * width,
        2 * (2 * rows * width + 5 * width * width),
        grid=(3,),
        in_specs=[
            whole(a.shape),
            whole(dq.shape),
            whole(memory.shape),
            pl.BlockSpec((1, count, width), lambda j: (jnp.maximum(j - 1, 0), 0, 0)),
            pl.BlockSpec((1, width, width), lambda j: (jnp.maximum(j, 1), 0, 0)),
        ],
        out_specs=[pl.BlockSpec((1, width, width), lambda j: (j, 0, 0)), whole(memory.shape), whole((1, width))],
        out_shape=[
            jax.ShapeDtypeStruct((3, width, width), LOW),
            jax.ShapeDtypeStruct((count, width), LOW),
            jax.ShapeDtypeStruct((1, width), FULL),
        ],
        scratch_shapes=[pltpu.VMEM((count, width), FULL)],
    )(a, dq, memory, dkv, w_cross)


def layer(slots, x, memory, cotangent, length, count, s_qkv, s_out, c_qkv, c_out, w_up, w_down, p, bias_up):
    a0, qkv = project_qkv(x, s_qkv, p)
    mixed0, level0 = attend(length, (qkv, 0), (qkv, 1), (qkv, 2), True, "self_attend")
    x1, a1, q1 = middle(x, mixed0, s_out, c_qkv, p)
    kv1 = project_memory(memory, c_qkv, p)
    mixed1, level1 = attend(count, (q1, 0), (kv1, 0), (kv1, 1), False, "cross_attend")
    (result, r, du, a2, g3, dx2, g2, grad_mixed1, bias_up_grad, bias_down_grad, bias_five, gain_two, shift_two) = feed(
        length, x1, mixed1, cotangent, c_out, w_up, w_down, p, bias_up
    )
    result = leave(result, slots)
    grad_down = weight_grad(r, g3, "down_grad")
    grad_up = weight_grad(a2, du, "up_grad")
    dq1, dkv1 = attend_back(count, (q1, 0), (kv1, 0), (kv1, 1), mixed1, grad_mixed1, level1, False, "cross_attend_back")
    grad_c_out = weight_grad(mixed1, g2, "cross_out_grad")
    dx1, g1, grad_mixed0, bias_three, bias_two, gain_one, shift_one = cross_back(x1, dq1, dx2, c_qkv, s_out, p)
    grad_c_qkv, grad_memory, bias_four = cross_grad(a1, dq1, memory, dkv1, c_qkv)
    grad_memory = leave(grad_memory, slots)
    grad_mixed0 = after(grad_mixed0, result)
    dq0, dkv0 = attend_back(length, (qkv, 0), (qkv, 1), (qkv, 2), mixed0, grad_mixed0, level0, True, "self_attend_back")
    grad_s_out = weight_grad(mixed0, g1, "self_out_grad")
    dx, bias_zero, bias_one, gain_zero, shift_zero = self_back(x, after(dq0, grad_memory), dkv0, dx1, s_qkv, p)
    dx = leave(dx, slots)
    grad_s_qkv = qkv_grad(a0, dq0, dkv0)
    bias_grads = jnp.concatenate([bias_zero, bias_one, bias_two, bias_three, bias_four, bias_five])
    gains = jnp.concatenate([gain_zero, gain_one, gain_two])
    shifts = jnp.concatenate([shift_zero, shift_one, shift_two])
    return (
        (result, dx, grad_memory),
        (grad_s_qkv, grad_s_out, grad_c_qkv, grad_c_out, grad_up, grad_down),
        (bias_grads, bias_up_grad[0], bias_down_grad[0], gains, shifts),
    )


def units_of(shards):
    base = shards[0].shape[1]
    wide = shards[0].shape[2]
    found = []
    for which, (lead, rows, cols) in enumerate(a.shape for a in shards):
        for l in range(lead):
            for r in range(rows // base):
                for k in range(cols // wide):
                    found.append((which, l, slice(r * base, (r + 1) * base), slice(k * wide, (k + 1) * wide)))
    return tuple(found)


AXES = ("dp", "fsdp")


def arrive(array, deal):
    return lax.all_to_all(jnp.take(array, deal, axis=0), AXES, split_axis=0, concat_axis=1, tiled=True)[0]


def leave(array, slots):
    return lax.all_to_all(array.reshape(slots, -1, array.shape[-1]), AXES, split_axis=0, concat_axis=0, tiled=True)


def after(value, *others):
    return lax.optimization_barrier((value, *others))[0]


def per_device(
    mesh,
    units,
    encoder,
    cotangent,
    deal,
    lengths,
    enc_counts,
    self_qkv,
    self_out,
    cross_qkv,
    cross_out,
    ffn_up,
    ffn_down,
    biases,
    ffn_bias_up,
    ffn_bias_down,
    norm_gain,
    norm_shift,
):
    slots = deal.shape[0]
    depth, ring = mesh.shape["dp"] // 2, mesh.shape["fsdp"]
    inverse = jnp.zeros((slots,), jnp.int32).at[deal].set(jnp.arange(slots, dtype=jnp.int32))
    place = lax.axis_index(AXES)
    length = lax.dynamic_slice_in_dim(lengths, place, 1)
    enc_count = lax.dynamic_slice_in_dim(enc_counts, place, 1)
    x = arrive(units, deal)

    big = [self_qkv, self_out[None], cross_qkv, cross_out[None], ffn_up[None], ffn_down[None]]
    pieces = units_of(big)
    rows = jnp.concatenate([biases, norm_gain, norm_shift, ffn_bias_down[None]])
    flat = jnp.concatenate([rows.reshape(-1), ffn_bias_up])
    size = -(-flat.shape[0] // 2048) * 2048
    little = jnp.pad(flat, (0, size - flat.shape[0])).reshape(1, size // 128, 128)
    little_piece = ((len(big), 0, slice(0, size // 128), slice(0, 128)),)
    gathered = gather_weights(mesh, big + [little], little_piece + pieces, 0)
    memory = arrive(after(encoder, x, gathered[-1]), deal)
    cot = arrive(after(cotangent, memory), deal)
    s_qkv, s_out, c_qkv, c_out, w_up, w_down = (
        g.reshape(g.shape[0], -1, g.shape[-1]) for g in gathered[:6]
    )
    flat = gathered[6].reshape(slots, size).astype(jnp.float32)
    p = flat[:, : rows.size].reshape((slots,) + rows.shape)
    p = jnp.moveaxis(p, 0, 1).reshape(rows.shape[0], -1)
    p = jnp.pad(p, ((0, 16 - rows.shape[0]), (0, 0)))
    bias_up = flat[:, rows.size : rows.size + ffn_bias_up.size].reshape(1, -1)

    leaving, grads, small_grads = layer(
        slots, x, memory, cot, length, enc_count, s_qkv, s_out[0], c_qkv, c_out[0], w_up[0], w_down[0], p, bias_up
    )

    def cut(g):
        g = g if g.ndim == 3 else g[None]
        return g.reshape(g.shape[0], depth, 2, ring, -1, g.shape[-1])

    sums = scatter_grads(mesh, [cut(g) for g in grads], pieces, 1)
    terms = jnp.concatenate(
        [
            jnp.moveaxis(g.reshape(g.shape[:-1] + (slots, -1)), -2, 0).reshape(slots, -1)
            for g in small_grads
        ],
        axis=1,
    )
    terms = lax.all_to_all(terms, AXES, split_axis=0, concat_axis=0, tiled=True)
    flat = jnp.sum(terms, axis=0)
    small_sums, at = [], 0
    for like in (biases, ffn_bias_up, ffn_bias_down, norm_gain, norm_shift):
        small_sums.append(flat[at : at + like.size].reshape(like.shape))
        at += like.size
    return (
        *(jnp.take(a, inverse, axis=0) for a in leaving),
        sums[0],
        sums[1][0],
        sums[2],
        sums[3][0],
        sums[4][0],
        sums[5][0],
        *small_sums,
    )


def solution(mesh):
    middle_rows = P(None, AXES, None)
    first_rows = P(AXES, None)
    last = P(None, AXES)
    weights = (middle_rows, first_rows, middle_rows, first_rows, first_rows, first_rows, last, P(AXES), P(AXES), last, last)
    return jax.shard_map(
        functools.partial(per_device, mesh),
        mesh=mesh,
        in_specs=(middle_rows,) * 3 + (P(),) * 3 + weights,
        out_specs=(middle_rows,) * 3 + weights,
        check_vma=False,
    )
```

```python
import functools

import jax
import jax.numpy as jnp
from jax import lax
from jax.experimental import pallas as pl
from jax.experimental.pallas import tpu as pltpu
from jax.sharding import PartitionSpec as P

HD = 64
EPSILON = 1e-05
SCALE = 0.125
NEGATIVE = -1e30
MESH = pl.DeviceIdType.MESH
ANY = pl.BlockSpec(memory_space=pl.ANY)
DMA = pltpu.SemaphoreType.DMA


def ring_place(f, ring):
    half = ring // 2
    upper, rest = f // half, f % half
    return upper * half + rest + upper * (half - 1 - 2 * rest)


class Place:
    def __init__(self, depth, ring):
        self.depth, self.ring, self.half = depth, ring, ring // 2
        d, f = lax.axis_index("dp"), lax.axis_index("fsdp")
        self.z, self.c, self.f = d // 2, d % 2, f
        self.at = ring_place(f, ring)
        self.right = ring_place((self.at + 1) % ring, ring)
        self.left = ring_place((self.at + ring - 1) % ring, ring)

    def greet(self):
        barrier = pltpu.get_barrier_semaphore()

        def hail(d, g):
            pl.semaphore_signal(barrier, inc=1, device_id=(d, g), device_id_type=MESH)

        for s in range(1, self.depth):
            hail((self.z + s) % self.depth * 2 + self.c, self.f)
        hail(self.z * 2 + self.c, self.right)
        hail(self.z * 2 + self.c, self.left)
        hail(self.z * 2 + 1 - self.c, self.f)
        pl.semaphore_wait(barrier, self.depth + 2)

    def to_z(self, src, dst, send, recv, s):
        return self.remote(src, dst, send, recv, (self.z + s) % self.depth * 2 + self.c, self.f)

    def to_side(self, src, dst, send, recv, way):
        return self.remote(src, dst, send, recv, self.z * 2 + self.c, (self.right, self.left)[way])

    def to_core(self, src, dst, send, recv):
        return self.remote(src, dst, send, recv, self.z * 2 + 1 - self.c, self.f)

    @staticmethod
    def remote(src, dst, send, recv, d, g):
        return pltpu.make_async_remote_copy(
            src_ref=src, dst_ref=dst, send_sem=send, recv_sem=recv,
            device_id=(d, g), device_id_type=MESH,
        )


def when(flag, run):
    if isinstance(flag, bool):
        if flag:
            run()
    else:
        pl.when(flag)(run)


def both(one, two):
    if isinstance(one, bool) and isinstance(two, bool):
        return one and two
    return jnp.logical_and(one, two)


def loop(count, run):
    def body(i, carry):
        run(i)
        return carry

    lax.fori_loop(0, count, body, 0)


class Gather:
    def __init__(self, place, count, shards, fulls, sems, ahead=2):
        self.place, self.count, self.shards, self.fulls = place, count, shards, fulls
        self.local, self.z_send, self.z_recv, self.r_send, self.r_recv, self.c_send, self.c_recv = sems
        self.ahead = min(ahead, count)

    @staticmethod
    def sems(mesh, n):
        depth, ring = mesh.shape["dp"] // 2, mesh.shape["fsdp"]
        half = ring // 2
        return [DMA((n,)), DMA((n, depth)), DMA((n, depth)), DMA((n, half, 2)), DMA((n, half, 2)), DMA((n, ring)), DMA((n, ring))]

    def chunk(self, u, zs, c, g):
        return self.fulls.at[u, zs, c, g]

    def kept(self, u):
        p = self.place
        return pltpu.make_async_copy(self.shards.at[u], self.chunk(u, p.z, p.c, p.f), self.local.at[u])

    def z_copy(self, u, s, incoming):
        p = self.place
        origin = (p.z + p.depth - s) % p.depth if incoming else p.z
        return p.to_z(self.shards.at[u], self.chunk(u, origin, p.c, p.f), self.z_send.at[u, s], self.z_recv.at[u, s], s)

    def ring_copy(self, u, t, way, incoming):
        p = self.place
        back = t - 1 + incoming
        origin = (p.at + p.ring - back) % p.ring if way == 0 else (p.at + back) % p.ring
        cut = p.depth // 2
        zs = slice(0, p.depth) if t < p.half else (slice(0, cut), slice(cut, p.depth))[way]
        piece = self.chunk(u, zs, p.c, ring_place(origin, p.ring))
        return p.to_side(piece, piece, self.r_send.at[u, t - 1, way], self.r_recv.at[u, t - 1, way], way)

    def core_copy(self, u, shift, incoming):
        p = self.place
        c = 1 - p.c if incoming else p.c
        piece = self.chunk(u, slice(0, p.depth), c, ring_place((p.at + shift) % p.ring, p.ring))
        return p.to_core(piece, piece, self.c_send.at[u, shift], self.c_recv.at[u, shift])

    def start_z(self, u):
        self.kept(u).start()
        for s in range(1, self.place.depth):
            self.z_copy(u, s, False).start()

    def start_ring(self, u, t):
        for way in range(2):
            self.ring_copy(u, t, way, 0).start()

    def start_core(self, u, t):
        half, ring = self.place.half, self.place.ring
        for shift in [0] if t == 0 else [t] if t == half else [ring - t, t]:
            self.core_copy(u, shift, False).start()

    def begin(self):
        for u in range(self.ahead):
            self.start_z(u)

    def steps(self):
        return self.count + self.place.half

    def step(self, i):
        place = self.place

        def first():
            self.kept(i).wait()
            for s in range(1, place.depth):
                self.z_copy(i, s, True).wait_recv()
            self.start_ring(i, 1)
            self.start_core(i, 0)

        def later(u, t):
            for way in range(2):
                self.ring_copy(u, t, way, 1).wait_recv()
            if t < place.half:
                self.start_ring(u, t + 1)
            self.start_core(u, t)

        when(i + self.ahead < self.count, lambda: self.start_z(i + self.ahead))
        when(i < self.count, first)
        for t in range(1, place.half + 1):
            u = i - t
            when(both(0 <= u, u < self.count), functools.partial(later, u, t))

    def finish(self):
        place = self.place

        def one(u):
            for s in range(1, place.depth):
                self.z_copy(u, s, False).wait_send()
            for t in range(1, place.half + 1):
                for way in range(2):
                    self.ring_copy(u, t, way, 0).wait_send()
            for shift in range(place.ring):
                self.core_copy(u, shift, False).wait_send()
                self.core_copy(u, shift, True).wait_recv()

        loop(self.count, one)


class Scatter:
    def __init__(self, place, count, rows, held, outs, refs, sems):
        self.place, self.count, self.rows, self.held, self.outs = place, count, rows, held, outs
        self.mine, self.theirs, self.rhalf, self.rfull, self.zbuf = refs
        self.c_send, self.c_recv, self.r_send, self.r_recv, self.z_send, self.z_recv = sems
        self.slots = held.shape[0]

    @staticmethod
    def refs(mesh, n, rows, cols, low):
        depth, ring = mesh.shape["dp"] // 2, mesh.shape["fsdp"]
        half, cut = ring // 2, depth // 2
        return [
            pltpu.VMEM((n, depth, ring, rows, cols), low),
            pltpu.VMEM((n, depth, ring * rows, cols), low),
            pltpu.VMEM((n, 2, cut, rows, cols), low),
            pltpu.VMEM((n, half - 1, 2, depth, rows, cols), low),
            pltpu.VMEM((n, depth - 1, rows, cols), low),
        ]

    @staticmethod
    def sems(mesh, n):
        depth, ring = mesh.shape["dp"] // 2, mesh.shape["fsdp"]
        half = ring // 2
        return [DMA((n,)), DMA((n,)), DMA((n, half, 2)), DMA((n, half, 2)), DMA((n, depth)), DMA((n, depth))]

    def core(self, u):
        p = self.place
        return p.to_core(self.held.at[u % self.slots, slice(0, p.depth), 1 - p.c], self.theirs.at[u], self.c_send.at[u], self.c_recv.at[u])

    def dest(self, t, way):
        p = self.place
        ahead = p.half - t + 1
        return ring_place((p.at + ahead) % p.ring if way == 0 else (p.at + p.ring - ahead) % p.ring, p.ring)

    def ring_copy(self, u, t, way):
        p = self.place
        g, cut = self.dest(t, way), p.depth // 2
        if t == 1:
            src = self.mine.at[u, slice(0, cut) if way == 0 else slice(cut, p.depth), g]
            dst = self.rhalf.at[u, way]
        else:
            src = self.mine.at[u, slice(0, p.depth), g]
            dst = self.rfull.at[u, t - 2, way]
        return p.to_side(src, dst, self.r_send.at[u, t - 1, way], self.r_recv.at[u, t - 1, way], way)

    def z_copy(self, u, s):
        p = self.place
        to = (p.z + s) % p.depth
        return p.to_z(self.mine.at[u, to, p.f], self.zbuf.at[u, s - 1], self.z_send.at[u, s], self.z_recv.at[u, s], s)

    def first_sum(self, u):
        p, full = self.place, jnp.float32
        self.core(u).wait_recv()

        def one(a):
            total = self.held[u % self.slots, a, p.c].astype(full) + self.theirs[u, a].astype(full)
            for g in range(p.ring):
                self.mine[u, a, g] = total[g * self.rows : (g + 1) * self.rows].astype(self.mine.dtype)

        loop(p.depth, one)
        for way in range(2):
            self.ring_copy(u, 1, way).start()

    def next_sum(self, u, t):
        p, full, mine = self.place, jnp.float32, self.mine
        for way in range(2):
            self.ring_copy(u, t, way).wait_recv()
        cut = p.depth // 2
        if t < p.half:
            for way in range(2):
                g = self.dest(t + 1, way)
                low = cut * way if t == 1 else 0
                src = self.rhalf.at[u, way] if t == 1 else self.rfull.at[u, t - 2, way]

                def one(a, g=g, low=low, src=src):
                    mine[u, low + a, g] = (mine[u, low + a, g].astype(full) + src[a].astype(full)).astype(mine.dtype)

                loop(cut if t == 1 else p.depth, one)
                self.ring_copy(u, t + 1, way).start()
        else:
            left, right = self.rfull.at[u, t - 2, 0], self.rfull.at[u, t - 2, 1]

            def one(a):
                mine[u, a, p.f] = (
                    mine[u, a, p.f].astype(full) + left[a].astype(full) + right[a].astype(full)
                ).astype(mine.dtype)

            loop(p.depth, one)
            for s in range(1, p.depth):
                self.z_copy(u, s).start()

    def last_sum(self, u):
        p, full = self.place, jnp.float32
        for s in range(1, p.depth):
            self.z_copy(u, s).wait_recv()
        total = self.mine[u, p.z, p.f].astype(full)
        for s in range(1, p.depth):
            total = total + self.zbuf[u, s - 1].astype(full)
        self.outs[u] = total

    def finish(self):
        p = self.place

        def one(u):
            for t in range(1, p.half + 1):
                for way in range(2):
                    self.ring_copy(u, t, way).wait_send()
            for s in range(1, p.depth):
                self.z_copy(u, s).wait_send()

        loop(self.count, one)
        for u in range(max(0, self.count - self.slots), self.count):
            self.core(u).wait_send()

    def steps(self):
        return self.count + self.place.half // 2 + 1

    def early(self, i):
        for t in range(1, self.place.half + 1, 2):
            u = i - (t + 1) // 2
            when(both(0 <= u, u < self.count), functools.partial(self.next_sum, u, t))

    def late(self, i):
        when(i < self.count, lambda: self.first_sum(i))
        for t in range(2, self.place.half + 1, 2):
            u = i - t // 2
            when(both(0 <= u, u < self.count), functools.partial(self.next_sum, u, t))
        u = i - self.place.half // 2 - 1
        when(both(0 <= u, u < self.count), lambda: self.last_sum(u))


def remote_params(ident):
    return pltpu.CompilerParams(collective_id=ident, has_side_effects=True, vmem_limit_bytes=60 * 2**20)


def first_gather_kernel(depth, ring, count, shard, little, full, little_full, *sems):
    place = Place(depth, ring)
    place.greet()
    small = Gather(place, 1, little, little_full, sems[:7])
    big = Gather(place, count, shard, full, sems[7:])
    small.begin()
    big.begin()
    for i in range(big.steps()):
        if i < small.steps():
            small.step(i)
        big.step(i)
    small.finish()
    big.finish()


def first_gather(mesh, shards, little, ident):
    depth, ring = mesh.shape["dp"] // 2, mesh.shape["fsdp"]
    count = shards.shape[0]

    def full(a):
        return jax.ShapeDtypeStruct((a.shape[0], depth, 2, ring) + a.shape[1:], a.dtype)

    return pl.pallas_call(
        functools.partial(first_gather_kernel, depth, ring, count),
        out_shape=[full(shards), full(little)],
        in_specs=[ANY] * 2,
        out_specs=[ANY] * 2,
        scratch_shapes=Gather.sems(mesh, 1) + Gather.sems(mesh, count),
        compiler_params=remote_params(ident),
        cost_estimate=pl.CostEstimate(flops=60_000_000_000, bytes_accessed=2 * 33_554_432, transcendentals=0),
        name="first_gather",
    )(shards, little)


NN = (((1,), (0,)), ((), ()))
NT = (((1,), (1,)), ((), ()))
TN = (((0,), (0,)), ((), ()))
LOW = jnp.bfloat16
FULL = jnp.float32
SMEM = pl.BlockSpec(memory_space=pltpu.SMEM)
VMEM = pl.BlockSpec(memory_space=pltpu.VMEM)
PAIR = 2 * HD
ROOM = 60 * 2**20


def dot(left, right, how):
    return lax.dot_general(left, right, how, preferred_element_type=FULL)


def calls(kernel, name, flops, moved, **kw):
    return pl.pallas_call(
        kernel,
        name=name,
        compiler_params=pltpu.CompilerParams(vmem_limit_bytes=ROOM),
        cost_estimate=pl.CostEstimate(flops=int(flops), bytes_accessed=int(moved), transcendentals=0),
        **kw,
    )


def whole(shape):
    return pl.BlockSpec(shape, lambda *_: (0,) * len(shape))


def normal(x):
    mean = jnp.mean(x, axis=-1, keepdims=True)
    centred = x - mean
    rstd = lax.rsqrt(jnp.mean(centred * centred, axis=-1, keepdims=True) + EPSILON)
    return centred * rstd, rstd


def normal_back(hat, rstd, grad, gain):
    scaled = grad * gain
    lean = jnp.mean(scaled, axis=-1, keepdims=True)
    tilt = jnp.mean(scaled * hat, axis=-1, keepdims=True)
    back = rstd * (scaled - lean - hat * tilt)
    return back, jnp.sum(grad * hat, axis=0, keepdims=True), jnp.sum(grad, axis=0, keepdims=True)


def add_row(ref, value, first):
    @pl.when(first)
    def _():
        ref[...] = value

    @pl.when(jnp.logical_not(first))
    def _():
        ref[...] += value


GAIN, SHIFT, DOWN = 6, 9, 12


def lanes(shape):
    return lax.broadcasted_iota(jnp.int32, shape, len(shape) - 1)


def rows_of(shape):
    return lax.broadcasted_iota(jnp.int32, shape, 0)


def head_mask(head):
    return jnp.where(lanes((1, PAIR)) // HD == head, 1.0, 0.0).astype(LOW)


def thirds(x):
    one = x.astype(LOW).astype(FULL)
    two = (x - one).astype(LOW).astype(FULL)
    return one, two, x - one - two


def wide_keys(k, v, n):
    count = k.shape[0]
    shut = jnp.where((lanes((count, PAIR)) == 0) & (rows_of((count, PAIR)) >= n), NEGATIVE, 0.0).astype(LOW)
    ones = jnp.ones((count, PAIR), LOW)
    return [
        (jnp.concatenate([k * head_mask(h), shut], axis=1), jnp.concatenate([v * head_mask(h), ones], axis=1))
        for h in range(2)
    ]


def attend_pair(causal, tile, h, n, q, k, v, store, l_ref):
    queries, count = q.shape[0], k.shape[0]
    first = jnp.where(lanes((queries, PAIR)) == 0, 1.0, 0.0).astype(LOW)
    wide_q = jnp.concatenate([q, first], axis=1)
    spots = lanes((tile, PAIR))
    heads = wide_keys(k, v, n)
    for i in range(queries // tile):
        at = slice(i * tile, (i + 1) * tile)
        seen = (i + 1) * tile if causal else count
        mixed = jnp.zeros((tile, PAIR), FULL)
        kept = l_ref[at]
        for head, (keys, values) in enumerate(heads):
            scores = dot(wide_q[at], keys[:seen], NT)
            if causal:
                square = (tile, tile)
                last = jnp.where(lanes(square) <= rows_of(square), scores[:, seen - tile :], NEGATIVE)
                scores = last if seen == tile else jnp.concatenate([scores[:, : seen - tile], last], axis=1)
            top = jnp.max(scores, axis=1, keepdims=True)
            weights = jnp.exp(scores - top).astype(LOW)
            sums = dot(weights, values[:seen], NN)
            total = sums[:, PAIR:]
            mixed = mixed + sums[:, :PAIR] / total
            kept = jnp.where(spots == 2 * h + head, top + jnp.log(total), kept)
        store(at, mixed.astype(LOW))
        l_ref[at] = kept


def forward_kernel(
    depth, ring, count, n_ref, m_ref, x_hbm, e_hbm, w_hbm, p_ref, shard,
    full, a0_hbm, qkv_hbm, o0_hbm, l0_hbm, x1_hbm, a1_hbm, q1_hbm, kv_hbm, o1_hbm, l1_hbm,
    x_ref, e_ref, w_ref, a_ref, qkv_ref, o_ref, l0_ref, x1_ref, q1_ref, kv_ref, l1_ref, a1_ref,
    w_sem, in_sem, out_sem, *sems,
):
    place = Place(depth, ring)
    place.greet()
    gather = Gather(place, count, shard, full, sems)
    gather.begin()
    rows, width = x_ref.shape
    tile = 256
    load_x = pltpu.make_async_copy(x_hbm, x_ref, in_sem.at[0])
    load_e = pltpu.make_async_copy(e_hbm, e_ref, in_sem.at[1])
    load_x.start()
    parts = w_ref.shape[0]
    loads = [pltpu.make_async_copy(w_hbm.at[u], w_ref.at[u], w_sem.at[u]) for u in range(parts)]
    for load in loads[:3]:
        load.start()
    load_e.start()
    for load in loads[3:]:
        load.start()
    leaving = []

    def send(src, dst):
        copy = pltpu.make_async_copy(src, dst, out_sem.at[len(leaving)])
        copy.start()
        leaving.append(copy)

    l0_ref[...] = jnp.zeros_like(l0_ref)
    l1_ref[...] = jnp.zeros_like(l1_ref)
    load_x.wait()
    gather.step(0)
    for i in range(rows // tile):
        at = slice(i * tile, (i + 1) * tile)
        hat, _ = normal(x_ref[at].astype(FULL))
        a_ref[at] = (hat * p_ref[GAIN : GAIN + 1] + p_ref[SHIFT : SHIFT + 1]).astype(LOW)
    send(a_ref, a0_hbm)
    for j in range(3):
        loads[j].wait()
        bias = (p_ref[0:1], None, p_ref[1:2])[j]

        def project(i, j=j, bias=bias):
            at = pl.ds(pl.multiple_of(i * 2 * tile, 2 * tile), 2 * tile)
            y = dot(a_ref[at], w_ref[j], NN)
            if bias is not None:
                y = y + bias
            qkv_ref[j, at] = (y * SCALE if j == 0 else y).astype(LOW)

        loop(rows // (2 * tile), project)
        send(qkv_ref.at[j], qkv_hbm.at[j])
        if j == 1:
            gather.step(1)

    pairs = width // PAIR

    def self_pair(h):
        cols = pl.ds(pl.multiple_of(h * PAIR, PAIR), PAIR)

        def store(at, value):
            o_ref[at, cols] = value

        attend_pair(True, tile, h, n_ref[0], qkv_ref[0, :, cols], qkv_ref[1, :, cols], qkv_ref[2, :, cols], store, l0_ref)
        when(h % 2 == 0, lambda: gather.step(2 + h // 2))

    loop(pairs, self_pair)
    send(o_ref, o0_hbm)
    send(l0_ref, l0_hbm)
    done = 2 + (pairs + 1) // 2
    loads[3].wait()
    loads[4].wait()

    def middle_part(i):
        at = pl.ds(pl.multiple_of(i * tile, tile), tile)
        x1 = x_ref[at].astype(FULL) + (dot(o_ref[at], w_ref[3], NN) + p_ref[2:3])
        x1_ref[at] = x1
        hat, _ = normal(x1)
        a = (hat * p_ref[GAIN + 1 : GAIN + 2] + p_ref[SHIFT + 1 : SHIFT + 2]).astype(LOW)
        a1_ref[at] = a
        q1_ref[at] = ((dot(a, w_ref[4], NN) + p_ref[3:4]) * SCALE).astype(LOW)
        when(i % 2 == 1, lambda: gather.step(done + i // 2))

    loop(rows // tile, middle_part)
    done = done + rows // tile // 2
    send(x1_ref, x1_hbm)
    send(a1_ref, a1_hbm)
    send(q1_ref, q1_hbm.at[0])
    load_e.wait()
    for j in range(2):
        loads[5 + j].wait()
        y = dot(e_ref[...], w_ref[5 + j], NN)
        kv_ref[j] = (y + p_ref[4:5] if j == 1 else y).astype(LOW)
    send(kv_ref, kv_hbm)
    leaving[4].wait()

    def cross_pair(h):
        cols = pl.ds(pl.multiple_of(h * PAIR, PAIR), PAIR)

        def store(at, value):
            o_ref[at, cols] = value

        attend_pair(False, tile, h, m_ref[0], q1_ref[:, cols], kv_ref[0, :, cols], kv_ref[1, :, cols], store, l1_ref)
        when(h % 2 == 0, lambda: gather.step(done + h // 2))

    loop(pairs, cross_pair)
    done = done + (pairs + 1) // 2
    send(o_ref, o1_hbm)
    send(l1_ref, l1_hbm)
    for i in range(done, gather.steps()):
        gather.step(i)
    gather.finish()
    for k, copy in enumerate(leaving):
        if k != 4:
            copy.wait()


def forward(mesh, length, enc_count, x, memory, w, p, shards, ident):
    depth, ring = mesh.shape["dp"] // 2, mesh.shape["fsdp"]
    count = shards.shape[0]
    rows, width = x.shape
    enc = memory.shape[0]
    low = jax.ShapeDtypeStruct((rows, width), LOW)
    level = jax.ShapeDtypeStruct((rows, PAIR), FULL)
    out_shape = [
        jax.ShapeDtypeStruct((count, depth, 2, ring) + shards.shape[1:], LOW),
        low,
        jax.ShapeDtypeStruct((3, rows, width), LOW),
        low,
        level,
        jax.ShapeDtypeStruct((rows, width), FULL),
        low,
        jax.ShapeDtypeStruct((1, rows, width), LOW),
        jax.ShapeDtypeStruct((2, enc, width), LOW),
        low,
        level,
    ]
    big = pltpu.VMEM((rows, width), LOW)
    return pl.pallas_call(
        functools.partial(forward_kernel, depth, ring, count),
        out_shape=out_shape,
        in_specs=[SMEM, SMEM, ANY, ANY, ANY, VMEM, ANY],
        out_specs=[ANY] * len(out_shape),
        scratch_shapes=[
            big,
            pltpu.VMEM((enc, width), LOW),
            pltpu.VMEM(w.shape, LOW),
            big,
            pltpu.VMEM((3, rows, width), LOW),
            big,
            pltpu.VMEM((rows, PAIR), FULL),
            pltpu.VMEM((rows, width), FULL),
            big,
            pltpu.VMEM((2, enc, width), LOW),
            pltpu.VMEM((rows, PAIR), FULL),
            big,
            DMA((w.shape[0],)),
            DMA((2,)),
            DMA((12,)),
        ]
        + Gather.sems(mesh, count),
        compiler_params=remote_params(ident),
        cost_estimate=pl.CostEstimate(flops=70_000_000_000, bytes_accessed=2 * 33_554_432, transcendentals=0),
        name="forward_gather",
    )(length, enc_count, x, memory, w, p, shards)


def back_pair(causal, tile, h, n, q, k, v, mixed, grad, level, acc_ref, store):
    queries, count = q.shape[0], k.shape[0]
    lane_k, lane_q = lanes((count, PAIR)), lanes((queries, PAIR))
    shut = jnp.where(rows_of((count, PAIR)) >= n, NEGATIVE, 0.0)
    open_k = jnp.where(lane_k == 0, shut, jnp.where(lane_k < 4, 1.0, 0.0)).astype(LOW)
    open_v = jnp.where(lane_k < 3, 1.0, 0.0).astype(LOW)
    product = grad.astype(FULL) * mixed.astype(FULL)
    acc_ref[...] = jnp.zeros_like(acc_ref)
    heads = []
    for head in range(2):
        mask = head_mask(head)
        lse = jnp.sum(jnp.where(lane_q == 2 * h + head, level, 0.0), axis=1, keepdims=True)
        one, two, three = thirds(-lse)
        tail = jnp.where(lane_q == 0, 1.0, jnp.where(lane_q == 1, one, jnp.where(lane_q == 2, two, jnp.where(lane_q == 3, three, 0.0))))
        wide_q = jnp.concatenate([q, tail.astype(LOW)], axis=1)
        inner = jnp.sum(jnp.where(lane_q // HD == head, product, 0.0), axis=1, keepdims=True)
        one, two, three = thirds(-inner)
        tail = jnp.where(lane_q == 0, one, jnp.where(lane_q == 1, two, jnp.where(lane_q == 2, three, 0.0)))
        wide_g = jnp.concatenate([grad, tail.astype(LOW)], axis=1)
        wide_k = jnp.concatenate([k * mask, open_k], axis=1)
        wide_v = jnp.concatenate([v * mask, open_v], axis=1)
        heads.append((wide_q, wide_g, wide_k, wide_v, q * mask, grad * mask, k * mask))
    for i in range(count // tile):
        at = slice(i * tile, (i + 1) * tile)
        low = i * tile if causal else 0
        grad_k = jnp.zeros((tile, PAIR), FULL)
        grad_v = jnp.zeros((tile, PAIR), FULL)
        for wide_q, wide_g, wide_k, wide_v, q_one, g_one, k_one in heads:
            scores = dot(wide_k[at], wide_q[low:], NT)
            if causal:
                square = (tile, tile)
                near = jnp.where(rows_of(square) <= lanes(square), scores[:, :tile], NEGATIVE)
                scores = near if low + tile == queries else jnp.concatenate([near, scores[:, tile:]], axis=1)
            probs = jnp.exp(scores)
            slope = (probs * dot(wide_v[at], wide_g[low:], NT)).astype(LOW)
            grad_v = grad_v + dot(probs.astype(LOW), g_one[low:], NN)
            grad_k = grad_k + dot(slope, q_one[low:], NN)
            acc_ref[low:] += dot(slope, k_one[at], TN)
        store(at, grad_k.astype(LOW), grad_v.astype(LOW))


def unit_grad(place, held, slot, a_ref, b_ref, scale):
    depth, part = held.shape[1], held.shape[3]
    width = a_ref.shape[1]
    piece = width // 2
    for m in range(2):
        value = dot(a_ref[:, m * piece : (m + 1) * piece], b_ref[...], TN)
        if scale is not None:
            value = value * scale
        value = value.astype(LOW)
        for k in range(piece // part):
            at = m * (piece // part) + k
            held[slot, at // 2, at % 2] = value[k * part : (k + 1) * part]


def feed_scatter_kernel(
    depth, ring, n_ref, a2_hbm, g3_hbm, du_hbm, r_hbm, qkv_hbm, mixed_hbm, grad_hbm, l_ref,
    outs, dq_hbm, dkv_hbm,
    a2_ref, g3_ref, moving, held, q_buf, acc_ref, dq_buf, dkv_buf, in_sem, move_sem, q_sem, out_sem, *rest,
):
    place = Place(depth, ring)
    place.greet()
    blocks = du_hbm.shape[0]
    count = 2 * blocks
    sums = Scatter(place, count, outs.shape[1], held, outs, rest[:5], rest[5:])
    pairs = mixed_hbm.shape[1] // PAIR
    slots = held.shape[0]
    load_a = pltpu.make_async_copy(a2_hbm, a2_ref, in_sem.at[0])
    load_g = pltpu.make_async_copy(g3_hbm, g3_ref, in_sem.at[1])

    def move(u, array, j):
        return pltpu.make_async_copy(array.at[j], moving.at[u % 2], move_sem.at[u % 2])

    def start_move(u):
        when(u < blocks, lambda: move(u, du_hbm, u).start())
        when(u >= blocks, lambda: move(u, r_hbm, jnp.maximum(u - blocks, 0)).start())

    def fetch(h):
        cols = pl.ds(pl.multiple_of(h * PAIR, PAIR), PAIR)
        sources = [qkv_hbm.at[0, :, cols], qkv_hbm.at[1, :, cols], qkv_hbm.at[2, :, cols], mixed_hbm.at[:, cols], grad_hbm.at[:, cols]]
        return [pltpu.make_async_copy(s, q_buf.at[h % 2, k], q_sem.at[h % 2, k]) for k, s in enumerate(sources)]

    def put(h):
        cols = pl.ds(pl.multiple_of(h * PAIR, PAIR), PAIR)
        return [
            pltpu.make_async_copy(dq_buf.at[h % 2], dq_hbm.at[:, cols], out_sem.at[h % 2, 0]),
            pltpu.make_async_copy(dkv_buf.at[h % 2], dkv_hbm.at[:, :, cols], out_sem.at[h % 2, 1]),
        ]

    load_a.start()
    start_move(0)
    for copy in fetch(0):
        copy.start()
    load_g.start()
    load_a.wait()

    def weights(i):
        when(i + 1 < count, lambda: start_move(i + 1))
        when(i == blocks, load_g.wait)
        move(i, du_hbm, 0).wait()
        when(i >= slots, lambda: sums.core(i - slots).wait_send())
        slot = i % slots
        when(i < blocks, lambda: unit_grad(place, held, slot, a2_ref, moving.at[i % 2], None))
        when(i >= blocks, lambda: unit_grad(place, held, slot, moving.at[i % 2], g3_ref, None))
        sums.core(i).start()

    def heads(h):
        def next_fetch():
            for copy in fetch(h + 1):
                copy.start()

        when(h + 1 < pairs, next_fetch)
        for copy in fetch(h):
            copy.wait()

        def free():
            for copy in put(h - 2):
                copy.wait()

        when(h >= 2, free)
        b = h % 2

        def store(at, grad_k, grad_v):
            dkv_buf[b, 0, at] = grad_k
            dkv_buf[b, 1, at] = grad_v

        back_pair(True, 256, h, n_ref[0], q_buf[b, 0], q_buf[b, 1], q_buf[b, 2], q_buf[b, 3], q_buf[b, 4], l_ref[...], acc_ref, store)
        dq_buf[b] = acc_ref[...].astype(LOW)
        for copy in put(h):
            copy.start()

    def step(i):
        when(i < count, lambda: weights(i))
        sums.early(i)
        when(i < pairs, lambda: heads(i))
        sums.late(i)

    loop(max(sums.steps(), pairs), step)
    for h in range(max(0, pairs - 2), pairs):
        for copy in put(h):
            copy.wait()
    sums.finish()


def feed_scatter(mesh, length, a2, g3, du, r, qkv, mixed, grad, level, ident):
    depth, ring = mesh.shape["dp"] // 2, mesh.shape["fsdp"]
    blocks, rows, width = du.shape
    own = width // (2 * depth * ring)
    count = 2 * blocks
    big = pltpu.VMEM((rows, width), LOW)
    return pl.pallas_call(
        functools.partial(feed_scatter_kernel, depth, ring),
        out_shape=[
            jax.ShapeDtypeStruct((count, own, width), FULL),
            jax.ShapeDtypeStruct((rows, width), LOW),
            jax.ShapeDtypeStruct((2, rows, width), LOW),
        ],
        in_specs=[SMEM] + [ANY] * 7 + [VMEM],
        out_specs=[VMEM, ANY, ANY],
        scratch_shapes=[
            big,
            big,
            pltpu.VMEM((2, rows, width), LOW),
            pltpu.VMEM((3, depth, 2, ring * own, width), LOW),
            pltpu.VMEM((2, 5, rows, PAIR), LOW),
            pltpu.VMEM((rows, PAIR), FULL),
            pltpu.VMEM((2, rows, PAIR), LOW),
            pltpu.VMEM((2, 2, rows, PAIR), LOW),
            DMA((2,)),
            DMA((2,)),
            DMA((2, 5)),
            DMA((2, 2)),
        ]
        + Scatter.refs(mesh, count, own, width, LOW)
        + Scatter.sems(mesh, count),
        compiler_params=remote_params(ident),
        cost_estimate=pl.CostEstimate(flops=60_000_000_000, bytes_accessed=2 * 33_554_432, transcendentals=0),
        name="feed_scatter",
    )(length, a2, g3, du, r, qkv, mixed, grad, level)


def last_scatter_kernel(
    depth, ring, made_hbm, o1_hbm, g2_hbm, a1_hbm, dq1_hbm, o0_hbm, g1_hbm, a0_hbm, dq0_hbm, dkv_hbm, tiny_ref,
    outs, tiny_out, left, right, held, tiny_held, left_sem, right_sem, made_sem, *rest,
):
    place = Place(depth, ring)
    place.greet()
    made = made_hbm.shape[0]
    pairs = [(a1_hbm, dq1_hbm), (o1_hbm, g2_hbm), (o0_hbm, g1_hbm), (a0_hbm, dq0_hbm), (a0_hbm, dkv_hbm.at[0]), (a0_hbm, dkv_hbm.at[1])]
    scaled = (0, 3)
    count = made + len(pairs)
    small = Scatter(place, 1, tiny_out.shape[1], tiny_held, tiny_out, rest[:5], rest[5:11])
    sums = Scatter(place, count, outs.shape[1], held, outs, rest[11:16], rest[16:])
    slots = held.shape[0]

    def load(k):
        a, b = pairs[k]
        return [
            pltpu.make_async_copy(a, left.at[k % 2], left_sem.at[k % 2]),
            pltpu.make_async_copy(b, right.at[k % 2], right_sem.at[k % 2]),
        ]

    given = [pltpu.make_async_copy(made_hbm.at[u], held.at[u], made_sem.at[u]) for u in range(made)]
    for copy in given:
        copy.start()
    for k in range(2):
        for copy in load(k):
            copy.start()
    tiny_held[0] = tiny_ref[...]
    small.core(0).start()
    for i in range(sums.steps()):
        if i < count:
            k = i - made
            if i < made:
                given[i].wait()
            else:
                for copy in load(k):
                    copy.wait()
                if i >= slots:
                    sums.core(i - slots).wait_send()
                unit_grad(place, held, i % slots, left.at[k % 2], right.at[k % 2], SCALE if k in scaled else None)
                if k + 2 < len(pairs):
                    for copy in load(k + 2):
                        copy.start()
            sums.core(i).start()
        if i < small.steps():
            small.early(i)
        sums.early(i)
        if i < small.steps():
            small.late(i)
        sums.late(i)
    small.finish()
    sums.finish()


def last_scatter(mesh, made, pairs, tiny, ident):
    depth, ring = mesh.shape["dp"] // 2, mesh.shape["fsdp"]
    n, width = made.shape[0], made.shape[-1]
    rows = pairs[0].shape[0]
    own = made.shape[3] // ring
    count = n + 6
    tiny_rows = tiny.shape[2] // ring
    return pl.pallas_call(
        functools.partial(last_scatter_kernel, depth, ring),
        out_shape=[
            jax.ShapeDtypeStruct((count, own, width), FULL),
            jax.ShapeDtypeStruct((1, tiny_rows, tiny.shape[3]), FULL),
        ],
        in_specs=[ANY] * (1 + len(pairs)) + [VMEM],
        out_specs=[VMEM, VMEM],
        scratch_shapes=[
            pltpu.VMEM((2, rows, width), LOW),
            pltpu.VMEM((2, rows, width), LOW),
            pltpu.VMEM((3,) + made.shape[1:], LOW),
            pltpu.VMEM((1,) + tiny.shape, FULL),
            DMA((2,)),
            DMA((2,)),
            DMA((n,)),
        ]
        + Scatter.refs(mesh, 1, tiny_rows, tiny.shape[3], FULL)
        + Scatter.sems(mesh, 1)
        + Scatter.refs(mesh, count, own, width, LOW)
        + Scatter.sems(mesh, count),
        compiler_params=remote_params(ident),
        cost_estimate=pl.CostEstimate(flops=60_000_000_000, bytes_accessed=2 * 33_554_432, transcendentals=0),
        name="last_scatter",
    )(made, *pairs, tiny)


CUBIC = 0.044715
ROOT = 0.7978845608028654


def feed_kernel(
    n_ref, x1_ref, o_ref, g_ref, w_hbm, p_ref, bu_ref,
    out_ref, r_ref, du_ref, a_ref, g3_ref, dx_ref, g2_ref, do_ref,
    sum_up, sum_down, sum_five, sum_gain, sum_shift,
    w_ref, slope_ref, sems,
):
    i = pl.program_id(0)
    first = i == 0
    tile, width = x1_ref.shape
    blocks = (w_hbm.shape[0] - 1) // 2
    order = [0] + [k * blocks + j + 1 for j in range(blocks) for k in range(2)]
    loads = {u: pltpu.make_async_copy(w_hbm.at[u], w_ref.at[u], sems.at[u]) for u in order}

    def ready(u):
        pl.when(first)(loads[u].wait)

    @pl.when(first)
    def _():
        for u in order:
            loads[u].start()
        loads[0].wait()

    valid = jnp.where(i * tile + rows_of((tile, 1)) < n_ref[0], 1.0, 0.0)
    x2 = x1_ref[...] + (dot(o_ref[...], w_ref[0], NN) + p_ref[5:6])
    hat, rstd = normal(x2)
    gain = p_ref[GAIN + 2 : GAIN + 3]
    a_ref[...] = (hat * gain + p_ref[SHIFT + 2 : SHIFT + 3]).astype(LOW)

    total = x2 + p_ref[DOWN : DOWN + 1]
    for j in range(blocks):
        cols = slice(j * width, (j + 1) * width)
        ready(1 + j)
        u = dot(a_ref[...], w_ref[1 + j], NN) + bu_ref[:, cols]
        square = u * u
        t = jnp.tanh(ROOT * (u * (1.0 + CUBIC * square)))
        half = 0.5 * (1.0 + t)
        r = (u * half).astype(LOW)
        r_ref[j] = r
        slope = half + 0.5 * u * (1.0 - t * t) * (ROOT * (1.0 + 3.0 * CUBIC * square))
        slope_ref[:, cols] = slope.astype(LOW)
        ready(1 + blocks + j)
        total = total + dot(r, w_ref[1 + blocks + j], NN)
    out_ref[...] = (total * valid).astype(LOW)
    grad_out = g_ref[...].astype(FULL) * valid
    g3 = grad_out.astype(LOW)
    g3_ref[...] = g3
    grad = jnp.zeros((tile, width), FULL)
    for j in range(blocks):
        cols = slice(j * width, (j + 1) * width)
        du = (dot(g3, w_ref[1 + blocks + j], NT) * slope_ref[:, cols].astype(FULL)).astype(LOW)
        du_ref[j] = du
        line = jnp.sum(du.astype(FULL), axis=0, keepdims=True)

        @pl.when(first)
        def _():
            sum_up[:, cols] = line

        @pl.when(jnp.logical_not(first))
        def _():
            sum_up[:, cols] += line

        grad = grad + dot(du, w_ref[1 + j], NT)
    back, lines, shifts = normal_back(hat, rstd, grad, gain)
    dx2 = grad_out + back
    dx_ref[...] = dx2
    g2 = dx2.astype(LOW)
    g2_ref[...] = g2
    do_ref[...] = dot(g2, w_ref[0], NT).astype(LOW)
    add_row(sum_down, jnp.sum(g3.astype(FULL), axis=0, keepdims=True), first)
    add_row(sum_five, jnp.sum(g2.astype(FULL), axis=0, keepdims=True), first)
    add_row(sum_gain, lines, first)
    add_row(sum_shift, shifts, first)


def feed(length, x1, mixed, cotangent, w, p, bias_up, tile=256):
    rows, width = x1.shape
    blocks = (w.shape[0] - 1) // 2
    inner = blocks * width
    part = pl.BlockSpec((tile, width), lambda i: (i, 0))
    broad = pl.BlockSpec((blocks, tile, width), lambda i: (0, i, 0))
    low = jax.ShapeDtypeStruct((rows, width), LOW)
    wide = jax.ShapeDtypeStruct((blocks, rows, width), LOW)
    line = jax.ShapeDtypeStruct((1, width), FULL)
    return calls(
        feed_kernel,
        "feed",
        2 * rows * width * (4 * inner + 2 * width),
        2 * rows * (9 * width + 2 * inner) + 4 * inner * width,
        grid=(rows // tile,),
        in_specs=[SMEM, part, part, part, ANY, whole(p.shape), whole(bias_up.shape)],
        out_specs=[part, broad, broad, part, part, part, part, part, whole((1, inner))] + [whole((1, width))] * 4,
        out_shape=[low, wide, wide, low, low, jax.ShapeDtypeStruct((rows, width), FULL), low, low,
                   jax.ShapeDtypeStruct((1, inner), FULL), line, line, line, line],
        scratch_shapes=[pltpu.VMEM(w.shape, LOW), pltpu.VMEM((tile, inner), LOW), DMA((w.shape[0],))],
    )(length, x1, mixed, cotangent, w, p, bias_up)


def unit_of(w, u):
    return pl.BlockSpec((1,) + w.shape[1:], lambda *_: (u, 0, 0))


def cross_attend_back_kernel(n_ref, q_ref, k_ref, v_ref, o_ref, g_ref, l_ref, dq_ref, dkv_ref, acc_ref):
    def store(at, grad_k, grad_v):
        dkv_ref[0, at] = grad_k
        dkv_ref[1, at] = grad_v

    h = pl.program_id(0)
    back_pair(False, k_ref.shape[1], h, n_ref[0], q_ref[0], k_ref[0], v_ref[0], o_ref[...], g_ref[...], l_ref[...], acc_ref, store)
    dq_ref[...] = acc_ref[...].astype(LOW)


def cross_attend_back(count, q, kv, mixed, grad, level):
    rows, width = mixed.shape
    enc = kv.shape[1]

    def cut(part, n):
        return pl.BlockSpec((1, n, PAIR), lambda h: (part, 0, h))

    column = pl.BlockSpec((rows, PAIR), lambda h: (0, h))
    return calls(
        cross_attend_back_kernel,
        "cross_attend_back",
        4 * 10 * rows * enc * width,
        2 * (4 * rows + 4 * enc) * width,
        grid=(width // PAIR,),
        in_specs=[SMEM, cut(0, rows), cut(0, enc), cut(1, enc), column, column, whole((rows, PAIR))],
        out_specs=[column, pl.BlockSpec((2, enc, PAIR), lambda h: (0, 0, h))],
        out_shape=[jax.ShapeDtypeStruct((rows, width), LOW), jax.ShapeDtypeStruct((2, enc, width), LOW)],
        scratch_shapes=[pltpu.VMEM((rows, PAIR), FULL)],
    )(count, q, kv, kv, mixed, grad, level)


def memory_grad_kernel(e_ref, b_ref, w_ref, o_ref, de_ref, sum_v, acc_ref):
    j = pl.program_id(0)
    o_ref[0] = dot(e_ref[...], b_ref[0], TN).astype(LOW)

    @pl.when(j == 0)
    def _():
        acc_ref[...] = dot(b_ref[0], w_ref[0], NT)

    @pl.when(j == 1)
    def _():
        de_ref[...] = (acc_ref[...] + dot(b_ref[0], w_ref[0], NT)).astype(LOW)
        sum_v[...] = jnp.sum(b_ref[0].astype(FULL), axis=0, keepdims=True)


def memory_grad(memory, dkv, w):
    count, width = memory.shape
    return calls(
        memory_grad_kernel,
        "memory_grad",
        8 * count * width * width,
        8 * width * width,
        grid=(2,),
        in_specs=[
            whole(memory.shape),
            pl.BlockSpec((1, count, width), lambda j: (j, 0, 0)),
            pl.BlockSpec((1, width, width), lambda j: (5 + j, 0, 0)),
        ],
        out_specs=[pl.BlockSpec((1, width, width), lambda j: (j, 0, 0)), whole(memory.shape), whole((1, width))],
        out_shape=[
            jax.ShapeDtypeStruct((2, width, width), LOW),
            jax.ShapeDtypeStruct((count, width), LOW),
            jax.ShapeDtypeStruct((1, width), FULL),
        ],
        scratch_shapes=[pltpu.VMEM((count, width), FULL)],
    )(memory, dkv, w)


def cross_back_kernel(x1_ref, dq_ref, dx2_ref, wq_ref, wo_ref, p_ref, dx_ref, g1_ref, do_ref,
                      sum_q, sum_out, sum_gain, sum_shift):
    first = pl.program_id(0) == 0
    grad = dot(dq_ref[...], wq_ref[0], NT) * SCALE
    hat, rstd = normal(x1_ref[...])
    back, lines, shifts = normal_back(hat, rstd, grad, p_ref[GAIN + 1 : GAIN + 2])
    dx1 = dx2_ref[...] + back
    dx_ref[...] = dx1
    g1 = dx1.astype(LOW)
    g1_ref[...] = g1
    do_ref[...] = dot(g1, wo_ref[0], NT).astype(LOW)
    add_row(sum_q, jnp.sum(dq_ref[...].astype(FULL), axis=0, keepdims=True) * SCALE, first)
    add_row(sum_out, jnp.sum(g1.astype(FULL), axis=0, keepdims=True), first)
    add_row(sum_gain, lines, first)
    add_row(sum_shift, shifts, first)


def cross_back(x1, dq, dx2, w, p, tile=256):
    rows, width = x1.shape
    part = pl.BlockSpec((tile, width), lambda i: (i, 0))
    low = jax.ShapeDtypeStruct((rows, width), LOW)
    line = jax.ShapeDtypeStruct((1, width), FULL)
    return calls(
        cross_back_kernel,
        "cross_back",
        4 * rows * width * width,
        16 * rows * width + 4 * width * width,
        grid=(rows // tile,),
        in_specs=[part, part, part, unit_of(w, 4), unit_of(w, 3), whole(p.shape)],
        out_specs=[part, part, part] + [whole((1, width))] * 4,
        out_shape=[jax.ShapeDtypeStruct((rows, width), FULL), low, low, line, line, line, line],
    )(x1, dq, dx2, w, w, p)


def self_back_kernel(x_ref, dq_ref, dkv_ref, dx1_ref, w_ref, p_ref, dx_ref, sum_q, sum_v, sum_gain, sum_shift):
    first = pl.program_id(0) == 0
    dq = dq_ref[...]
    grad = dot(dq, w_ref[0], NT) * SCALE + dot(dkv_ref[0], w_ref[1], NT) + dot(dkv_ref[1], w_ref[2], NT)
    hat, rstd = normal(x_ref[...].astype(FULL))
    back, lines, shifts = normal_back(hat, rstd, grad, p_ref[GAIN : GAIN + 1])
    dx_ref[...] = (dx1_ref[...] + back).astype(LOW)
    add_row(sum_q, jnp.sum(dq.astype(FULL), axis=0, keepdims=True) * SCALE, first)
    add_row(sum_v, jnp.sum(dkv_ref[1].astype(FULL), axis=0, keepdims=True), first)
    add_row(sum_gain, lines, first)
    add_row(sum_shift, shifts, first)


def self_back(x, dq, dkv, dx1, w, p, tile=256):
    rows, width = x.shape
    part = pl.BlockSpec((tile, width), lambda i: (i, 0))
    line = jax.ShapeDtypeStruct((1, width), FULL)
    return calls(
        self_back_kernel,
        "self_back",
        6 * rows * width * width,
        14 * rows * width + 6 * width * width,
        grid=(rows // tile,),
        in_specs=[part, part, pl.BlockSpec((2, tile, width), lambda i: (0, i, 0)), part, whole((3, width, width)), whole(p.shape)],
        out_specs=[part] + [whole((1, width))] * 4,
        out_shape=[jax.ShapeDtypeStruct((rows, width), LOW), line, line, line, line],
    )(x, dq, dkv, dx1, w, p)


AXES = ("dp", "fsdp")


def exchange(array):
    return lax.all_to_all(array, AXES, split_axis=0, concat_axis=0, tiled=True)


def leave(array, slots):
    return exchange(array.reshape(slots, -1, array.shape[-1]))


def after(value, *others):
    return lax.optimization_barrier((value, *others))[0]


def per_device(
    mesh,
    units,
    encoder,
    cotangent,
    deal,
    lengths,
    enc_counts,
    self_qkv,
    self_out,
    cross_qkv,
    cross_out,
    ffn_up,
    ffn_down,
    biases,
    ffn_bias_up,
    ffn_bias_down,
    norm_gain,
    norm_shift,
):
    slots = deal.shape[0]
    depth, ring = mesh.shape["dp"] // 2, mesh.shape["fsdp"]
    own, width = self_out.shape
    blocks = ffn_up.shape[1] // width
    inverse = jnp.zeros((slots,), jnp.int32).at[deal].set(jnp.arange(slots, dtype=jnp.int32))
    place = lax.axis_index(AXES)
    length = lax.dynamic_slice_in_dim(lengths, place, 1)
    enc_count = lax.dynamic_slice_in_dim(enc_counts, place, 1)
    tokens = units.shape[1]
    arrived = exchange(jnp.take(jnp.concatenate([units, encoder], axis=1), deal, axis=0))
    x = arrived[:, :tokens].reshape(-1, width)
    memory = arrived[:, tokens:].reshape(-1, width)

    up = ffn_up.reshape(own, slots, blocks, own).transpose(2, 0, 1, 3).reshape(blocks, own, width)
    early = jnp.concatenate([self_qkv, self_out[None], cross_qkv])
    late = jnp.concatenate([cross_out[None], up, ffn_down.reshape(blocks, own, width)])
    rows = jnp.concatenate([biases, norm_gain, norm_shift, ffn_bias_down[None]])
    flat = jnp.concatenate([rows.reshape(-1), ffn_bias_up])
    size = -(-flat.shape[0] // 2048) * 2048
    little = jnp.pad(flat, (0, size - flat.shape[0])).reshape(1, size // 128, 128)
    w_one, little = first_gather(mesh, early, little, 0)
    w_one = w_one.reshape(early.shape[0], width, width)
    flat = little.reshape(slots, size).astype(FULL)
    p = flat[:, : rows.size].reshape((slots,) + rows.shape)
    p = jnp.moveaxis(p, 0, 1).reshape(rows.shape[0], -1)
    p = jnp.pad(p, ((0, 16 - rows.shape[0]), (0, 0)))
    bias_up = flat[:, rows.size : rows.size + ffn_bias_up.size].reshape(slots, blocks, own)
    bias_up = bias_up.transpose(1, 0, 2).reshape(1, -1)

    cot = exchange(jnp.take(after(cotangent, arrived), deal, axis=0)).reshape(-1, width)
    w_two, a0, qkv, mixed0, level0, x1, a1, q1, kv1, mixed1, level1 = forward(
        mesh, length, enc_count, x, memory, w_one, p, late, 1
    )
    w_two = w_two.reshape(late.shape[0], width, width)
    (result, r, du, a2, g3, dx2, g2, grad_mixed1, bias_up_grad, bias_down_grad, bias_five, gain_two, shift_two) = feed(
        length, x1, mixed1, cot, w_two, p, bias_up
    )
    result = leave(result, slots)
    dq1, dkv1 = cross_attend_back(enc_count, q1, kv1, mixed1, grad_mixed1, level1)
    dx1, g1, grad_mixed0, bias_three, bias_two, gain_one, shift_one = cross_back(x1, dq1, dx2, w_one, p)
    made, grad_memory, bias_four = memory_grad(memory, dkv1, w_one)
    grad_memory = leave(after(grad_memory, result), slots)
    sums_one, dq0, dkv0 = feed_scatter(mesh, length, a2, g3, du, r, qkv, mixed0, grad_mixed0, level0, 2)
    dx, bias_zero, bias_one, gain_zero, shift_zero = self_back(x, dq0, dkv0, dx1, w_one, p)
    dx = leave(after(dx, grad_memory), slots)

    bias_up_grad = bias_up_grad.reshape(blocks, slots, own).transpose(1, 0, 2).reshape(slots, -1)

    def by_owner(*lines):
        return jnp.concatenate(lines).reshape(len(lines), slots, own).transpose(1, 0, 2).reshape(slots, -1)

    terms = jnp.concatenate(
        [
            by_owner(
                bias_zero, bias_one, bias_two, bias_three, bias_four, bias_five, bias_down_grad,
                gain_zero, gain_one, gain_two, shift_zero, shift_one, shift_two,
            ),
            bias_up_grad,
        ],
        axis=1,
    )
    tiny = -(-terms.shape[1] // 1024) * 8
    terms = jnp.pad(terms, ((0, 0), (0, tiny * 128 - terms.shape[1]))).reshape(depth, 2, ring * tiny, 128)
    part = ring * own
    pairs = (mixed1, g2, a1, dq1, mixed0, g1, a0, dq0, dkv0)
    sums_two, tiny_sums = last_scatter(mesh, made.reshape(2, depth, 2, part, width), pairs, terms, 3)
    flat = tiny_sums.reshape(-1)
    lines = flat[: 13 * own].reshape(13, own)
    up_sum = sums_one[:blocks].reshape(blocks, own, slots, own).transpose(1, 2, 0, 3).reshape(own, -1)
    return (
        jnp.take(result, inverse, axis=0),
        jnp.take(dx, inverse, axis=0),
        jnp.take(grad_memory, inverse, axis=0),
        sums_two[5:8],
        sums_two[4],
        jnp.concatenate([sums_two[2:3], sums_two[0:2]]),
        sums_two[3],
        up_sum,
        sums_one[blocks:].reshape(blocks * own, width),
        lines[:6],
        flat[13 * own : 13 * own + ffn_bias_up.size],
        lines[6],
        lines[7:10],
        lines[10:13],
    )


def solution(mesh):
    middle_rows = P(None, AXES, None)
    first_rows = P(AXES, None)
    last = P(None, AXES)
    weights = (middle_rows, first_rows, middle_rows, first_rows, first_rows, first_rows, last, P(AXES), P(AXES), last, last)
    return jax.shard_map(
        functools.partial(per_device, mesh),
        mesh=mesh,
        in_specs=(middle_rows,) * 3 + (P(),) * 3 + weights,
        out_specs=(middle_rows,) * 3 + weights,
        check_vma=False,
    )
```

```python
import functools

import jax
import jax.numpy as jnp
from jax import lax
from jax.experimental import pallas as pl
from jax.experimental.pallas import tpu as pltpu
from jax.sharding import PartitionSpec as P

HD = 64
EPSILON = 1e-05
SCALE = 0.125
NEGATIVE = -1e30
MESH = pl.DeviceIdType.MESH
ANY = pl.BlockSpec(memory_space=pl.ANY)
DMA = pltpu.SemaphoreType.DMA


def ring_place(f, ring):
    half = ring // 2
    upper, rest = f // half, f % half
    return upper * half + rest + upper * (half - 1 - 2 * rest)


class Place:
    def __init__(self, depth, ring):
        self.depth, self.ring, self.half = depth, ring, ring // 2
        d, f = lax.axis_index("dp"), lax.axis_index("fsdp")
        self.z, self.c, self.f = d // 2, d % 2, f
        self.at = ring_place(f, ring)
        self.right = ring_place((self.at + 1) % ring, ring)
        self.left = ring_place((self.at + ring - 1) % ring, ring)

    def greet(self):
        barrier = pltpu.get_barrier_semaphore()

        def hail(d, g):
            pl.semaphore_signal(barrier, inc=1, device_id=(d, g), device_id_type=MESH)

        for s in range(1, self.depth):
            hail((self.z + s) % self.depth * 2 + self.c, self.f)
        hail(self.z * 2 + self.c, self.right)
        hail(self.z * 2 + self.c, self.left)
        hail(self.z * 2 + 1 - self.c, self.f)
        pl.semaphore_wait(barrier, self.depth + 2)

    def peers(self):
        return 2 * self.depth * self.ring

    def peer(self, k, sign):
        dz, dc, df = k % self.depth, k // self.depth % 2, k // self.depth // 2
        z = (self.z + sign * dz + self.depth) % self.depth
        f = (self.f + sign * df + self.ring) % self.ring
        return z * 2 + (self.c + dc) % 2, f

    def greet_all(self):
        barrier = pltpu.get_barrier_semaphore()

        def hail(k):
            pl.semaphore_signal(barrier, inc=1, device_id=self.peer(k + 1, 1), device_id_type=MESH)

        loop(self.peers() - 1, hail)
        pl.semaphore_wait(barrier, self.peers() - 1)

    def to_z(self, src, dst, send, recv, s):
        return self.remote(src, dst, send, recv, (self.z + s) % self.depth * 2 + self.c, self.f)

    def to_side(self, src, dst, send, recv, way):
        return self.remote(src, dst, send, recv, self.z * 2 + self.c, (self.right, self.left)[way])

    def to_core(self, src, dst, send, recv):
        return self.remote(src, dst, send, recv, self.z * 2 + 1 - self.c, self.f)

    @staticmethod
    def remote(src, dst, send, recv, d, g):
        return pltpu.make_async_remote_copy(
            src_ref=src, dst_ref=dst, send_sem=send, recv_sem=recv,
            device_id=(d, g), device_id_type=MESH,
        )


def when(flag, run):
    if isinstance(flag, bool):
        if flag:
            run()
    else:
        pl.when(flag)(run)


def both(one, two):
    if isinstance(one, bool) and isinstance(two, bool):
        return one and two
    return jnp.logical_and(one, two)


def loop(count, run):
    def body(i, carry):
        run(i)
        return carry

    lax.fori_loop(0, count, body, 0)


class Gather:
    def __init__(self, place, count, shards, fulls, sems, ahead=2):
        self.place, self.count, self.shards, self.fulls = place, count, shards, fulls
        self.local, self.z_send, self.z_recv, self.r_send, self.r_recv, self.c_send, self.c_recv = sems
        self.ahead = min(ahead, count)

    @staticmethod
    def sems(mesh, n):
        depth, ring = mesh.shape["dp"] // 2, mesh.shape["fsdp"]
        half = ring // 2
        return [DMA((n,)), DMA((n, depth)), DMA((n, depth)), DMA((n, half, 2)), DMA((n, half, 2)), DMA((n, ring)), DMA((n, ring))]

    def chunk(self, u, zs, c, g):
        return self.fulls.at[u, zs, c, g]

    def shard(self, u):
        if callable(self.shards):
            return self.shards(u if isinstance(u, int) else 0)
        return self.shards.at[u]

    def kept(self, u):
        p = self.place
        return pltpu.make_async_copy(self.shard(u), self.chunk(u, p.z, p.c, p.f), self.local.at[u])

    def z_copy(self, u, s, incoming):
        p = self.place
        origin = (p.z + p.depth - s) % p.depth if incoming else p.z
        return p.to_z(self.shard(u), self.chunk(u, origin, p.c, p.f), self.z_send.at[u, s], self.z_recv.at[u, s], s)

    def ring_copy(self, u, t, way, incoming):
        p = self.place
        back = t - 1 + incoming
        origin = (p.at + p.ring - back) % p.ring if way == 0 else (p.at + back) % p.ring
        cut = p.depth // 2
        zs = slice(0, p.depth) if t < p.half else (slice(0, cut), slice(cut, p.depth))[way]
        piece = self.chunk(u, zs, p.c, ring_place(origin, p.ring))
        return p.to_side(piece, piece, self.r_send.at[u, t - 1, way], self.r_recv.at[u, t - 1, way], way)

    def core_copy(self, u, shift, incoming):
        p = self.place
        c = 1 - p.c if incoming else p.c
        piece = self.chunk(u, slice(0, p.depth), c, ring_place((p.at + shift) % p.ring, p.ring))
        return p.to_core(piece, piece, self.c_send.at[u, shift], self.c_recv.at[u, shift])

    def start_z(self, u):
        self.kept(u).start()
        for s in range(1, self.place.depth):
            self.z_copy(u, s, False).start()

    def start_ring(self, u, t):
        for way in range(2):
            self.ring_copy(u, t, way, 0).start()

    def start_core(self, u, t):
        half, ring = self.place.half, self.place.ring
        for shift in [0] if t == 0 else [t] if t == half else [ring - t, t]:
            self.core_copy(u, shift, False).start()

    def begin(self):
        for u in range(self.ahead):
            self.start_z(u)

    def steps(self):
        return self.count + self.place.half

    def step(self, i):
        place = self.place

        def first():
            self.kept(i).wait()
            for s in range(1, place.depth):
                self.z_copy(i, s, True).wait_recv()
            self.start_ring(i, 1)
            self.start_core(i, 0)

        def later(u, t):
            for way in range(2):
                self.ring_copy(u, t, way, 1).wait_recv()
            if t < place.half:
                self.start_ring(u, t + 1)
            self.start_core(u, t)

        when(i + self.ahead < self.count, lambda: self.start_z(i + self.ahead))
        when(i < self.count, first)
        for t in range(1, place.half + 1):
            u = i - t
            when(both(0 <= u, u < self.count), functools.partial(later, u, t))

    def finish(self):
        place = self.place

        def one(u):
            for s in range(1, place.depth):
                self.z_copy(u, s, False).wait_send()
            for t in range(1, place.half + 1):
                for way in range(2):
                    self.ring_copy(u, t, way, 0).wait_send()
            for shift in range(place.ring):
                self.core_copy(u, shift, False).wait_send()
                self.core_copy(u, shift, True).wait_recv()

        loop(self.count, one)


class Exchange:
    def __init__(self, place, arrays, steps, sems):
        self.place, self.arrays = place, arrays
        self.send, self.recv, self.local = sems
        self.each = -(-(place.peers() - 1) // steps)

    @staticmethod
    def sems(mesh, n):
        peers = 2 * (mesh.shape["dp"] // 2) * mesh.shape["fsdp"]
        return [DMA((n, peers)), DMA((n, peers)), DMA((n,))]

    def block(self, d, f):
        return d * self.place.ring + f

    def own(self, a):
        p = self.place
        src, dst = self.arrays[a]
        me = self.block(p.z * 2 + p.c, p.f)
        return pltpu.make_async_copy(src.at[me], dst.at[me], self.local.at[a])

    def copy(self, a, k, incoming):
        p = self.place
        src, dst = self.arrays[a]
        d, f = p.peer(k, 1)
        at, g = p.peer(k, -1) if incoming else (p.z * 2 + p.c, p.f)
        return p.remote(src.at[self.block(d, f)], dst.at[self.block(at, g)], self.send.at[a, k], self.recv.at[a, k], d, f)

    def begin(self):
        for a in range(len(self.arrays)):
            self.own(a).start()

    def start(self, k):
        for a in range(len(self.arrays)):
            self.copy(a, k, False).start()

    def step(self, i):
        for j in range(self.each):
            k = 1 + i * self.each + j
            when(k < self.place.peers(), functools.partial(self.start, k))

    def finish(self):
        def one(k):
            for a in range(len(self.arrays)):
                self.copy(a, k + 1, False).wait_send()
                self.copy(a, k + 1, True).wait_recv()

        loop(self.place.peers() - 1, one)
        for a in range(len(self.arrays)):
            self.own(a).wait()


class Scatter:
    def __init__(self, place, count, rows, held, put, refs, sems):
        self.place, self.count, self.rows, self.held, self.put = place, count, rows, held, put
        self.mine, self.theirs, self.rhalf, self.rfull, self.zbuf = refs
        self.c_send, self.c_recv, self.r_send, self.r_recv, self.z_send, self.z_recv = sems
        self.slots = held.shape[0]

    @staticmethod
    def refs(mesh, n, rows, cols, low):
        depth, ring = mesh.shape["dp"] // 2, mesh.shape["fsdp"]
        half, cut = ring // 2, depth // 2
        return [
            pltpu.VMEM((n, depth, ring, rows, cols), low),
            pltpu.VMEM((n, depth, ring * rows, cols), low),
            pltpu.VMEM((n, 2, cut, rows, cols), low),
            pltpu.VMEM((n, half - 1, 2, depth, rows, cols), low),
            pltpu.VMEM((n, depth - 1, rows, cols), low),
        ]

    @staticmethod
    def sems(mesh, n):
        depth, ring = mesh.shape["dp"] // 2, mesh.shape["fsdp"]
        half = ring // 2
        return [DMA((n,)), DMA((n,)), DMA((n, half, 2)), DMA((n, half, 2)), DMA((n, depth)), DMA((n, depth))]

    def core(self, u):
        p = self.place
        return p.to_core(self.held.at[u % self.slots, slice(0, p.depth), 1 - p.c], self.theirs.at[u], self.c_send.at[u], self.c_recv.at[u])

    def dest(self, t, way):
        p = self.place
        ahead = p.half - t + 1
        return ring_place((p.at + ahead) % p.ring if way == 0 else (p.at + p.ring - ahead) % p.ring, p.ring)

    def ring_copy(self, u, t, way):
        p = self.place
        g, cut = self.dest(t, way), p.depth // 2
        if t == 1:
            src = self.mine.at[u, slice(0, cut) if way == 0 else slice(cut, p.depth), g]
            dst = self.rhalf.at[u, way]
        else:
            src = self.mine.at[u, slice(0, p.depth), g]
            dst = self.rfull.at[u, t - 2, way]
        return p.to_side(src, dst, self.r_send.at[u, t - 1, way], self.r_recv.at[u, t - 1, way], way)

    def z_copy(self, u, s):
        p = self.place
        to = (p.z + s) % p.depth
        return p.to_z(self.mine.at[u, to, p.f], self.zbuf.at[u, s - 1], self.z_send.at[u, s], self.z_recv.at[u, s], s)

    def first_sum(self, u):
        p, full = self.place, jnp.float32
        self.core(u).wait_recv()

        def one(a):
            total = self.held[u % self.slots, a, p.c].astype(full) + self.theirs[u, a].astype(full)
            for g in range(p.ring):
                self.mine[u, a, g] = total[g * self.rows : (g + 1) * self.rows].astype(self.mine.dtype)

        loop(p.depth, one)
        for way in range(2):
            self.ring_copy(u, 1, way).start()

    def next_sum(self, u, t):
        p, full, mine = self.place, jnp.float32, self.mine
        for way in range(2):
            self.ring_copy(u, t, way).wait_recv()
        cut = p.depth // 2
        if t < p.half:
            for way in range(2):
                g = self.dest(t + 1, way)
                low = cut * way if t == 1 else 0
                src = self.rhalf.at[u, way] if t == 1 else self.rfull.at[u, t - 2, way]

                def one(a, g=g, low=low, src=src):
                    mine[u, low + a, g] = (mine[u, low + a, g].astype(full) + src[a].astype(full)).astype(mine.dtype)

                loop(cut if t == 1 else p.depth, one)
                self.ring_copy(u, t + 1, way).start()
        else:
            left, right = self.rfull.at[u, t - 2, 0], self.rfull.at[u, t - 2, 1]

            def one(a):
                mine[u, a, p.f] = (
                    mine[u, a, p.f].astype(full) + left[a].astype(full) + right[a].astype(full)
                ).astype(mine.dtype)

            loop(p.depth, one)
            for s in range(1, p.depth):
                self.z_copy(u, s).start()

    def last_sum(self, u):
        p, full = self.place, jnp.float32
        for s in range(1, p.depth):
            self.z_copy(u, s).wait_recv()
        total = self.mine[u, p.z, p.f].astype(full)
        for s in range(1, p.depth):
            total = total + self.zbuf[u, s - 1].astype(full)
        self.put(u, total)

    def finish(self):
        p = self.place

        def one(u):
            for t in range(1, p.half + 1):
                for way in range(2):
                    self.ring_copy(u, t, way).wait_send()
            for s in range(1, p.depth):
                self.z_copy(u, s).wait_send()

        loop(self.count, one)
        for u in range(max(0, self.count - self.slots), self.count):
            self.core(u).wait_send()

    def steps(self):
        return self.count + self.place.half // 2 + 1

    def early(self, i):
        for t in range(1, self.place.half + 1, 2):
            u = i - (t + 1) // 2
            when(both(0 <= u, u < self.count), functools.partial(self.next_sum, u, t))

    def late(self, i):
        when(i < self.count, lambda: self.first_sum(i))
        for t in range(2, self.place.half + 1, 2):
            u = i - t // 2
            when(both(0 <= u, u < self.count), functools.partial(self.next_sum, u, t))
        u = i - self.place.half // 2 - 1
        when(both(0 <= u, u < self.count), lambda: self.last_sum(u))


def remote_params(ident):
    return pltpu.CompilerParams(collective_id=ident, has_side_effects=True, vmem_limit_bytes=60 * 2**20)


def first_gather_kernel(depth, ring, where, n_w, n_x, *refs):
    weights, little, sent = refs[:n_w], refs[n_w], refs[n_w + 1 : n_w + 1 + n_x]
    full, little_full, arrived = refs[n_w + 1 + n_x], refs[n_w + 2 + n_x], refs[n_w + 3 + n_x : n_w + 3 + 2 * n_x]
    sems = refs[n_w + 3 + 2 * n_x :]
    place = Place(depth, ring)
    place.greet_all()
    count = len(where)

    def shard(u):
        which, lead = where[u]
        return weights[which] if lead is None else weights[which].at[lead]

    small = Gather(place, 1, little, little_full, sems[:7])
    big = Gather(place, count, shard, full, sems[7:14], ahead=count)
    swap = Exchange(place, tuple(zip(sent, arrived, strict=True)), max(1, big.steps() - 3), sems[14:])
    small.begin()
    big.begin()
    swap.begin()
    for i in range(big.steps()):
        swap.step(i)
        if i < small.steps():
            small.step(i)
        big.step(i)
    small.finish()
    big.finish()
    swap.finish()


def first_gather(mesh, weights, little, sent, ident):
    depth, ring = mesh.shape["dp"] // 2, mesh.shape["fsdp"]
    where = []
    for which, a in enumerate(weights):
        where += [(which, None)] if a.ndim == 2 else [(which, lead) for lead in range(a.shape[0])]
    count = len(where)

    def full(n, a):
        return jax.ShapeDtypeStruct((n, depth, 2, ring) + a.shape[-2:], a.dtype)

    same = [jax.ShapeDtypeStruct(a.shape, a.dtype) for a in sent]
    return pl.pallas_call(
        functools.partial(first_gather_kernel, depth, ring, tuple(where), len(weights), len(sent)),
        out_shape=[full(count, weights[0]), full(1, little)] + same,
        in_specs=[pl.BlockSpec(memory_space=pltpu.VMEM)] * (len(weights) + 1) + [ANY] * len(sent),
        out_specs=[ANY] * (2 + len(sent)),
        scratch_shapes=Gather.sems(mesh, 1) + Gather.sems(mesh, count) + Exchange.sems(mesh, len(sent)),
        compiler_params=remote_params(ident),
        cost_estimate=pl.CostEstimate(flops=60_000_000_000, bytes_accessed=2 * 33_554_432, transcendentals=0),
        name="first_gather",
    )(*weights, little, *sent)


def deal_kernel(out_of, n, deal_ref, *refs):
    sources, dests, held, sem = refs[:n], refs[n : 2 * n], refs[2 * n : 3 * n], refs[3 * n]
    slots = deal_ref.shape[0]

    def load(a, i):
        return pltpu.make_async_copy(sources[a].at[i if out_of else deal_ref[i]], held[a].at[i], sem.at[0, a, i])

    def store(a, i):
        return pltpu.make_async_copy(held[a].at[i], dests[a].at[deal_ref[i] if out_of else i], sem.at[1, a, i])

    def begin(i):
        for a in range(n):
            load(a, i).start()

    def turn(i):
        for a in range(n):
            load(a, i).wait()
            store(a, i).start()

    def end(i):
        for a in range(n):
            store(a, i).wait()

    loop(slots, begin)
    loop(slots, turn)
    loop(slots, end)


def deal_blocks(deal, arrays, out_of, name):
    n = len(arrays)
    return pl.pallas_call(
        functools.partial(deal_kernel, out_of, n),
        out_shape=[jax.ShapeDtypeStruct(a.shape, a.dtype) for a in arrays],
        in_specs=[pl.BlockSpec(memory_space=pltpu.SMEM)] + [ANY] * n,
        out_specs=[ANY] * n,
        scratch_shapes=[pltpu.VMEM(a.shape, a.dtype) for a in arrays] + [DMA((2, n, deal.shape[0]))],
        compiler_params=pltpu.CompilerParams(vmem_limit_bytes=60 * 2**20),
        name=name,
    )(deal, *arrays)


NN = (((1,), (0,)), ((), ()))
NT = (((1,), (1,)), ((), ()))
TN = (((0,), (0,)), ((), ()))
LOW = jnp.bfloat16
FULL = jnp.float32
SMEM = pl.BlockSpec(memory_space=pltpu.SMEM)
VMEM = pl.BlockSpec(memory_space=pltpu.VMEM)
PAIR = 2 * HD
ROOM = 60 * 2**20


def dot(left, right, how):
    return lax.dot_general(left, right, how, preferred_element_type=FULL)


def calls(kernel, name, flops, moved, **kw):
    return pl.pallas_call(
        kernel,
        name=name,
        compiler_params=pltpu.CompilerParams(vmem_limit_bytes=ROOM),
        cost_estimate=pl.CostEstimate(flops=int(flops), bytes_accessed=int(moved), transcendentals=0),
        **kw,
    )


def whole(shape):
    return pl.BlockSpec(shape, lambda *_: (0,) * len(shape))


def normal(x):
    mean = jnp.mean(x, axis=-1, keepdims=True)
    centred = x - mean
    rstd = lax.rsqrt(jnp.mean(centred * centred, axis=-1, keepdims=True) + EPSILON)
    return centred * rstd, rstd


def normal_back(hat, rstd, grad, gain):
    scaled = grad * gain
    lean = jnp.mean(scaled, axis=-1, keepdims=True)
    tilt = jnp.mean(scaled * hat, axis=-1, keepdims=True)
    back = rstd * (scaled - lean - hat * tilt)
    return back, jnp.sum(grad * hat, axis=0, keepdims=True), jnp.sum(grad, axis=0, keepdims=True)


GAIN, SHIFT, DOWN = 6, 9, 12


def lanes(shape):
    return lax.broadcasted_iota(jnp.int32, shape, len(shape) - 1)


def rows_of(shape):
    return lax.broadcasted_iota(jnp.int32, shape, 0)


def head_mask(head):
    return jnp.where(lanes((1, PAIR)) // HD == head, 1.0, 0.0).astype(LOW)


def thirds(x):
    one = x.astype(LOW).astype(FULL)
    two = (x - one).astype(LOW).astype(FULL)
    return one, two, x - one - two


def wide_keys(k, v, n):
    count = k.shape[0]
    shut = jnp.where((lanes((count, PAIR)) == 0) & (rows_of((count, PAIR)) >= n), NEGATIVE, 0.0).astype(LOW)
    ones = jnp.ones((count, PAIR), LOW)
    return [
        (jnp.concatenate([k * head_mask(h), shut], axis=1), jnp.concatenate([v * head_mask(h), ones], axis=1))
        for h in range(2)
    ]


def attend_pair(causal, tile, h, n, q, k, v, store, l_ref):
    queries, count = q.shape[0], k.shape[0]
    first = jnp.where(lanes((queries, PAIR)) == 0, 1.0, 0.0).astype(LOW)
    wide_q = jnp.concatenate([q, first], axis=1)
    spots = lanes((tile, PAIR))
    heads = wide_keys(k, v, n)
    for i in range(queries // tile):
        at = slice(i * tile, (i + 1) * tile)
        seen = (i + 1) * tile if causal else count
        mixed = jnp.zeros((tile, PAIR), FULL)
        kept = l_ref[at]
        for head, (keys, values) in enumerate(heads):
            scores = dot(wide_q[at], keys[:seen], NT)
            if causal:
                square = (tile, tile)
                last = jnp.where(lanes(square) <= rows_of(square), scores[:, seen - tile :], NEGATIVE)
                scores = last if seen == tile else jnp.concatenate([scores[:, : seen - tile], last], axis=1)
            top = jnp.max(scores, axis=1, keepdims=True)
            weights = jnp.exp(scores - top).astype(LOW)
            sums = dot(weights, values[:seen], NN)
            total = sums[:, PAIR:]
            mixed = mixed + sums[:, :PAIR] / total
            kept = jnp.where(spots == 2 * h + head, top + jnp.log(total), kept)
        store(at, mixed.astype(LOW))
        l_ref[at] = kept


def parts_of(value, heads, spare):
    lane = lanes(value.shape)
    shown = jnp.where(lane < heads, value, 0.0)
    shown = shown + pltpu.roll(shown, heads, 1) + pltpu.roll(shown, 2 * heads, 1)
    one, two, three = thirds(-shown)
    part = jnp.where(lane < heads, one, jnp.where(lane < 2 * heads, two, three))
    return jnp.where(lane == 3 * heads, spare, part).astype(LOW)


def take_part(head, heads):
    lane = lanes((1, PAIR))
    return jnp.where((lane < 3 * heads) & (lane % heads == head), 1.0, 0.0)


def forward_kernel(
    depth, ring, count, n_ref, m_ref, x_hbm, e_hbm, w_hbm, p_ref, shard, sent,
    full, arrived, a0_hbm, qkv_hbm, o0_hbm, l0_hbm, x1_hbm, a1_hbm, q1_hbm, kv_hbm, o1_hbm, l1_hbm,
    x_ref, e_ref, w_ref, a_ref, qkv_ref, o_ref, l0_ref, x1_ref, q1_ref, kv_ref, l1_ref, a1_ref, lp_ref,
    w_sem, in_sem, out_sem, *sems,
):
    place = Place(depth, ring)
    place.greet_all()
    gather = Gather(place, count, shard, full, sems[:7], ahead=count)
    swap = Exchange(place, ((sent, arrived),), gather.steps() - 2, sems[7:])
    gather.begin()
    swap.begin()

    def advance(i):
        swap.step(i)
        gather.step(i)

    rows, width = x_ref.shape
    tile = 256
    load_x = pltpu.make_async_copy(x_hbm, x_ref, in_sem.at[0])
    load_e = pltpu.make_async_copy(e_hbm, e_ref, in_sem.at[1])
    load_x.start()
    parts = w_ref.shape[0]
    loads = [pltpu.make_async_copy(w_hbm.at[u], w_ref.at[u], w_sem.at[u]) for u in range(parts)]
    for load in loads[:3]:
        load.start()
    load_e.start()
    for load in loads[3:]:
        load.start()
    leaving = []

    def send(src, dst):
        copy = pltpu.make_async_copy(src, dst, out_sem.at[len(leaving)])
        copy.start()
        leaving.append(copy)

    l0_ref[...] = jnp.zeros_like(l0_ref)
    l1_ref[...] = jnp.zeros_like(l1_ref)
    load_x.wait()
    advance(0)
    for i in range(rows // tile):
        at = slice(i * tile, (i + 1) * tile)
        hat, _ = normal(x_ref[at].astype(FULL))
        a_ref[at] = (hat * p_ref[GAIN : GAIN + 1] + p_ref[SHIFT : SHIFT + 1]).astype(LOW)
    send(a_ref, a0_hbm)
    for j in range(3):
        loads[j].wait()
        bias = (p_ref[0:1], None, p_ref[1:2])[j]

        def project(i, j=j, bias=bias):
            at = pl.ds(pl.multiple_of(i * 2 * tile, 2 * tile), 2 * tile)
            y = dot(a_ref[at], w_ref[j], NN)
            if bias is not None:
                y = y + bias
            qkv_ref[j, at] = (y * SCALE if j == 0 else y).astype(LOW)

        loop(rows // (2 * tile), project)
        send(qkv_ref.at[j], qkv_hbm.at[j])
        if j == 1:
            advance(1)

    pairs = width // PAIR

    def self_pair(h):
        cols = pl.ds(pl.multiple_of(h * PAIR, PAIR), PAIR)

        def store(at, value):
            o_ref[at, cols] = value

        attend_pair(True, tile, h, n_ref[0], qkv_ref[0, :, cols], qkv_ref[1, :, cols], qkv_ref[2, :, cols], store, l0_ref)
        when(h % 2 == 0, lambda: advance(2 + h // 2))

    loop(pairs, self_pair)
    send(o_ref, o0_hbm)
    heads = 2 * pairs
    lp_ref[0] = parts_of(l0_ref[...], heads, 1.0)
    send(lp_ref.at[0], l0_hbm)
    done = 2 + (pairs + 1) // 2
    loads[3].wait()
    loads[4].wait()

    def middle_part(i):
        at = pl.ds(pl.multiple_of(i * tile, tile), tile)
        x1 = x_ref[at].astype(FULL) + (dot(o_ref[at], w_ref[3], NN) + p_ref[2:3])
        x1_ref[at] = x1
        hat, _ = normal(x1)
        a = (hat * p_ref[GAIN + 1 : GAIN + 2] + p_ref[SHIFT + 1 : SHIFT + 2]).astype(LOW)
        a1_ref[at] = a
        q1_ref[at] = ((dot(a, w_ref[4], NN) + p_ref[3:4]) * SCALE).astype(LOW)
        when(i % 2 == 1, lambda: advance(done + i // 2))

    loop(rows // tile, middle_part)
    done = done + rows // tile // 2
    send(x1_ref, x1_hbm)
    send(a1_ref, a1_hbm)
    send(q1_ref, q1_hbm.at[0])
    load_e.wait()
    for j in range(2):
        loads[5 + j].wait()
        y = dot(e_ref[...], w_ref[5 + j], NN)
        kv_ref[j] = (y + p_ref[4:5] if j == 1 else y).astype(LOW)
    send(kv_ref, kv_hbm)
    leaving[4].wait()

    def cross_pair(h):
        cols = pl.ds(pl.multiple_of(h * PAIR, PAIR), PAIR)

        def store(at, value):
            o_ref[at, cols] = value

        attend_pair(False, tile, h, m_ref[0], q1_ref[:, cols], kv_ref[0, :, cols], kv_ref[1, :, cols], store, l1_ref)
        when(h % 2 == 0, lambda: advance(done + h // 2))

    loop(pairs, cross_pair)
    done = done + (pairs + 1) // 2
    send(o_ref, o1_hbm)
    lp_ref[1] = parts_of(l1_ref[...], heads, 1.0)
    send(lp_ref.at[1], l1_hbm)
    for i in range(done, gather.steps()):
        advance(i)
    gather.finish()
    swap.finish()
    for k, copy in enumerate(leaving):
        if k != 4:
            copy.wait()


def forward(mesh, length, enc_count, x, memory, w, p, shards, sent, ident):
    depth, ring = mesh.shape["dp"] // 2, mesh.shape["fsdp"]
    count = shards.shape[0]
    rows, width = x.shape
    enc = memory.shape[0]
    low = jax.ShapeDtypeStruct((rows, width), LOW)
    level = jax.ShapeDtypeStruct((rows, PAIR), LOW)
    out_shape = [
        jax.ShapeDtypeStruct((count, depth, 2, ring) + shards.shape[1:], LOW),
        jax.ShapeDtypeStruct(sent.shape, sent.dtype),
        low,
        jax.ShapeDtypeStruct((3, rows, width), LOW),
        low,
        level,
        jax.ShapeDtypeStruct((rows, width), FULL),
        low,
        jax.ShapeDtypeStruct((1, rows, width), LOW),
        jax.ShapeDtypeStruct((2, enc, width), LOW),
        low,
        level,
    ]
    big = pltpu.VMEM((rows, width), LOW)
    return pl.pallas_call(
        functools.partial(forward_kernel, depth, ring, count),
        out_shape=out_shape,
        in_specs=[SMEM, SMEM, ANY, ANY, ANY, VMEM, VMEM, ANY],
        out_specs=[ANY] * len(out_shape),
        scratch_shapes=[
            big,
            pltpu.VMEM((enc, width), LOW),
            pltpu.VMEM(w.shape, LOW),
            big,
            pltpu.VMEM((3, rows, width), LOW),
            big,
            pltpu.VMEM((rows, PAIR), FULL),
            pltpu.VMEM((rows, width), FULL),
            big,
            pltpu.VMEM((2, enc, width), LOW),
            pltpu.VMEM((rows, PAIR), FULL),
            big,
            pltpu.VMEM((2, rows, PAIR), LOW),
            DMA((w.shape[0],)),
            DMA((2,)),
            DMA((12,)),
        ]
        + Gather.sems(mesh, count)
        + Exchange.sems(mesh, 1),
        compiler_params=remote_params(ident),
        cost_estimate=pl.CostEstimate(flops=70_000_000_000, bytes_accessed=2 * 33_554_432, transcendentals=0),
        name="forward_gather",
    )(length, enc_count, x, memory, w, p, shards, sent)


def back_pair(causal, tile, h, heads, n, q, k, v, grad, level, inner, acc_ref, store):
    queries, count = q.shape[0], k.shape[0]
    acc_ref[...] = jnp.zeros_like(acc_ref)
    wide_q = jnp.concatenate([q, level], axis=1)
    wide_g = jnp.concatenate([grad, inner], axis=1)
    shut = jnp.where(rows_of((count, PAIR)) >= n, NEGATIVE, 0.0)
    both_heads = []
    for head in range(2):
        mask = head_mask(head)
        mine = take_part(2 * h + head, heads)
        open_k = jnp.where(lanes((count, PAIR)) == 3 * heads, shut, mine).astype(LOW)
        open_v = jnp.broadcast_to(mine, (count, PAIR)).astype(LOW)
        wide_k = jnp.concatenate([k * mask, open_k], axis=1)
        wide_v = jnp.concatenate([v * mask, open_v], axis=1)
        both_heads.append((wide_k, wide_v, q * mask, grad * mask, k * mask))
    for i in range(count // tile):
        at = slice(i * tile, (i + 1) * tile)
        low = i * tile if causal else 0
        grad_k = jnp.zeros((tile, PAIR), FULL)
        grad_v = jnp.zeros((tile, PAIR), FULL)
        for wide_k, wide_v, q_one, g_one, k_one in both_heads:
            scores = dot(wide_k[at], wide_q[low:], NT)
            if causal:
                square = (tile, tile)
                near = jnp.where(rows_of(square) <= lanes(square), scores[:, :tile], NEGATIVE)
                scores = near if low + tile == queries else jnp.concatenate([near, scores[:, tile:]], axis=1)
            probs = jnp.exp(scores)
            slope = (probs * dot(wide_v[at], wide_g[low:], NT)).astype(LOW)
            grad_v = grad_v + dot(probs.astype(LOW), g_one[low:], NN)
            grad_k = grad_k + dot(slope, q_one[low:], NN)
            acc_ref[low:] += dot(slope, k_one[at], TN)
        store(at, grad_k.astype(LOW), grad_v.astype(LOW))


def inner_parts(grad, mixed, heads):
    width = grad.shape[1]
    product = grad.astype(FULL) * mixed.astype(FULL)
    head = (rows_of((width, PAIR)) // HD == lanes((width, PAIR))).astype(FULL).astype(LOW)
    high = product.astype(LOW)
    rest = product - high.astype(FULL)
    return parts_of(dot(high, head, NN) + dot(rest.astype(LOW), head, NN), heads, 0.0)


def unit_grad(place, held, slot, a_ref, b_ref, scale):
    depth, part = held.shape[1], held.shape[3]
    width = a_ref.shape[1]
    piece = width // 2
    for m in range(2):
        value = dot(a_ref[:, m * piece : (m + 1) * piece], b_ref[...], TN)
        if scale is not None:
            value = value * scale
        value = value.astype(LOW)
        for k in range(piece // part):
            at = m * (piece // part) + k
            held[slot, at // 2, at % 2] = value[k * part : (k + 1) * part]


def feed_scatter_kernel(
    depth, ring, n_ref, a2_hbm, g3_hbm, du_hbm, r_hbm, qkv_hbm, grad_hbm, l_ref, i_ref, sent,
    outs, dq_hbm, dkv_hbm, arrived,
    a2_ref, g3_ref, moving, held, q_buf, acc_ref, dq_buf, dkv_buf, in_sem, move_sem, q_sem, out_sem, *rest,
):
    place = Place(depth, ring)
    place.greet_all()
    blocks = du_hbm.shape[0]
    count = 2 * blocks

    def put_sum(u, total):
        outs[u] = total

    sums = Scatter(place, count, outs.shape[1], held, put_sum, rest[:5], rest[5:11])
    swap = Exchange(place, ((sent, arrived),), count, rest[11:])
    pairs = grad_hbm.shape[1] // PAIR
    swap.begin()
    slots = held.shape[0]
    load_a = pltpu.make_async_copy(a2_hbm, a2_ref, in_sem.at[0])
    load_g = pltpu.make_async_copy(g3_hbm, g3_ref, in_sem.at[1])

    def move(u, array, j):
        return pltpu.make_async_copy(array.at[j], moving.at[u % 2], move_sem.at[u % 2])

    def start_move(u):
        when(u < blocks, lambda: move(u, du_hbm, u).start())
        when(u >= blocks, lambda: move(u, r_hbm, jnp.maximum(u - blocks, 0)).start())

    def fetch(h):
        cols = pl.ds(pl.multiple_of(h * PAIR, PAIR), PAIR)
        sources = [qkv_hbm.at[0, :, cols], qkv_hbm.at[1, :, cols], qkv_hbm.at[2, :, cols], grad_hbm.at[:, cols]]
        return [pltpu.make_async_copy(s, q_buf.at[h % 2, k], q_sem.at[h % 2, k]) for k, s in enumerate(sources)]

    def put(h):
        cols = pl.ds(pl.multiple_of(h * PAIR, PAIR), PAIR)
        return [
            pltpu.make_async_copy(dq_buf.at[h % 2], dq_hbm.at[:, cols], out_sem.at[h % 2, 0]),
            pltpu.make_async_copy(dkv_buf.at[h % 2], dkv_hbm.at[:, :, cols], out_sem.at[h % 2, 1]),
        ]

    load_a.start()
    start_move(0)
    for copy in fetch(0):
        copy.start()
    load_g.start()
    load_a.wait()

    def weights(i):
        when(i + 1 < count, lambda: start_move(i + 1))
        when(i == blocks, load_g.wait)
        move(i, du_hbm, 0).wait()
        when(i >= slots, lambda: sums.core(i - slots).wait_send())
        slot = i % slots
        when(i < blocks, lambda: unit_grad(place, held, slot, a2_ref, moving.at[i % 2], None))
        when(i >= blocks, lambda: unit_grad(place, held, slot, moving.at[i % 2], g3_ref, None))
        sums.core(i).start()

    def heads(h):
        def next_fetch():
            for copy in fetch(h + 1):
                copy.start()

        when(h + 1 < pairs, next_fetch)
        for copy in fetch(h):
            copy.wait()

        def free():
            for copy in put(h - 2):
                copy.wait()

        when(h >= 2, free)
        b = h % 2

        def store(at, grad_k, grad_v):
            dkv_buf[b, 0, at] = grad_k
            dkv_buf[b, 1, at] = grad_v

        back_pair(True, 256, h, 2 * pairs, n_ref[0], q_buf[b, 0], q_buf[b, 1], q_buf[b, 2], q_buf[b, 3], l_ref[...], i_ref[...], acc_ref, store)
        dq_buf[b] = acc_ref[...].astype(LOW)
        for copy in put(h):
            copy.start()

    def step(i):
        when(i < count, lambda: weights(i))
        sums.early(i)
        when(i < pairs, lambda: heads(i))
        sums.late(i)
        swap.step(i)

    loop(max(sums.steps(), pairs), step)
    for h in range(max(0, pairs - 2), pairs):
        for copy in put(h):
            copy.wait()
    sums.finish()
    swap.finish()


def feed_scatter(mesh, length, a2, g3, du, r, qkv, grad, level, inner, sent, ident):
    depth, ring = mesh.shape["dp"] // 2, mesh.shape["fsdp"]
    blocks, rows, width = du.shape
    own = width // (2 * depth * ring)
    count = 2 * blocks
    big = pltpu.VMEM((rows, width), LOW)
    return pl.pallas_call(
        functools.partial(feed_scatter_kernel, depth, ring),
        out_shape=[
            jax.ShapeDtypeStruct((count, own, width), FULL),
            jax.ShapeDtypeStruct((rows, width), LOW),
            jax.ShapeDtypeStruct((2, rows, width), LOW),
            jax.ShapeDtypeStruct(sent.shape, sent.dtype),
        ],
        in_specs=[SMEM] + [ANY] * 6 + [VMEM, VMEM, ANY],
        out_specs=[VMEM, ANY, ANY, ANY],
        scratch_shapes=[
            big,
            big,
            pltpu.VMEM((2, rows, width), LOW),
            pltpu.VMEM((3, depth, 2, ring * own, width), LOW),
            pltpu.VMEM((2, 4, rows, PAIR), LOW),
            pltpu.VMEM((rows, PAIR), FULL),
            pltpu.VMEM((2, rows, PAIR), LOW),
            pltpu.VMEM((2, 2, rows, PAIR), LOW),
            DMA((2,)),
            DMA((2,)),
            DMA((2, 4)),
            DMA((2, 2)),
        ]
        + Scatter.refs(mesh, count, own, width, LOW)
        + Scatter.sems(mesh, count)
        + Exchange.sems(mesh, 1),
        compiler_params=remote_params(ident),
        cost_estimate=pl.CostEstimate(flops=60_000_000_000, bytes_accessed=2 * 33_554_432, transcendentals=0),
        name="feed_scatter",
    )(length, a2, g3, du, r, qkv, grad, level, inner, sent)


def last_scatter_kernel(
    depth, ring, made_hbm, o1_hbm, g2_hbm, a1_hbm, dq1_hbm, o0_hbm, g1_hbm, a0_hbm, dq0_hbm, dkv_hbm, tiny_ref, sent,
    s_qkv, s_out, c_qkv, c_out, tiny_out, arrived, left, right, held, tiny_held, left_sem, right_sem, made_sem, *rest,
):
    place = Place(depth, ring)
    place.greet_all()
    made = made_hbm.shape[0]
    spots = [c_qkv.at[1], c_qkv.at[2], c_qkv.at[0], c_out, s_out, s_qkv.at[0], s_qkv.at[1], s_qkv.at[2]]

    def put_sum(u, total):
        spots[u][...] = total

    def put_tiny(u, total):
        tiny_out[u] = total

    pairs = [(a1_hbm, dq1_hbm), (o1_hbm, g2_hbm), (o0_hbm, g1_hbm), (a0_hbm, dq0_hbm), (a0_hbm, dkv_hbm.at[0]), (a0_hbm, dkv_hbm.at[1])]
    scaled = (0, 3)
    count = made + len(pairs)
    small = Scatter(place, 1, tiny_out.shape[1], tiny_held, put_tiny, rest[:5], rest[5:11])
    sums = Scatter(place, count, s_out.shape[0], held, put_sum, rest[11:16], rest[16:22])
    swap = Exchange(place, ((sent, arrived),), count, rest[22:])
    swap.begin()
    slots = held.shape[0]

    def load(k):
        a, b = pairs[k]
        return [
            pltpu.make_async_copy(a, left.at[k % 2], left_sem.at[k % 2]),
            pltpu.make_async_copy(b, right.at[k % 2], right_sem.at[k % 2]),
        ]

    given = [pltpu.make_async_copy(made_hbm.at[u], held.at[u], made_sem.at[u]) for u in range(made)]
    for copy in given:
        copy.start()
    for k in range(2):
        for copy in load(k):
            copy.start()
    tiny_held[0] = tiny_ref[...]
    small.core(0).start()
    for i in range(sums.steps()):
        if i < count:
            k = i - made
            if i < made:
                given[i].wait()
            else:
                for copy in load(k):
                    copy.wait()
                if i >= slots:
                    sums.core(i - slots).wait_send()
                unit_grad(place, held, i % slots, left.at[k % 2], right.at[k % 2], SCALE if k in scaled else None)
                if k + 2 < len(pairs):
                    for copy in load(k + 2):
                        copy.start()
            sums.core(i).start()
        if i < small.steps():
            small.early(i)
        sums.early(i)
        if i < small.steps():
            small.late(i)
        sums.late(i)
        swap.step(i)
    small.finish()
    sums.finish()
    swap.finish()


def last_scatter(mesh, made, pairs, tiny, sent, ident):
    depth, ring = mesh.shape["dp"] // 2, mesh.shape["fsdp"]
    n, width = made.shape[0], made.shape[-1]
    rows = pairs[0].shape[0]
    own = made.shape[3] // ring
    count = n + 6
    tiny_rows = tiny.shape[2] // ring
    return pl.pallas_call(
        functools.partial(last_scatter_kernel, depth, ring),
        out_shape=[
            jax.ShapeDtypeStruct((3, own, width), FULL),
            jax.ShapeDtypeStruct((own, width), FULL),
            jax.ShapeDtypeStruct((3, own, width), FULL),
            jax.ShapeDtypeStruct((own, width), FULL),
            jax.ShapeDtypeStruct((1, tiny_rows, tiny.shape[3]), FULL),
            jax.ShapeDtypeStruct(sent.shape, sent.dtype),
        ],
        in_specs=[ANY] * (1 + len(pairs)) + [VMEM, ANY],
        out_specs=[VMEM] * 5 + [ANY],
        scratch_shapes=[
            pltpu.VMEM((2, rows, width), LOW),
            pltpu.VMEM((2, rows, width), LOW),
            pltpu.VMEM((3,) + made.shape[1:], LOW),
            pltpu.VMEM((1,) + tiny.shape, FULL),
            DMA((2,)),
            DMA((2,)),
            DMA((n,)),
        ]
        + Scatter.refs(mesh, 1, tiny_rows, tiny.shape[3], FULL)
        + Scatter.sems(mesh, 1)
        + Scatter.refs(mesh, count, own, width, LOW)
        + Scatter.sems(mesh, count)
        + Exchange.sems(mesh, 1),
        compiler_params=remote_params(ident),
        cost_estimate=pl.CostEstimate(flops=60_000_000_000, bytes_accessed=2 * 33_554_432, transcendentals=0),
        name="last_scatter",
    )(made, *pairs, tiny, sent)


CUBIC = 0.044715
ROOT = 0.7978845608028654


def feed_kernel(
    n_ref, x1_ref, o_ref, g_ref, w_hbm, p_ref, bu_ref,
    out_ref, r_ref, du_ref, a_ref, g3_ref, dx_ref, g2_ref, do_ref, inner_ref,
    sum_up, sum_down, sum_five, sum_gain, sum_shift,
    w_ref, slope_ref, sems,
):
    i = pl.program_id(0)
    first = i == 0
    tile, width = x1_ref.shape
    blocks = (w_hbm.shape[0] - 1) // 2
    order = [0] + [k * blocks + j + 1 for j in range(blocks) for k in range(2)]
    loads = {u: pltpu.make_async_copy(w_hbm.at[u], w_ref.at[u], sems.at[u]) for u in order}

    @pl.when(first)
    def _():
        for u in order:
            loads[u].start()
        for ref in (sum_up, sum_down, sum_five, sum_gain, sum_shift):
            ref[...] = jnp.zeros_like(ref)
        loads[0].wait()

    valid = jnp.where(i * tile + rows_of((tile, 1)) < n_ref[0], 1.0, 0.0)
    x2 = x1_ref[...] + (dot(o_ref[...], w_ref[0], NN) + p_ref[5:6])
    hat, rstd = normal(x2)
    gain = p_ref[GAIN + 2 : GAIN + 3]
    a_ref[...] = (hat * gain + p_ref[SHIFT + 2 : SHIFT + 3]).astype(LOW)

    @pl.when(first)
    def _():
        for u in order[1:]:
            loads[u].wait()

    total = x2 + p_ref[DOWN : DOWN + 1]
    for j in range(blocks):
        cols = slice(j * width, (j + 1) * width)
        u = dot(a_ref[...], w_ref[1 + j], NN) + bu_ref[:, cols]
        square = u * u
        t = jnp.tanh(ROOT * (u * (1.0 + CUBIC * square)))
        half = 0.5 * (1.0 + t)
        r = (u * half).astype(LOW)
        r_ref[j] = r
        slope = half + 0.5 * u * (1.0 - t * t) * (ROOT * (1.0 + 3.0 * CUBIC * square))
        slope_ref[:, cols] = slope.astype(LOW)
        total = total + dot(r, w_ref[1 + blocks + j], NN)
    out_ref[...] = (total * valid).astype(LOW)
    grad_out = g_ref[...].astype(FULL) * valid
    g3 = grad_out.astype(LOW)
    g3_ref[...] = g3
    grad = jnp.zeros((tile, width), FULL)
    for j in range(blocks):
        cols = slice(j * width, (j + 1) * width)
        du = (dot(g3, w_ref[1 + blocks + j], NT) * slope_ref[:, cols].astype(FULL)).astype(LOW)
        du_ref[j] = du
        line = jnp.sum(du.astype(FULL), axis=0, keepdims=True)

        sum_up[:, cols] += line
        grad = grad + dot(du, w_ref[1 + j], NT)
    back, lines, shifts = normal_back(hat, rstd, grad, gain)
    dx2 = grad_out + back
    dx_ref[...] = dx2
    g2 = dx2.astype(LOW)
    g2_ref[...] = g2
    grad_mixed = dot(g2, w_ref[0], NT).astype(LOW)
    do_ref[...] = grad_mixed
    inner_ref[...] = inner_parts(grad_mixed, o_ref[...], width // HD)
    sum_down[...] += jnp.sum(g3.astype(FULL), axis=0, keepdims=True)
    sum_five[...] += jnp.sum(g2.astype(FULL), axis=0, keepdims=True)
    sum_gain[...] += lines
    sum_shift[...] += shifts


def feed(length, x1, mixed, cotangent, w, p, bias_up, tile=256):
    rows, width = x1.shape
    blocks = (w.shape[0] - 1) // 2
    inner = blocks * width
    part = pl.BlockSpec((tile, width), lambda i: (i, 0))
    broad = pl.BlockSpec((blocks, tile, width), lambda i: (0, i, 0))
    thin = pl.BlockSpec((tile, PAIR), lambda i: (i, 0))
    low = jax.ShapeDtypeStruct((rows, width), LOW)
    wide = jax.ShapeDtypeStruct((blocks, rows, width), LOW)
    line = jax.ShapeDtypeStruct((1, width), FULL)
    return calls(
        feed_kernel,
        "feed",
        2 * rows * width * (4 * inner + 2 * width),
        2 * rows * (9 * width + 2 * inner) + 4 * inner * width,
        grid=(rows // tile,),
        in_specs=[SMEM, part, part, part, ANY, whole(p.shape), whole(bias_up.shape)],
        out_specs=[part, broad, broad, part, part, part, part, part, thin, whole((1, inner))] + [whole((1, width))] * 4,
        out_shape=[low, wide, wide, low, low, jax.ShapeDtypeStruct((rows, width), FULL), low, low,
                   jax.ShapeDtypeStruct((rows, PAIR), LOW), jax.ShapeDtypeStruct((1, inner), FULL), line, line, line, line],
        scratch_shapes=[pltpu.VMEM(w.shape, LOW), pltpu.VMEM((tile, inner), LOW), DMA((w.shape[0],))],
    )(length, x1, mixed, cotangent, w, p, bias_up)


def unit_of(w, u):
    return pl.BlockSpec((1,) + w.shape[1:], lambda *_: (u, 0, 0))


def cross_attend_back_kernel(heads, n_ref, q_ref, k_ref, v_ref, g_ref, l_ref, i_ref, dq_ref, dkv_ref, acc_ref):
    def store(at, grad_k, grad_v):
        dkv_ref[0, at] = grad_k
        dkv_ref[1, at] = grad_v

    h = pl.program_id(0)
    back_pair(False, k_ref.shape[1], h, heads, n_ref[0], q_ref[0], k_ref[0], v_ref[0], g_ref[...], l_ref[...], i_ref[...], acc_ref, store)
    dq_ref[...] = acc_ref[...].astype(LOW)


def cross_attend_back(count, q, kv, grad, level, inner):
    rows, width = grad.shape
    enc = kv.shape[1]

    def cut(part, n):
        return pl.BlockSpec((1, n, PAIR), lambda h: (part, 0, h))

    column = pl.BlockSpec((rows, PAIR), lambda h: (0, h))
    return calls(
        functools.partial(cross_attend_back_kernel, width // HD),
        "cross_attend_back",
        4 * 10 * rows * enc * width,
        2 * (4 * rows + 4 * enc) * width,
        grid=(width // PAIR,),
        in_specs=[SMEM, cut(0, rows), cut(0, enc), cut(1, enc), column, whole((rows, PAIR)), whole((rows, PAIR))],
        out_specs=[column, pl.BlockSpec((2, enc, PAIR), lambda h: (0, 0, h))],
        out_shape=[jax.ShapeDtypeStruct((rows, width), LOW), jax.ShapeDtypeStruct((2, enc, width), LOW)],
        scratch_shapes=[pltpu.VMEM((rows, PAIR), FULL)],
    )(count, q, kv, kv, grad, level, inner)


def memory_grad_kernel(e_ref, b_ref, w_ref, o_ref, de_ref, sum_v, acc_ref):
    j = pl.program_id(0)
    o_ref[0] = dot(e_ref[...], b_ref[0], TN).astype(LOW)

    @pl.when(j == 0)
    def _():
        acc_ref[...] = dot(b_ref[0], w_ref[0], NT)

    @pl.when(j == 1)
    def _():
        de_ref[...] = (acc_ref[...] + dot(b_ref[0], w_ref[0], NT)).astype(LOW)
        sum_v[...] = jnp.sum(b_ref[0].astype(FULL), axis=0, keepdims=True)


def memory_grad(memory, dkv, w):
    count, width = memory.shape
    return calls(
        memory_grad_kernel,
        "memory_grad",
        8 * count * width * width,
        8 * width * width,
        grid=(2,),
        in_specs=[
            whole(memory.shape),
            pl.BlockSpec((1, count, width), lambda j: (j, 0, 0)),
            pl.BlockSpec((1, width, width), lambda j: (5 + j, 0, 0)),
        ],
        out_specs=[pl.BlockSpec((1, width, width), lambda j: (j, 0, 0)), whole(memory.shape), whole((1, width))],
        out_shape=[
            jax.ShapeDtypeStruct((2, width, width), LOW),
            jax.ShapeDtypeStruct((count, width), LOW),
            jax.ShapeDtypeStruct((1, width), FULL),
        ],
        scratch_shapes=[pltpu.VMEM((count, width), FULL)],
    )(memory, dkv, w)


def cross_back_kernel(x1_ref, dq_ref, dx2_ref, o_ref, wq_ref, wo_ref, p_ref, dx_ref, g1_ref, do_ref, inner_ref,
                      sum_q, sum_out, sum_gain, sum_shift):
    @pl.when(pl.program_id(0) == 0)
    def _():
        for ref in (sum_q, sum_out, sum_gain, sum_shift):
            ref[...] = jnp.zeros_like(ref)

    grad = dot(dq_ref[...], wq_ref[0], NT) * SCALE
    hat, rstd = normal(x1_ref[...])
    back, lines, shifts = normal_back(hat, rstd, grad, p_ref[GAIN + 1 : GAIN + 2])
    dx1 = dx2_ref[...] + back
    dx_ref[...] = dx1
    g1 = dx1.astype(LOW)
    g1_ref[...] = g1
    grad_mixed = dot(g1, wo_ref[0], NT).astype(LOW)
    do_ref[...] = grad_mixed
    inner_ref[...] = inner_parts(grad_mixed, o_ref[...], g1.shape[1] // HD)
    sum_q[...] += jnp.sum(dq_ref[...].astype(FULL), axis=0, keepdims=True) * SCALE
    sum_out[...] += jnp.sum(g1.astype(FULL), axis=0, keepdims=True)
    sum_gain[...] += lines
    sum_shift[...] += shifts


def cross_back(x1, dq, dx2, mixed, w, p, tile=256):
    rows, width = x1.shape
    part = pl.BlockSpec((tile, width), lambda i: (i, 0))
    low = jax.ShapeDtypeStruct((rows, width), LOW)
    line = jax.ShapeDtypeStruct((1, width), FULL)
    return calls(
        cross_back_kernel,
        "cross_back",
        4 * rows * width * width,
        16 * rows * width + 4 * width * width,
        grid=(rows // tile,),
        in_specs=[part, part, part, part, unit_of(w, 4), unit_of(w, 3), whole(p.shape)],
        out_specs=[part, part, part, pl.BlockSpec((tile, PAIR), lambda i: (i, 0))] + [whole((1, width))] * 4,
        out_shape=[jax.ShapeDtypeStruct((rows, width), FULL), low, low, jax.ShapeDtypeStruct((rows, PAIR), LOW), line, line, line, line],
    )(x1, dq, dx2, mixed, w, w, p)


def self_back_kernel(x_ref, dq_ref, dkv_ref, dx1_ref, w_ref, p_ref, dx_ref, sum_q, sum_v, sum_gain, sum_shift):
    @pl.when(pl.program_id(0) == 0)
    def _():
        for ref in (sum_q, sum_v, sum_gain, sum_shift):
            ref[...] = jnp.zeros_like(ref)

    dq = dq_ref[...]
    grad = dot(dq, w_ref[0], NT) * SCALE + dot(dkv_ref[0], w_ref[1], NT) + dot(dkv_ref[1], w_ref[2], NT)
    hat, rstd = normal(x_ref[...].astype(FULL))
    back, lines, shifts = normal_back(hat, rstd, grad, p_ref[GAIN : GAIN + 1])
    dx_ref[...] = (dx1_ref[...] + back).astype(LOW)
    sum_q[...] += jnp.sum(dq.astype(FULL), axis=0, keepdims=True) * SCALE
    sum_v[...] += jnp.sum(dkv_ref[1].astype(FULL), axis=0, keepdims=True)
    sum_gain[...] += lines
    sum_shift[...] += shifts


def self_back(x, dq, dkv, dx1, w, p, tile=256):
    rows, width = x.shape
    part = pl.BlockSpec((tile, width), lambda i: (i, 0))
    line = jax.ShapeDtypeStruct((1, width), FULL)
    return calls(
        self_back_kernel,
        "self_back",
        6 * rows * width * width,
        14 * rows * width + 6 * width * width,
        grid=(rows // tile,),
        in_specs=[part, part, pl.BlockSpec((2, tile, width), lambda i: (0, i, 0)), part, whole((3, width, width)), whole(p.shape)],
        out_specs=[part] + [whole((1, width))] * 4,
        out_shape=[jax.ShapeDtypeStruct((rows, width), LOW), line, line, line, line],
    )(x, dq, dkv, dx1, w, p)


AXES = ("dp", "fsdp")


def exchange(array):
    return lax.all_to_all(array, AXES, split_axis=0, concat_axis=0, tiled=True)


def leave(array, slots):
    return exchange(array.reshape(slots, -1, array.shape[-1]))


def after(value, *others):
    return lax.optimization_barrier((value, *others))[0]


def per_device(
    mesh,
    units,
    encoder,
    cotangent,
    deal,
    lengths,
    enc_counts,
    self_qkv,
    self_out,
    cross_qkv,
    cross_out,
    ffn_up,
    ffn_down,
    biases,
    ffn_bias_up,
    ffn_bias_down,
    norm_gain,
    norm_shift,
):
    slots = deal.shape[0]
    depth, ring = mesh.shape["dp"] // 2, mesh.shape["fsdp"]
    own, width = self_out.shape
    blocks = ffn_up.shape[1] // width
    place = lax.axis_index(AXES)
    length = lax.dynamic_slice_in_dim(lengths, place, 1)
    enc_count = lax.dynamic_slice_in_dim(enc_counts, place, 1)
    sent_x, sent_e, sent_c = deal_blocks(deal, [units, encoder, cotangent], False, "deal_in")

    up = ffn_up.reshape(own, slots, blocks, own).transpose(2, 0, 1, 3).reshape(blocks, own, width)
    late = jnp.concatenate([cross_out[None], up, ffn_down.reshape(blocks, own, width)])
    rows = jnp.concatenate([biases, norm_gain, norm_shift, ffn_bias_down[None]])
    flat = jnp.concatenate([rows.reshape(-1), ffn_bias_up])
    size = -(-flat.shape[0] // 2048) * 2048
    little = jnp.pad(flat, (0, size - flat.shape[0])).reshape(1, size // 128, 128)
    w_one, little, x, memory = first_gather(mesh, [self_qkv, self_out, cross_qkv], little, [sent_x, sent_e], 0)
    w_one = w_one.reshape(-1, width, width)
    x, memory = x.reshape(-1, width), memory.reshape(-1, width)
    flat = little.reshape(slots, size).astype(FULL)
    p = flat[:, : rows.size].reshape((slots,) + rows.shape)
    p = jnp.moveaxis(p, 0, 1).reshape(rows.shape[0], -1)
    p = jnp.pad(p, ((0, 16 - rows.shape[0]), (0, 0)))
    bias_up = flat[:, rows.size : rows.size + ffn_bias_up.size].reshape(slots, blocks, own)
    bias_up = bias_up.transpose(1, 0, 2).reshape(1, -1)

    w_two, cot, a0, qkv, mixed0, level0, x1, a1, q1, kv1, mixed1, level1 = forward(
        mesh, length, enc_count, x, memory, w_one, p, late, sent_c, 1
    )
    cot = cot.reshape(-1, width)
    w_two = w_two.reshape(late.shape[0], width, width)
    (result, r, du, a2, g3, dx2, g2, grad_mixed1, inner1, bias_up_grad, bias_down_grad, bias_five, gain_two, shift_two) = feed(
        length, x1, mixed1, cot, w_two, p, bias_up
    )
    result = leave(result, slots)
    dq1, dkv1 = cross_attend_back(enc_count, q1, kv1, grad_mixed1, level1, inner1)
    dx1, g1, grad_mixed0, inner0, bias_three, bias_two, gain_one, shift_one = cross_back(x1, dq1, dx2, mixed0, w_one, p)
    made, grad_memory, bias_four = memory_grad(memory, dkv1, w_one)
    grad_memory = after(grad_memory, result).reshape(slots, -1, width)
    sums_one, dq0, dkv0, grad_memory = feed_scatter(
        mesh, length, a2, g3, du, r, qkv, grad_mixed0, level0, inner0, grad_memory, 2
    )
    up_sum = sums_one[:blocks].reshape(blocks, own, slots, own).transpose(1, 2, 0, 3).reshape(own, -1)
    down_sum = sums_one[blocks:].reshape(blocks * own, width)
    dx, bias_zero, bias_one, gain_zero, shift_zero = self_back(x, dq0, dkv0, dx1, w_one, p)

    bias_up_grad = bias_up_grad.reshape(blocks, slots, own).transpose(1, 0, 2).reshape(slots, -1)

    def by_owner(*lines):
        return jnp.concatenate(lines).reshape(len(lines), slots, own).transpose(1, 0, 2).reshape(slots, -1)

    terms = jnp.concatenate(
        [
            by_owner(
                bias_zero, bias_one, bias_two, bias_three, bias_four, bias_five, bias_down_grad,
                gain_zero, gain_one, gain_two, shift_zero, shift_one, shift_two,
            ),
            bias_up_grad,
        ],
        axis=1,
    )
    tiny = -(-terms.shape[1] // 1024) * 8
    terms = jnp.pad(terms, ((0, 0), (0, tiny * 128 - terms.shape[1]))).reshape(depth, 2, ring * tiny, 128)
    part = ring * own
    pairs = (mixed1, g2, a1, dq1, mixed0, g1, a0, dq0, dkv0)
    terms = after(terms, up_sum, down_sum)
    self_qkv_sum, self_out_sum, cross_qkv_sum, cross_out_sum, tiny_sums, dx = last_scatter(
        mesh, made.reshape(2, depth, 2, part, width), pairs, terms, dx.reshape(slots, -1, width), 3
    )
    result, dx, grad_memory = deal_blocks(deal, [result, dx, grad_memory], True, "deal_out")
    flat = tiny_sums.reshape(-1)
    lines = flat[: 13 * own].reshape(13, own)
    return (
        result,
        dx,
        grad_memory,
        self_qkv_sum,
        self_out_sum,
        cross_qkv_sum,
        cross_out_sum,
        up_sum,
        down_sum,
        lines[:6],
        flat[13 * own : 13 * own + ffn_bias_up.size],
        lines[6],
        lines[7:10],
        lines[10:13],
    )


def solution(mesh):
    middle_rows = P(None, AXES, None)
    first_rows = P(AXES, None)
    last = P(None, AXES)
    weights = (middle_rows, first_rows, middle_rows, first_rows, first_rows, first_rows, last, P(AXES), P(AXES), last, last)
    return jax.shard_map(
        functools.partial(per_device, mesh),
        mesh=mesh,
        in_specs=(middle_rows,) * 3 + (P(),) * 3 + weights,
        out_specs=(middle_rows,) * 3 + weights,
        check_vma=False,
    )
```

```python
import functools

import jax
import jax.numpy as jnp
from jax import lax
from jax.experimental import pallas as pl
from jax.experimental.pallas import tpu as pltpu
from jax.sharding import PartitionSpec as P

HD = 64
EPSILON = 1e-05
SCALE = 0.125
NEGATIVE = -1e30
MESH = pl.DeviceIdType.MESH
ANY = pl.BlockSpec(memory_space=pl.ANY)
DMA = pltpu.SemaphoreType.DMA


def ring_place(f, ring):
    half = ring // 2
    upper, rest = f // half, f % half
    return upper * half + rest + upper * (half - 1 - 2 * rest)


class Place:
    def __init__(self, depth, ring):
        self.depth, self.ring, self.half = depth, ring, ring // 2
        d, f = lax.axis_index("dp"), lax.axis_index("fsdp")
        self.z, self.c, self.f = d // 2, d % 2, f
        self.at = ring_place(f, ring)
        self.right = ring_place((self.at + 1) % ring, ring)
        self.left = ring_place((self.at + ring - 1) % ring, ring)

    def greet(self):
        barrier = pltpu.get_barrier_semaphore()

        def hail(d, g):
            pl.semaphore_signal(barrier, inc=1, device_id=(d, g), device_id_type=MESH)

        for s in range(1, self.depth):
            hail((self.z + s) % self.depth * 2 + self.c, self.f)
        hail(self.z * 2 + self.c, self.right)
        hail(self.z * 2 + self.c, self.left)
        hail(self.z * 2 + 1 - self.c, self.f)
        pl.semaphore_wait(barrier, self.depth + 2)

    def index(self):
        return (self.z * 2 + self.c) * self.ring + self.f

    def peers(self):
        return 2 * self.depth * self.ring

    def peer(self, k, sign):
        dz, dc, df = k % self.depth, k // self.depth % 2, k // self.depth // 2
        z = (self.z + sign * dz + self.depth) % self.depth
        f = (self.f + sign * df + self.ring) % self.ring
        return z * 2 + (self.c + dc) % 2, f

    def greet_all(self):
        barrier = pltpu.get_barrier_semaphore()

        def hail(k):
            pl.semaphore_signal(barrier, inc=1, device_id=self.peer(k + 1, 1), device_id_type=MESH)

        loop(self.peers() - 1, hail)
        pl.semaphore_wait(barrier, self.peers() - 1)

    def to_z(self, src, dst, send, recv, s):
        return self.remote(src, dst, send, recv, (self.z + s) % self.depth * 2 + self.c, self.f)

    def to_side(self, src, dst, send, recv, way):
        return self.remote(src, dst, send, recv, self.z * 2 + self.c, (self.right, self.left)[way])

    def to_core(self, src, dst, send, recv):
        return self.remote(src, dst, send, recv, self.z * 2 + 1 - self.c, self.f)

    @staticmethod
    def remote(src, dst, send, recv, d, g):
        return pltpu.make_async_remote_copy(
            src_ref=src, dst_ref=dst, send_sem=send, recv_sem=recv,
            device_id=(d, g), device_id_type=MESH,
        )


def when(flag, run):
    if isinstance(flag, bool):
        if flag:
            run()
    else:
        pl.when(flag)(run)


def both(one, two):
    if isinstance(one, bool) and isinstance(two, bool):
        return one and two
    return jnp.logical_and(one, two)


def loop(count, run):
    def body(i, carry):
        run(i)
        return carry

    lax.fori_loop(0, count, body, 0)


class Gather:
    def __init__(self, place, count, shards, fulls, sems, ahead=2):
        self.place, self.count, self.shards, self.fulls = place, count, shards, fulls
        self.local, self.z_send, self.z_recv, self.r_send, self.r_recv, self.c_send, self.c_recv = sems
        self.ahead = min(ahead, count)

    @staticmethod
    def sems(mesh, n):
        depth, ring = mesh.shape["dp"] // 2, mesh.shape["fsdp"]
        half = ring // 2
        return [DMA((n,)), DMA((n, depth)), DMA((n, depth)), DMA((n, half, 2)), DMA((n, half, 2)), DMA((n, ring)), DMA((n, ring))]

    def chunk(self, u, zs, c, g):
        return self.fulls.at[u, zs, c, g]

    def shard(self, u):
        if callable(self.shards):
            return self.shards(u if isinstance(u, int) else 0)
        return self.shards.at[u]

    def kept(self, u):
        p = self.place
        return pltpu.make_async_copy(self.shard(u), self.chunk(u, p.z, p.c, p.f), self.local.at[u])

    def z_copy(self, u, s, incoming):
        p = self.place
        origin = (p.z + p.depth - s) % p.depth if incoming else p.z
        return p.to_z(self.shard(u), self.chunk(u, origin, p.c, p.f), self.z_send.at[u, s], self.z_recv.at[u, s], s)

    def ring_copy(self, u, t, way, incoming):
        p = self.place
        back = t - 1 + incoming
        origin = (p.at + p.ring - back) % p.ring if way == 0 else (p.at + back) % p.ring
        cut = p.depth // 2
        zs = slice(0, p.depth) if t < p.half else (slice(0, cut), slice(cut, p.depth))[way]
        piece = self.chunk(u, zs, p.c, ring_place(origin, p.ring))
        return p.to_side(piece, piece, self.r_send.at[u, t - 1, way], self.r_recv.at[u, t - 1, way], way)

    def core_copy(self, u, shift, incoming):
        p = self.place
        c = 1 - p.c if incoming else p.c
        piece = self.chunk(u, slice(0, p.depth), c, ring_place((p.at + shift) % p.ring, p.ring))
        return p.to_core(piece, piece, self.c_send.at[u, shift], self.c_recv.at[u, shift])

    def start_z(self, u):
        self.kept(u).start()
        for s in range(1, self.place.depth):
            self.z_copy(u, s, False).start()

    def start_ring(self, u, t):
        for way in range(2):
            self.ring_copy(u, t, way, 0).start()

    def start_core(self, u, t):
        half, ring = self.place.half, self.place.ring
        for shift in [0] if t == 0 else [t] if t == half else [ring - t, t]:
            self.core_copy(u, shift, False).start()

    def begin(self):
        for u in range(self.ahead):
            self.start_z(u)

    def steps(self):
        return self.count + self.place.half

    def step(self, i):
        place = self.place

        def first():
            self.kept(i).wait()
            for s in range(1, place.depth):
                self.z_copy(i, s, True).wait_recv()
            self.start_ring(i, 1)
            self.start_core(i, 0)

        def later(u, t):
            for way in range(2):
                self.ring_copy(u, t, way, 1).wait_recv()
            if t < place.half:
                self.start_ring(u, t + 1)
            self.start_core(u, t)

        when(i + self.ahead < self.count, lambda: self.start_z(i + self.ahead))
        when(i < self.count, first)
        for t in range(1, place.half + 1):
            u = i - t
            when(both(0 <= u, u < self.count), functools.partial(later, u, t))

    def finish(self):
        place = self.place

        def one(u):
            for s in range(1, place.depth):
                self.z_copy(u, s, False).wait_send()
            for t in range(1, place.half + 1):
                for way in range(2):
                    self.ring_copy(u, t, way, 0).wait_send()
            for shift in range(place.ring):
                self.core_copy(u, shift, False).wait_send()
                self.core_copy(u, shift, True).wait_recv()

        loop(self.count, one)


class Exchange:
    def __init__(self, place, arrays, steps, sems):
        self.place, self.arrays = place, arrays
        self.send, self.recv, self.local = sems
        self.each = -(-(place.peers() - 1) // steps)

    @staticmethod
    def sems(mesh, n):
        peers = 2 * (mesh.shape["dp"] // 2) * mesh.shape["fsdp"]
        return [DMA((n, peers)), DMA((n, peers)), DMA((n,))]

    def block(self, d, f):
        return d * self.place.ring + f

    def own(self, a):
        p = self.place
        src, dst = self.arrays[a]
        me = self.block(p.z * 2 + p.c, p.f)
        return pltpu.make_async_copy(src.at[me], dst.at[me], self.local.at[a])

    def copy(self, a, k, incoming):
        p = self.place
        src, dst = self.arrays[a]
        d, f = p.peer(k, 1)
        at, g = p.peer(k, -1) if incoming else (p.z * 2 + p.c, p.f)
        return p.remote(src.at[self.block(d, f)], dst.at[self.block(at, g)], self.send.at[a, k], self.recv.at[a, k], d, f)

    def begin(self):
        for a in range(len(self.arrays)):
            self.own(a).start()

    def start(self, k):
        for a in range(len(self.arrays)):
            self.copy(a, k, False).start()

    def step(self, i):
        for j in range(self.each):
            k = 1 + i * self.each + j
            when(k < self.place.peers(), functools.partial(self.start, k))

    def finish(self):
        def one(k):
            for a in range(len(self.arrays)):
                self.copy(a, k + 1, False).wait_send()
                self.copy(a, k + 1, True).wait_recv()

        loop(self.place.peers() - 1, one)
        for a in range(len(self.arrays)):
            self.own(a).wait()


class Scatter:
    def __init__(self, place, count, rows, held, put, refs, sems):
        self.place, self.count, self.rows, self.held, self.put = place, count, rows, held, put
        self.mine, self.theirs, self.rhalf, self.rfull, self.zbuf = refs
        self.c_send, self.c_recv, self.r_send, self.r_recv, self.z_send, self.z_recv = sems
        self.slots = held.shape[0]

    @staticmethod
    def refs(mesh, n, rows, cols, low):
        depth, ring = mesh.shape["dp"] // 2, mesh.shape["fsdp"]
        half, cut = ring // 2, depth // 2
        return [
            pltpu.VMEM((n, depth, ring, rows, cols), low),
            pltpu.VMEM((n, depth, ring * rows, cols), low),
            pltpu.VMEM((n, 2, cut, rows, cols), low),
            pltpu.VMEM((n, half - 1, 2, depth, rows, cols), low),
            pltpu.VMEM((n, depth - 1, rows, cols), low),
        ]

    @staticmethod
    def sems(mesh, n):
        depth, ring = mesh.shape["dp"] // 2, mesh.shape["fsdp"]
        half = ring // 2
        return [DMA((n,)), DMA((n,)), DMA((n, half, 2)), DMA((n, half, 2)), DMA((n, depth)), DMA((n, depth))]

    def core(self, u):
        p = self.place
        return p.to_core(self.held.at[u % self.slots, slice(0, p.depth), 1 - p.c], self.theirs.at[u], self.c_send.at[u], self.c_recv.at[u])

    def dest(self, t, way):
        p = self.place
        ahead = p.half - t + 1
        return ring_place((p.at + ahead) % p.ring if way == 0 else (p.at + p.ring - ahead) % p.ring, p.ring)

    def ring_copy(self, u, t, way):
        p = self.place
        g, cut = self.dest(t, way), p.depth // 2
        if t == 1:
            src = self.mine.at[u, slice(0, cut) if way == 0 else slice(cut, p.depth), g]
            dst = self.rhalf.at[u, way]
        else:
            src = self.mine.at[u, slice(0, p.depth), g]
            dst = self.rfull.at[u, t - 2, way]
        return p.to_side(src, dst, self.r_send.at[u, t - 1, way], self.r_recv.at[u, t - 1, way], way)

    def z_copy(self, u, s):
        p = self.place
        to = (p.z + s) % p.depth
        return p.to_z(self.mine.at[u, to, p.f], self.zbuf.at[u, s - 1], self.z_send.at[u, s], self.z_recv.at[u, s], s)

    def first_sum(self, u):
        p, full = self.place, jnp.float32
        self.core(u).wait_recv()

        def one(a):
            total = self.held[u % self.slots, a, p.c].astype(full) + self.theirs[u, a].astype(full)
            for g in range(p.ring):
                self.mine[u, a, g] = total[g * self.rows : (g + 1) * self.rows].astype(self.mine.dtype)

        loop(p.depth, one)
        for way in range(2):
            self.ring_copy(u, 1, way).start()

    def next_sum(self, u, t):
        p, full, mine = self.place, jnp.float32, self.mine
        for way in range(2):
            self.ring_copy(u, t, way).wait_recv()
        cut = p.depth // 2
        if t < p.half:
            for way in range(2):
                g = self.dest(t + 1, way)
                low = cut * way if t == 1 else 0
                src = self.rhalf.at[u, way] if t == 1 else self.rfull.at[u, t - 2, way]

                def one(a, g=g, low=low, src=src):
                    mine[u, low + a, g] = (mine[u, low + a, g].astype(full) + src[a].astype(full)).astype(mine.dtype)

                loop(cut if t == 1 else p.depth, one)
                self.ring_copy(u, t + 1, way).start()
        else:
            left, right = self.rfull.at[u, t - 2, 0], self.rfull.at[u, t - 2, 1]

            def one(a):
                mine[u, a, p.f] = (
                    mine[u, a, p.f].astype(full) + left[a].astype(full) + right[a].astype(full)
                ).astype(mine.dtype)

            loop(p.depth, one)
            for s in range(1, p.depth):
                self.z_copy(u, s).start()

    def last_sum(self, u):
        p, full = self.place, jnp.float32
        for s in range(1, p.depth):
            self.z_copy(u, s).wait_recv()
        total = self.mine[u, p.z, p.f].astype(full)
        for s in range(1, p.depth):
            total = total + self.zbuf[u, s - 1].astype(full)
        self.put(u, total)

    def finish(self):
        p = self.place

        def one(u):
            for t in range(1, p.half + 1):
                for way in range(2):
                    self.ring_copy(u, t, way).wait_send()
            for s in range(1, p.depth):
                self.z_copy(u, s).wait_send()

        loop(self.count, one)
        for u in range(max(0, self.count - self.slots), self.count):
            self.core(u).wait_send()

    def last_sums(self):
        for u in range(self.count):
            self.last_sum(u)

    def steps(self):
        return self.count + self.place.half // 2

    def early(self, i):
        for t in range(1, self.place.half + 1, 2):
            u = i - (t + 1) // 2
            when(both(0 <= u, u < self.count), functools.partial(self.next_sum, u, t))

    def late(self, i):
        when(i < self.count, lambda: self.first_sum(i))
        for t in range(2, self.place.half + 1, 2):
            u = i - t // 2
            when(both(0 <= u, u < self.count), functools.partial(self.next_sum, u, t))


def remote_params(ident):
    return pltpu.CompilerParams(collective_id=ident, has_side_effects=True, vmem_limit_bytes=60 * 2**20)


def first_gather_kernel(depth, ring, where, n_w, n_x, *refs):
    weights, little, sent = refs[:n_w], refs[n_w], refs[n_w + 1 : n_w + 1 + n_x]
    full, little_full, arrived = refs[n_w + 1 + n_x], refs[n_w + 2 + n_x], refs[n_w + 3 + n_x : n_w + 3 + 2 * n_x]
    sems = refs[n_w + 3 + 2 * n_x :]
    place = Place(depth, ring)
    place.greet_all()
    count = len(where)

    def shard(u):
        which, lead = where[u]
        return weights[which] if lead is None else weights[which].at[lead]

    small = Gather(place, 1, little, little_full, sems[:7])
    big = Gather(place, count, shard, full, sems[7:14], ahead=count)
    swap = Exchange(place, tuple(zip(sent, arrived, strict=True)), max(1, big.steps() - 3), sems[14:])
    small.begin()
    big.begin()
    swap.begin()
    for i in range(big.steps()):
        swap.step(i)
        if i < small.steps():
            small.step(i)
        big.step(i)
    small.finish()
    big.finish()
    swap.finish()


def first_gather(mesh, weights, little, sent, ident):
    depth, ring = mesh.shape["dp"] // 2, mesh.shape["fsdp"]
    where = []
    for which, a in enumerate(weights):
        where += [(which, None)] if a.ndim == 2 else [(which, lead) for lead in range(a.shape[0])]
    count = len(where)

    def full(n, a):
        return jax.ShapeDtypeStruct((n, depth, 2, ring) + a.shape[-2:], a.dtype)

    same = [jax.ShapeDtypeStruct(a.shape, a.dtype) for a in sent]
    return pl.pallas_call(
        functools.partial(first_gather_kernel, depth, ring, tuple(where), len(weights), len(sent)),
        out_shape=[full(count, weights[0]), full(1, little)] + same,
        in_specs=[pl.BlockSpec(memory_space=pltpu.VMEM)] * (len(weights) + 1) + [ANY] * len(sent),
        out_specs=[ANY] * (2 + len(sent)),
        scratch_shapes=Gather.sems(mesh, 1) + Gather.sems(mesh, count) + Exchange.sems(mesh, len(sent)),
        compiler_params=remote_params(ident),
        cost_estimate=pl.CostEstimate(flops=60_000_000_000, bytes_accessed=2 * 33_554_432, transcendentals=0),
        name="first_gather",
    )(*weights, little, *sent)


def deal_kernel(out_of, n, deal_ref, *refs):
    sources, dests, held, sem = refs[:n], refs[n : 2 * n], refs[2 * n : 3 * n], refs[3 * n]
    slots = deal_ref.shape[0]

    def load(a, i):
        return pltpu.make_async_copy(sources[a].at[i if out_of else deal_ref[i]], held[a].at[i], sem.at[0, a, i])

    def store(a, i):
        return pltpu.make_async_copy(held[a].at[i], dests[a].at[deal_ref[i] if out_of else i], sem.at[1, a, i])

    def begin(i):
        for a in range(n):
            load(a, i).start()

    def turn(i):
        for a in range(n):
            load(a, i).wait()
            store(a, i).start()

    def end(i):
        for a in range(n):
            store(a, i).wait()

    loop(slots, begin)
    loop(slots, turn)
    loop(slots, end)


def deal_blocks(deal, arrays, out_of, name):
    n = len(arrays)
    return pl.pallas_call(
        functools.partial(deal_kernel, out_of, n),
        out_shape=[jax.ShapeDtypeStruct(a.shape, a.dtype) for a in arrays],
        in_specs=[pl.BlockSpec(memory_space=pltpu.SMEM)] + [ANY] * n,
        out_specs=[ANY] * n,
        scratch_shapes=[pltpu.VMEM(a.shape, a.dtype) for a in arrays] + [DMA((2, n, deal.shape[0]))],
        compiler_params=pltpu.CompilerParams(vmem_limit_bytes=60 * 2**20),
        name=name,
    )(deal, *arrays)


NN = (((1,), (0,)), ((), ()))
NT = (((1,), (1,)), ((), ()))
TN = (((0,), (0,)), ((), ()))
LOW = jnp.bfloat16
FULL = jnp.float32
SMEM = pl.BlockSpec(memory_space=pltpu.SMEM)
VMEM = pl.BlockSpec(memory_space=pltpu.VMEM)
PAIR = 2 * HD
ROOM = 60 * 2**20


def dot(left, right, how):
    return lax.dot_general(left, right, how, preferred_element_type=FULL)


def calls(kernel, name, flops, moved, **kw):
    return pl.pallas_call(
        kernel,
        name=name,
        compiler_params=pltpu.CompilerParams(vmem_limit_bytes=ROOM),
        cost_estimate=pl.CostEstimate(flops=int(flops), bytes_accessed=int(moved), transcendentals=0),
        **kw,
    )


def whole(shape):
    return pl.BlockSpec(shape, lambda *_: (0,) * len(shape))


def normal(x):
    mean = jnp.mean(x, axis=-1, keepdims=True)
    centred = x - mean
    rstd = lax.rsqrt(jnp.mean(centred * centred, axis=-1, keepdims=True) + EPSILON)
    return centred * rstd, rstd


def normal_back(hat, rstd, grad, gain):
    scaled = grad * gain
    lean = jnp.mean(scaled, axis=-1, keepdims=True)
    tilt = jnp.mean(scaled * hat, axis=-1, keepdims=True)
    back = rstd * (scaled - lean - hat * tilt)
    return back, jnp.sum(grad * hat, axis=0, keepdims=True), jnp.sum(grad, axis=0, keepdims=True)


GAIN, SHIFT, DOWN = 6, 9, 12


def lanes(shape):
    return lax.broadcasted_iota(jnp.int32, shape, len(shape) - 1)


def rows_of(shape):
    return lax.broadcasted_iota(jnp.int32, shape, 0)


def head_mask(head):
    return jnp.where(lanes((1, PAIR)) // HD == head, 1.0, 0.0).astype(LOW)


def thirds(x):
    one = x.astype(LOW).astype(FULL)
    two = (x - one).astype(LOW).astype(FULL)
    return one, two, x - one - two


def wide_keys(k, v, n):
    count = k.shape[0]
    shut = jnp.where((lanes((count, PAIR)) == 0) & (rows_of((count, PAIR)) >= n), NEGATIVE, 0.0).astype(LOW)
    ones = jnp.ones((count, PAIR), LOW)
    return [
        (jnp.concatenate([k * head_mask(h), shut], axis=1), jnp.concatenate([v * head_mask(h), ones], axis=1))
        for h in range(2)
    ]


def attend_pair(causal, tile, h, n, q, k, v, store, l_ref):
    queries, count = q.shape[0], k.shape[0]
    first = jnp.where(lanes((queries, PAIR)) == 0, 1.0, 0.0).astype(LOW)
    wide_q = jnp.concatenate([q, first], axis=1)
    spots = lanes((tile, PAIR))
    heads = wide_keys(k, v, n)
    for i in range(queries // tile):
        at = slice(i * tile, (i + 1) * tile)
        seen = (i + 1) * tile if causal else count
        mixed = jnp.zeros((tile, PAIR), FULL)
        kept = l_ref[at]
        for head, (keys, values) in enumerate(heads):
            scores = dot(wide_q[at], keys[:seen], NT)
            if causal:
                square = (tile, tile)
                last = jnp.where(lanes(square) <= rows_of(square), scores[:, seen - tile :], NEGATIVE)
                scores = last if seen == tile else jnp.concatenate([scores[:, : seen - tile], last], axis=1)
            top = jnp.max(scores, axis=1, keepdims=True)
            weights = jnp.exp(scores - top).astype(LOW)
            sums = dot(weights, values[:seen], NN)
            total = sums[:, PAIR:]
            mixed = mixed + sums[:, :PAIR] / total
            kept = jnp.where(spots == 2 * h + head, top + jnp.log(total), kept)
        store(at, mixed.astype(LOW))
        l_ref[at] = kept


def parts_of(value, heads, spare):
    lane = lanes(value.shape)
    shown = jnp.where(lane < heads, value, 0.0)
    shown = shown + pltpu.roll(shown, heads, 1) + pltpu.roll(shown, 2 * heads, 1)
    one, two, three = thirds(-shown)
    part = jnp.where(lane < heads, one, jnp.where(lane < 2 * heads, two, three))
    return jnp.where(lane == 3 * heads, spare, part).astype(LOW)


def take_part(head, heads):
    lane = lanes((1, PAIR))
    return jnp.where((lane < 3 * heads) & (lane % heads == head), 1.0, 0.0)


def forward_kernel(
    depth, ring, count, n_ref, m_ref, x_hbm, e_hbm, w_hbm, p_ref, shard, sent,
    full, arrived, a0_hbm, qkv_hbm, o0_hbm, l0_hbm, x1_hbm, a1_hbm, q1_hbm, kv_hbm, o1_hbm, l1_hbm,
    x_ref, e_ref, w_ref, a_ref, qkv_ref, o_ref, l0_ref, x1_ref, q1_ref, kv_ref, l1_ref, a1_ref, lp_ref,
    w_sem, in_sem, out_sem, *sems,
):
    place = Place(depth, ring)
    place.greet_all()
    me = place.index()
    gather = Gather(place, count, shard, full, sems[:7], ahead=count)
    swap = Exchange(place, ((sent, arrived),), gather.steps() - 2, sems[7:])
    gather.begin()
    swap.begin()

    def advance(i):
        swap.step(i)
        gather.step(i)

    rows, width = x_ref.shape
    tile = 256
    load_x = pltpu.make_async_copy(x_hbm, x_ref, in_sem.at[0])
    load_e = pltpu.make_async_copy(e_hbm, e_ref, in_sem.at[1])
    load_x.start()
    parts = w_ref.shape[0]
    loads = [pltpu.make_async_copy(w_hbm.at[u], w_ref.at[u], w_sem.at[u]) for u in range(parts)]
    for load in loads[:3]:
        load.start()
    load_e.start()
    for load in loads[3:]:
        load.start()
    leaving = []

    def send(src, dst):
        copy = pltpu.make_async_copy(src, dst, out_sem.at[len(leaving)])
        copy.start()
        leaving.append(copy)

    l0_ref[...] = jnp.zeros_like(l0_ref)
    l1_ref[...] = jnp.zeros_like(l1_ref)
    load_x.wait()
    advance(0)
    for i in range(rows // tile):
        at = slice(i * tile, (i + 1) * tile)
        hat, _ = normal(x_ref[at].astype(FULL))
        a_ref[at] = (hat * p_ref[GAIN : GAIN + 1] + p_ref[SHIFT : SHIFT + 1]).astype(LOW)
    send(a_ref, a0_hbm)
    for j in range(3):
        loads[j].wait()
        bias = (p_ref[0:1], None, p_ref[1:2])[j]

        def project(i, j=j, bias=bias):
            at = pl.ds(pl.multiple_of(i * 2 * tile, 2 * tile), 2 * tile)
            y = dot(a_ref[at], w_ref[j], NN)
            if bias is not None:
                y = y + bias
            qkv_ref[j, at] = (y * SCALE if j == 0 else y).astype(LOW)

        loop(rows // (2 * tile), project)
        send(qkv_ref.at[j], qkv_hbm.at[j])
        if j == 1:
            advance(1)

    pairs = width // PAIR

    def self_pair(h):
        cols = pl.ds(pl.multiple_of(h * PAIR, PAIR), PAIR)

        def store(at, value):
            o_ref[at, cols] = value

        attend_pair(True, tile, h, n_ref[me], qkv_ref[0, :, cols], qkv_ref[1, :, cols], qkv_ref[2, :, cols], store, l0_ref)
        when(h % 2 == 0, lambda: advance(2 + h // 2))

    loop(pairs, self_pair)
    send(o_ref, o0_hbm)
    heads = 2 * pairs
    lp_ref[0] = parts_of(l0_ref[...], heads, 1.0)
    send(lp_ref.at[0], l0_hbm)
    done = 2 + (pairs + 1) // 2
    loads[3].wait()
    loads[4].wait()

    def middle_part(i):
        at = pl.ds(pl.multiple_of(i * tile, tile), tile)
        x1 = x_ref[at].astype(FULL) + (dot(o_ref[at], w_ref[3], NN) + p_ref[2:3])
        x1_ref[at] = x1
        hat, _ = normal(x1)
        a = (hat * p_ref[GAIN + 1 : GAIN + 2] + p_ref[SHIFT + 1 : SHIFT + 2]).astype(LOW)
        a1_ref[at] = a
        q1_ref[at] = ((dot(a, w_ref[4], NN) + p_ref[3:4]) * SCALE).astype(LOW)
        when(i % 2 == 1, lambda: advance(done + i // 2))

    loop(rows // tile, middle_part)
    done = done + rows // tile // 2
    send(x1_ref, x1_hbm)
    send(a1_ref, a1_hbm)
    send(q1_ref, q1_hbm.at[0])
    load_e.wait()
    for j in range(2):
        loads[5 + j].wait()
        y = dot(e_ref[...], w_ref[5 + j], NN)
        kv_ref[j] = (y + p_ref[4:5] if j == 1 else y).astype(LOW)
    send(kv_ref, kv_hbm)
    leaving[4].wait()

    def cross_pair(h):
        cols = pl.ds(pl.multiple_of(h * PAIR, PAIR), PAIR)

        def store(at, value):
            o_ref[at, cols] = value

        attend_pair(False, tile, h, m_ref[me], q1_ref[:, cols], kv_ref[0, :, cols], kv_ref[1, :, cols], store, l1_ref)
        when(h % 2 == 0, lambda: advance(done + h // 2))

    loop(pairs, cross_pair)
    done = done + (pairs + 1) // 2
    send(o_ref, o1_hbm)
    lp_ref[1] = parts_of(l1_ref[...], heads, 1.0)
    send(lp_ref.at[1], l1_hbm)
    for i in range(done, gather.steps()):
        advance(i)
    gather.finish()
    swap.finish()
    for k, copy in enumerate(leaving):
        if k != 4:
            copy.wait()


def forward(mesh, length, enc_count, x, memory, w, p, shards, sent, ident):
    depth, ring = mesh.shape["dp"] // 2, mesh.shape["fsdp"]
    count = shards.shape[0]
    rows, width = x.shape
    enc = memory.shape[0]
    low = jax.ShapeDtypeStruct((rows, width), LOW)
    level = jax.ShapeDtypeStruct((rows, PAIR), LOW)
    out_shape = [
        jax.ShapeDtypeStruct((count, depth, 2, ring) + shards.shape[1:], LOW),
        jax.ShapeDtypeStruct(sent.shape, sent.dtype),
        low,
        jax.ShapeDtypeStruct((3, rows, width), LOW),
        low,
        level,
        jax.ShapeDtypeStruct((rows, width), FULL),
        low,
        jax.ShapeDtypeStruct((1, rows, width), LOW),
        jax.ShapeDtypeStruct((2, enc, width), LOW),
        low,
        level,
    ]
    big = pltpu.VMEM((rows, width), LOW)
    return pl.pallas_call(
        functools.partial(forward_kernel, depth, ring, count),
        out_shape=out_shape,
        in_specs=[SMEM, SMEM, ANY, ANY, ANY, VMEM, VMEM, ANY],
        out_specs=[ANY] * len(out_shape),
        scratch_shapes=[
            big,
            pltpu.VMEM((enc, width), LOW),
            pltpu.VMEM(w.shape, LOW),
            big,
            pltpu.VMEM((3, rows, width), LOW),
            big,
            pltpu.VMEM((rows, PAIR), FULL),
            pltpu.VMEM((rows, width), FULL),
            big,
            pltpu.VMEM((2, enc, width), LOW),
            pltpu.VMEM((rows, PAIR), FULL),
            big,
            pltpu.VMEM((2, rows, PAIR), LOW),
            DMA((w.shape[0],)),
            DMA((2,)),
            DMA((12,)),
        ]
        + Gather.sems(mesh, count)
        + Exchange.sems(mesh, 1),
        compiler_params=remote_params(ident),
        cost_estimate=pl.CostEstimate(flops=70_000_000_000, bytes_accessed=2 * 33_554_432, transcendentals=0),
        name="forward_gather",
    )(length, enc_count, x, memory, w, p, shards, sent)


def back_pair(causal, tile, h, heads, n, q, k, v, grad, level, inner, acc_ref, store):
    queries, count = q.shape[0], k.shape[0]
    acc_ref[...] = jnp.zeros_like(acc_ref)
    wide_q = jnp.concatenate([q, level], axis=1)
    wide_g = jnp.concatenate([grad, inner], axis=1)
    shut = jnp.where(rows_of((count, PAIR)) >= n, NEGATIVE, 0.0)
    both_heads = []
    for head in range(2):
        mask = head_mask(head)
        mine = take_part(2 * h + head, heads)
        open_k = jnp.where(lanes((count, PAIR)) == 3 * heads, shut, mine).astype(LOW)
        open_v = jnp.broadcast_to(mine, (count, PAIR)).astype(LOW)
        wide_k = jnp.concatenate([k * mask, open_k], axis=1)
        wide_v = jnp.concatenate([v * mask, open_v], axis=1)
        both_heads.append((wide_k, wide_v, q * mask, grad * mask, k * mask))
    for i in range(count // tile):
        at = slice(i * tile, (i + 1) * tile)
        low = i * tile if causal else 0
        grad_k = jnp.zeros((tile, PAIR), FULL)
        grad_v = jnp.zeros((tile, PAIR), FULL)
        for wide_k, wide_v, q_one, g_one, k_one in both_heads:
            scores = dot(wide_k[at], wide_q[low:], NT)
            if causal:
                square = (tile, tile)
                near = jnp.where(rows_of(square) <= lanes(square), scores[:, :tile], NEGATIVE)
                scores = near if low + tile == queries else jnp.concatenate([near, scores[:, tile:]], axis=1)
            probs = jnp.exp(scores)
            slope = (probs * dot(wide_v[at], wide_g[low:], NT)).astype(LOW)
            grad_v = grad_v + dot(probs.astype(LOW), g_one[low:], NN)
            grad_k = grad_k + dot(slope, q_one[low:], NN)
            acc_ref[low:] += dot(slope, k_one[at], TN)
        store(at, grad_k.astype(LOW), grad_v.astype(LOW))


def inner_parts(grad, mixed, heads):
    width = grad.shape[1]
    product = grad.astype(FULL) * mixed.astype(FULL)
    head = (rows_of((width, PAIR)) // HD == lanes((width, PAIR))).astype(FULL).astype(LOW)
    high = product.astype(LOW)
    rest = product - high.astype(FULL)
    return parts_of(dot(high, head, NN) + dot(rest.astype(LOW), head, NN), heads, 0.0)


def unit_grad(place, held, slot, a_ref, b_ref, scale):
    depth, part = held.shape[1], held.shape[3]
    width = a_ref.shape[1]
    piece = width // 2
    for m in range(2):
        value = dot(a_ref[:, m * piece : (m + 1) * piece], b_ref[...], TN)
        if scale is not None:
            value = value * scale
        value = value.astype(LOW)
        for k in range(piece // part):
            at = m * (piece // part) + k
            held[slot, at // 2, at % 2] = value[k * part : (k + 1) * part]


def back_scatter_kernel(
    depth, ring, n_ref, m_ref, a2_hbm, g3_hbm, du_hbm, r_hbm, qkv_hbm, q1_hbm, kv_hbm, do1_hbm, l1_ref, i1_ref,
    x1_hbm, dx2_hbm, o0_hbm, w_hbm, l0_ref, p_ref, sent,
    up_out, down_out, dq1_hbm, dkv1_hbm, dx1_hbm, g1_hbm, dq_hbm, dkv_hbm, arrived, sum_q, sum_out, sum_gain, sum_shift,
    kept_ref, moving, held, q_buf, acc_ref, dq_buf, dkv_buf, dq1_ref, kv_ref, dkv1_ref, w_ref,
    x1_buf, dx2_buf, o_buf, dx1_buf, g1_buf, i0_ref, up_ref,
    in_sem, move_sem, q_sem, out_sem, tile_in, tile_out, *rest,
):
    place = Place(depth, ring)
    place.greet_all()
    me = place.index()
    blocks = du_hbm.shape[0]
    count = 2 * blocks
    rows, width = do1_hbm.shape
    pairs = width // PAIR
    tile = x1_buf.shape[1]
    tiles = rows // tile

    own = up_out.shape[0]

    def put_sum(u, total):
        if u < blocks:
            up_ref[u] = total
        else:
            down_out[(u - blocks) * own : (u - blocks + 1) * own] = total

    def place_up():
        for k in range(width // own):
            lines = [up_ref[j, :, k * own : (k + 1) * own] for j in range(blocks)]
            up_out[:, k * blocks * own : (k + 1) * blocks * own] = jnp.concatenate(lines, axis=1)

    sums = Scatter(place, count, own, held, put_sum, rest[:5], rest[5:11])
    swap = Exchange(place, ((sent, arrived),), count, rest[11:])
    slots = held.shape[0]
    load_a = pltpu.make_async_copy(a2_hbm, kept_ref, in_sem.at[0])
    load_g = pltpu.make_async_copy(g3_hbm, kept_ref, in_sem.at[1])
    load_kv = pltpu.make_async_copy(kv_hbm, kv_ref, in_sem.at[2])
    load_w = [pltpu.make_async_copy(w_hbm.at[u], w_ref.at[k], in_sem.at[3 + k]) for k, u in enumerate((4, 3))]
    send_dq1 = pltpu.make_async_copy(dq1_ref, dq1_hbm, in_sem.at[5])
    send_dkv1 = pltpu.make_async_copy(dkv1_ref, dkv1_hbm, in_sem.at[6])

    def move(u):
        source = du_hbm.at[u] if u < blocks else r_hbm.at[u - blocks]
        return pltpu.make_async_copy(source, moving, move_sem.at[0])

    def columns(h):
        return pl.ds(pl.multiple_of(h * PAIR, PAIR), PAIR)

    def fetch_cross(h):
        cols = columns(h)
        sources = [q1_hbm.at[0, :, cols], do1_hbm.at[:, cols]]
        return [pltpu.make_async_copy(s, q_buf.at[h % 2, k], q_sem.at[h % 2, k]) for k, s in enumerate(sources)]

    def fetch(h):
        cols = columns(h)
        return [pltpu.make_async_copy(qkv_hbm.at[k, :, cols], q_buf.at[h % 2, k], q_sem.at[h % 2, k]) for k in range(3)]

    def put(h):
        cols = columns(h)
        return [
            pltpu.make_async_copy(dq_buf.at[h % 2], dq_hbm.at[:, cols], out_sem.at[h % 2, 0]),
            pltpu.make_async_copy(dkv_buf.at[h % 2], dkv_hbm.at[:, :, cols], out_sem.at[h % 2, 1]),
        ]

    def load_tile(i):
        at, b = slice(i * tile, (i + 1) * tile), i % 2
        sources = ((x1_hbm, x1_buf), (dx2_hbm, dx2_buf), (o0_hbm, o_buf))
        return [pltpu.make_async_copy(s.at[at], d.at[b], tile_in.at[b, k]) for k, (s, d) in enumerate(sources)]

    def store_tile(i):
        at = slice(i * tile, (i + 1) * tile)
        targets = ((dx1_buf, dx1_hbm), (g1_buf, g1_hbm))
        return [pltpu.make_async_copy(s, d.at[at], tile_out.at[k]) for k, (s, d) in enumerate(targets)]

    def start(copies):
        for copy in copies:
            copy.start()

    def wait(copies):
        for copy in copies:
            copy.wait()

    load_a.start()
    move(0).start()
    load_kv.start()
    start(fetch_cross(0))
    swap.begin()
    start(load_w)
    for ref in (sum_q, sum_out, sum_gain, sum_shift):
        ref[...] = jnp.zeros_like(ref)
    load_a.wait()

    def weights(i):
        if i == blocks:
            load_g.wait()
        move(i).wait()
        if i >= slots:
            sums.core(i - slots).wait_send()
        if i < blocks:
            unit_grad(place, held, i % slots, kept_ref, moving, None)
            if i == blocks - 1:
                load_g.start()
        else:
            unit_grad(place, held, i % slots, moving, kept_ref, None)
        if i + 1 < count:
            move(i + 1).start()
        sums.core(i).start()

    def cross_pair(h):
        pl.when(h + 1 < pairs)(lambda: start(fetch_cross(h + 1)))
        wait(fetch_cross(h))
        b, cols = h % 2, columns(h)

        def store(at, grad_k, grad_v):
            dkv1_ref[0, at, cols] = grad_k
            dkv1_ref[1, at, cols] = grad_v

        back_pair(False, kv_ref.shape[1], h, 2 * pairs, m_ref[me], q_buf[b, 0], kv_ref[0, :, cols], kv_ref[1, :, cols],
                  q_buf[b, 1], l1_ref[...], i1_ref[...], acc_ref, store)
        dq1_ref[:, cols] = acc_ref[...].astype(LOW)

    def between(i):
        at, b = slice(i * tile, (i + 1) * tile), i % 2
        if i + 1 < tiles:
            start(load_tile(i + 1))
        wait(load_tile(i))
        dq = dq1_ref[at]
        grad = dot(dq, w_ref[0], NT) * SCALE
        hat, rstd = normal(x1_buf[b])
        back, lines, shifts = normal_back(hat, rstd, grad, p_ref[GAIN + 1 : GAIN + 2])
        dx1 = dx2_buf[b] + back
        g1 = dx1.astype(LOW)
        if i > 0:
            wait(store_tile(i - 1))
        dx1_buf[...] = dx1
        g1_buf[...] = g1
        start(store_tile(i))
        grad_mixed = dot(g1, w_ref[1], NT).astype(LOW)
        dq1_ref[at] = grad_mixed
        i0_ref[at] = inner_parts(grad_mixed, o_buf[b], 2 * pairs)
        sum_q[...] += jnp.sum(dq.astype(FULL), axis=0, keepdims=True) * SCALE
        sum_out[...] += jnp.sum(g1.astype(FULL), axis=0, keepdims=True)
        sum_gain[...] += lines
        sum_shift[...] += shifts

    def self_pair(h):
        pl.when(h + 1 < pairs)(lambda: start(fetch(h + 1)))
        wait(fetch(h))
        pl.when(h >= 2)(lambda: wait(put(h - 2)))
        b, cols = h % 2, columns(h)

        def store(at, grad_k, grad_v):
            dkv_buf[b, 0, at] = grad_k
            dkv_buf[b, 1, at] = grad_v

        back_pair(True, 256, h, 2 * pairs, n_ref[me], q_buf[b, 0], q_buf[b, 1], q_buf[b, 2], dq1_ref[:, cols],
                  l0_ref[...], i0_ref[...], acc_ref, store)
        dq_buf[b] = acc_ref[...].astype(LOW)
        start(put(h))

    def run(part, low, high):
        loop(high - low, lambda j: part(low + j))

    def work(i):
        if i < 2:
            if i == 0:
                load_kv.wait()
            run(cross_pair, i * (pairs // 2), (i + 1) * (pairs // 2))
            if i == 1:
                send_dq1.start()
                send_dkv1.start()
                start(load_tile(0))
                start(fetch(0))
                wait(load_w)
        elif i < 4:
            if i == 2:
                send_dq1.wait()
            for j in range((i - 2) * tiles // 2, (i - 1) * tiles // 2):
                between(j)
            if i == 3:
                wait(store_tile(tiles - 1))
        else:
            run(self_pair, shares[i - 4], shares[i - 3])

    steps = sums.steps()
    left = steps - 4
    shares = [pairs - ((left - k) * pairs + left - 1) // left for k in range(left + 1)]
    for i in range(steps):
        if i < count:
            weights(i)
        sums.early(i)
        work(i)
        sums.late(i)
        swap.step(i)
    for h in range(pairs - 2, pairs):
        wait(put(h))
    send_dkv1.wait()
    sums.last_sums()
    place_up()
    sums.finish()
    swap.finish()


def back_scatter(mesh, length, enc_count, a2, g3, du, r, qkv, q1, kv1, do1, level1, inner1, x1, dx2, mixed0, w, level0, p, sent, ident):
    depth, ring = mesh.shape["dp"] // 2, mesh.shape["fsdp"]
    blocks, rows, width = du.shape
    own = width // (2 * depth * ring)
    count = 2 * blocks
    enc = kv1.shape[1]
    tile = 256
    big = pltpu.VMEM((rows, width), LOW)
    low = jax.ShapeDtypeStruct((rows, width), LOW)
    line = jax.ShapeDtypeStruct((1, width), FULL)
    return pl.pallas_call(
        functools.partial(back_scatter_kernel, depth, ring),
        out_shape=[
            jax.ShapeDtypeStruct((own, blocks * width), FULL),
            jax.ShapeDtypeStruct((blocks * own, width), FULL),
            low,
            jax.ShapeDtypeStruct((2, enc, width), LOW),
            jax.ShapeDtypeStruct((rows, width), FULL),
            low,
            low,
            jax.ShapeDtypeStruct((2, rows, width), LOW),
            jax.ShapeDtypeStruct(sent.shape, sent.dtype),
            line,
            line,
            line,
            line,
        ],
        in_specs=[SMEM, SMEM] + [ANY] * 8 + [VMEM, VMEM] + [ANY] * 4 + [VMEM, VMEM, ANY],
        out_specs=[VMEM] * 2 + [ANY] * 7 + [VMEM] * 4,
        scratch_shapes=[
            big,
            big,
            pltpu.VMEM((2, depth, 2, ring * own, width), LOW),
            pltpu.VMEM((2, 3, rows, PAIR), LOW),
            pltpu.VMEM((rows, PAIR), FULL),
            pltpu.VMEM((2, rows, PAIR), LOW),
            pltpu.VMEM((2, 2, rows, PAIR), LOW),
            big,
            pltpu.VMEM((2, enc, width), LOW),
            pltpu.VMEM((2, enc, width), LOW),
            pltpu.VMEM((2, width, width), LOW),
            pltpu.VMEM((2, tile, width), FULL),
            pltpu.VMEM((2, tile, width), FULL),
            pltpu.VMEM((2, tile, width), LOW),
            pltpu.VMEM((tile, width), FULL),
            pltpu.VMEM((tile, width), LOW),
            pltpu.VMEM((rows, PAIR), LOW),
            pltpu.VMEM((blocks, own, width), FULL),
            DMA((7,)),
            DMA((1,)),
            DMA((2, 3)),
            DMA((2, 2)),
            DMA((2, 3)),
            DMA((2,)),
        ]
        + Scatter.refs(mesh, count, own, width, LOW)
        + Scatter.sems(mesh, count)
        + Exchange.sems(mesh, 1),
        compiler_params=remote_params(ident),
        cost_estimate=pl.CostEstimate(flops=90_000_000_000, bytes_accessed=2 * 33_554_432, transcendentals=0),
        name="back_scatter",
    )(length, enc_count, a2, g3, du, r, qkv, q1, kv1, do1, level1, inner1, x1, dx2, mixed0, w, level0, p, sent)


def last_scatter_kernel(
    depth, ring, e_hbm, dkv1_hbm, w_hbm, x_hbm, dx1_hbm, o1_hbm, g2_hbm, a1_hbm, dq1_hbm, o0_hbm, g1_hbm, a0_hbm, dq0_hbm,
    dkv_hbm, p_ref, tiny_ref,
    s_qkv, s_out, c_qkv, c_out, tiny_out, arrived, arrived_e, sent, sent_e,
    left, right, held, tiny_held, e_ref, dkv1_ref, w_ref, de_ref, x_buf, dq_buf, dkv_buf, dx1_buf, dx_buf,
    sum_q, sum_v, sum_m, sum_gain, sum_shift, left_sem, right_sem, in_sem, w_sem, tile_in, tile_out, *rest,
):
    place = Place(depth, ring)
    place.greet_all()
    made = 2
    spots = [c_qkv.at[1], c_qkv.at[2], c_qkv.at[0], c_out, s_out, s_qkv.at[0], s_qkv.at[1], s_qkv.at[2]]
    own = s_out.shape[0]

    def put_sum(u, total):
        spots[u][...] = total

    def put_tiny(u, total):
        tiny_out[u] = total

    pairs = [(a1_hbm, dq1_hbm), (o1_hbm, g2_hbm), (o0_hbm, g1_hbm), (a0_hbm, dq0_hbm), (a0_hbm, dkv_hbm.at[0]), (a0_hbm, dkv_hbm.at[1])]
    scaled = (0, 3)
    count = made + len(pairs)
    small = Scatter(place, 1, tiny_out.shape[1], tiny_held, put_tiny, rest[:5], rest[5:11])
    sums = Scatter(place, count, own, held, put_sum, rest[11:16], rest[16:22])
    slots = held.shape[0]
    rows, width = x_hbm.shape
    tile = x_buf.shape[1]
    tiles = rows // tile
    begun = 3
    swap = Exchange(place, ((sent, arrived), (sent_e, arrived_e)), count - begun, rest[22:])
    leaves = dx_buf.shape[1]

    def load(k):
        a, b = pairs[k]
        return [
            pltpu.make_async_copy(a, left.at[k % 2], left_sem.at[k % 2]),
            pltpu.make_async_copy(b, right.at[k % 2], right_sem.at[k % 2]),
        ]

    def load_tile(i):
        at, b = slice(i * tile, (i + 1) * tile), i % 2
        sources = ((x_hbm.at[at], x_buf), (dq0_hbm.at[at], dq_buf), (dkv_hbm.at[:, at], dkv_buf), (dx1_hbm.at[at], dx1_buf))
        return [pltpu.make_async_copy(s, d.at[b], tile_in.at[b, k]) for k, (s, d) in enumerate(sources)]

    def store_tile(i):
        many = tile // leaves
        return pltpu.make_async_copy(dx_buf, sent.at[i * many : (i + 1) * many], tile_out.at[0])

    def start(copies):
        for copy in copies:
            copy.start()

    def wait(copies):
        for copy in copies:
            copy.wait()

    load_e = [pltpu.make_async_copy(e_hbm, e_ref, in_sem.at[0]), pltpu.make_async_copy(dkv1_hbm, dkv1_ref, in_sem.at[1])]
    load_m = [pltpu.make_async_copy(w_hbm.at[5 + j], w_ref.at[j], w_sem.at[j]) for j in range(2)]
    load_w = [pltpu.make_async_copy(w_hbm.at[j], w_ref.at[j], w_sem.at[j]) for j in range(3)]
    send_e = pltpu.make_async_copy(de_ref, sent_e, in_sem.at[2])
    start(load_e)
    start(load_m)
    start(load_tile(0))
    for k in range(2):
        start(load(k))
    tiny_held[0] = tiny_ref[...]
    for ref in (sum_q, sum_v, sum_gain, sum_shift):
        ref[...] = jnp.zeros_like(ref)
    wait(load_e)

    def weights(i):
        if i >= slots:
            sums.core(i - slots).wait_send()
        if i < made:
            unit_grad(place, held, i % slots, e_ref, dkv1_ref.at[i], None)
        else:
            k = i - made
            wait(load(k))
            unit_grad(place, held, i % slots, left.at[k % 2], right.at[k % 2], SCALE if k in scaled else None)
            if k + 2 < len(pairs):
                start(load(k + 2))
        sums.core(i).start()

    def memory_back():
        wait(load_m)
        back = dot(dkv1_ref[0], w_ref[0], NT) + dot(dkv1_ref[1], w_ref[1], NT)
        de_ref[...] = back.astype(LOW).reshape(de_ref.shape)
        send_e.start()
        start(load_w)
        sum_m[...] = jnp.sum(dkv1_ref[1].astype(FULL), axis=0, keepdims=True)

    def part(i):
        b = i % 2
        if i + 1 < tiles:
            start(load_tile(i + 1))
        wait(load_tile(i))
        if i == 0:
            wait(load_w)
        dq = dq_buf[b]
        grad = dot(dq, w_ref[0], NT) * SCALE + dot(dkv_buf[b, 0], w_ref[1], NT) + dot(dkv_buf[b, 1], w_ref[2], NT)
        hat, rstd = normal(x_buf[b].astype(FULL))
        back, lines, shifts = normal_back(hat, rstd, grad, p_ref[GAIN : GAIN + 1])
        dx = (dx1_buf[b] + back).astype(LOW)
        if i > 0:
            store_tile(i - 1).wait()
        dx_buf[...] = dx.reshape(dx_buf.shape)
        store_tile(i).start()
        sum_q[...] += jnp.sum(dq.astype(FULL), axis=0, keepdims=True) * SCALE
        sum_v[...] += jnp.sum(dkv_buf[b, 1].astype(FULL), axis=0, keepdims=True)
        sum_gain[...] += lines
        sum_shift[...] += shifts

    def place_lines():
        for line, ref in ((0, sum_q), (1, sum_v), (4, sum_m), (7, sum_gain), (10, sum_shift)):
            row, lane = line * own // 128, line * own % 128
            for k in range(width // own):
                d, g = k // ring, k % ring
                at = g * tiny_out.shape[1] + row
                tiny_held[0, d // 2, d % 2, at : at + 1, lane : lane + own] = ref[:, k * own : (k + 1) * own]

    def work(i):
        if i == 0:
            memory_back()
        elif i == 1:
            for j in range(tiles // 2):
                part(j)
        elif i == 2:
            for j in range(tiles // 2, tiles):
                part(j)
            store_tile(tiles - 1).wait()
            send_e.wait()
            swap.begin()
            place_lines()
            small.core(0).start()

    for i in range(sums.steps()):
        if i < count:
            weights(i)
        sums.early(i)
        if 0 <= i - begun < small.steps():
            small.early(i - begun)
        work(i)
        sums.late(i)
        if 0 <= i - begun < small.steps():
            small.late(i - begun)
        if i >= begun - 1:
            swap.step(i - begun + 1)
    small.last_sums()
    sums.last_sums()
    small.finish()
    sums.finish()
    swap.finish()


def last_scatter(mesh, memory, dkv1, w, x, dx1, pairs, p, tiny, like, like_e, ident):
    depth, ring = mesh.shape["dp"] // 2, mesh.shape["fsdp"]
    rows, width = x.shape
    enc = memory.shape[0]
    own = width // (2 * depth * ring)
    count = 8
    tile = 256
    tiny_rows = tiny.shape[2] // ring
    line = pltpu.VMEM((1, width), FULL)
    moved = [jax.ShapeDtypeStruct(like, LOW), jax.ShapeDtypeStruct(like_e, LOW)]
    return pl.pallas_call(
        functools.partial(last_scatter_kernel, depth, ring),
        out_shape=[
            jax.ShapeDtypeStruct((3, own, width), FULL),
            jax.ShapeDtypeStruct((own, width), FULL),
            jax.ShapeDtypeStruct((3, own, width), FULL),
            jax.ShapeDtypeStruct((own, width), FULL),
            jax.ShapeDtypeStruct((1, tiny_rows, tiny.shape[3]), FULL),
        ]
        + moved
        + moved,
        in_specs=[ANY] * (5 + len(pairs)) + [VMEM, VMEM],
        out_specs=[VMEM] * 5 + [ANY] * 4,
        scratch_shapes=[
            pltpu.VMEM((2, rows, width), LOW),
            pltpu.VMEM((2, rows, width), LOW),
            pltpu.VMEM((2, depth, 2, ring * own, width), LOW),
            pltpu.VMEM((1,) + tiny.shape, FULL),
            pltpu.VMEM((enc, width), LOW),
            pltpu.VMEM((2, enc, width), LOW),
            pltpu.VMEM((3, width, width), LOW),
            pltpu.VMEM(like_e, LOW),
            pltpu.VMEM((2, tile, width), LOW),
            pltpu.VMEM((2, tile, width), LOW),
            pltpu.VMEM((2, 2, tile, width), LOW),
            pltpu.VMEM((2, tile, width), FULL),
            pltpu.VMEM((tile // like[1],) + like[1:], LOW),
            line,
            line,
            line,
            line,
            line,
            DMA((2,)),
            DMA((2,)),
            DMA((3,)),
            DMA((3,)),
            DMA((2, 4)),
            DMA((1,)),
        ]
        + Scatter.refs(mesh, 1, tiny_rows, tiny.shape[3], FULL)
        + Scatter.sems(mesh, 1)
        + Scatter.refs(mesh, count, own, width, LOW)
        + Scatter.sems(mesh, count)
        + Exchange.sems(mesh, 2),
        compiler_params=remote_params(ident),
        cost_estimate=pl.CostEstimate(flops=60_000_000_000, bytes_accessed=2 * 33_554_432, transcendentals=0),
        name="last_scatter",
    )(memory, dkv1, w, x, dx1, *pairs, p, tiny)


CUBIC = 0.044715
ROOT = 0.7978845608028654


def feed_kernel(
    n_ref, x1_ref, o_ref, g_ref, w_hbm, p_ref, bu_ref,
    out_ref, r_ref, du_ref, a_ref, g3_ref, dx_ref, g2_ref, do_ref, inner_ref,
    sum_up, sum_down, sum_five, sum_gain, sum_shift,
    w_ref, slope_ref, sems,
):
    i = pl.program_id(0)
    first = i == 0
    tile, width = x1_ref.shape
    blocks = (w_hbm.shape[0] - 1) // 2
    order = [0] + [k * blocks + j + 1 for j in range(blocks) for k in range(2)]
    loads = {u: pltpu.make_async_copy(w_hbm.at[u], w_ref.at[u], sems.at[u]) for u in order}

    @pl.when(first)
    def _():
        for u in order:
            loads[u].start()
        for ref in (sum_up, sum_down, sum_five, sum_gain, sum_shift):
            ref[...] = jnp.zeros_like(ref)
        loads[0].wait()

    valid = jnp.where(i * tile + rows_of((tile, 1)) < n_ref[lax.axis_index(AXES)], 1.0, 0.0)
    x2 = x1_ref[...] + (dot(o_ref[...], w_ref[0], NN) + p_ref[5:6])
    hat, rstd = normal(x2)
    gain = p_ref[GAIN + 2 : GAIN + 3]
    a_ref[...] = (hat * gain + p_ref[SHIFT + 2 : SHIFT + 3]).astype(LOW)

    @pl.when(first)
    def _():
        for u in order[1:]:
            loads[u].wait()

    total = x2 + p_ref[DOWN : DOWN + 1]
    for j in range(blocks):
        cols = slice(j * width, (j + 1) * width)
        u = dot(a_ref[...], w_ref[1 + j], NN) + bu_ref[:, cols]
        square = u * u
        t = jnp.tanh(ROOT * (u * (1.0 + CUBIC * square)))
        half = 0.5 * (1.0 + t)
        r = (u * half).astype(LOW)
        r_ref[j] = r
        slope = half + 0.5 * u * (1.0 - t * t) * (ROOT * (1.0 + 3.0 * CUBIC * square))
        slope_ref[:, cols] = slope.astype(LOW)
        total = total + dot(r, w_ref[1 + blocks + j], NN)
    out_ref[...] = (total * valid).astype(LOW)
    grad_out = g_ref[...].astype(FULL) * valid
    g3 = grad_out.astype(LOW)
    g3_ref[...] = g3
    grad = jnp.zeros((tile, width), FULL)
    for j in range(blocks):
        cols = slice(j * width, (j + 1) * width)
        du = (dot(g3, w_ref[1 + blocks + j], NT) * slope_ref[:, cols].astype(FULL)).astype(LOW)
        du_ref[j] = du
        line = jnp.sum(du.astype(FULL), axis=0, keepdims=True)

        sum_up[:, cols] += line
        grad = grad + dot(du, w_ref[1 + j], NT)
    back, lines, shifts = normal_back(hat, rstd, grad, gain)
    dx2 = grad_out + back
    dx_ref[...] = dx2
    g2 = dx2.astype(LOW)
    g2_ref[...] = g2
    grad_mixed = dot(g2, w_ref[0], NT).astype(LOW)
    do_ref[...] = grad_mixed
    inner_ref[...] = inner_parts(grad_mixed, o_ref[...], width // HD)
    sum_down[...] += jnp.sum(g3.astype(FULL), axis=0, keepdims=True)
    sum_five[...] += jnp.sum(g2.astype(FULL), axis=0, keepdims=True)
    sum_gain[...] += lines
    sum_shift[...] += shifts


def feed(length, x1, mixed, cotangent, w, p, bias_up, tile=256):
    rows, width = x1.shape
    blocks = (w.shape[0] - 1) // 2
    inner = blocks * width
    part = pl.BlockSpec((tile, width), lambda i: (i, 0))
    broad = pl.BlockSpec((blocks, tile, width), lambda i: (0, i, 0))
    thin = pl.BlockSpec((tile, PAIR), lambda i: (i, 0))
    low = jax.ShapeDtypeStruct((rows, width), LOW)
    wide = jax.ShapeDtypeStruct((blocks, rows, width), LOW)
    line = jax.ShapeDtypeStruct((1, width), FULL)
    return calls(
        feed_kernel,
        "feed",
        2 * rows * width * (4 * inner + 2 * width),
        2 * rows * (9 * width + 2 * inner) + 4 * inner * width,
        grid=(rows // tile,),
        in_specs=[SMEM, part, part, part, ANY, whole(p.shape), whole(bias_up.shape)],
        out_specs=[part, broad, broad, part, part, part, part, part, thin, whole((1, inner))] + [whole((1, width))] * 4,
        out_shape=[low, wide, wide, low, low, jax.ShapeDtypeStruct((rows, width), FULL), low, low,
                   jax.ShapeDtypeStruct((rows, PAIR), LOW), jax.ShapeDtypeStruct((1, inner), FULL), line, line, line, line],
        scratch_shapes=[pltpu.VMEM(w.shape, LOW), pltpu.VMEM((tile, inner), LOW), DMA((w.shape[0],))],
    )(length, x1, mixed, cotangent, w, p, bias_up)


AXES = ("dp", "fsdp")


def per_device(
    mesh,
    units,
    encoder,
    cotangent,
    deal,
    lengths,
    enc_counts,
    self_qkv,
    self_out,
    cross_qkv,
    cross_out,
    ffn_up,
    ffn_down,
    biases,
    ffn_bias_up,
    ffn_bias_down,
    norm_gain,
    norm_shift,
):
    slots = deal.shape[0]
    depth, ring = mesh.shape["dp"] // 2, mesh.shape["fsdp"]
    own, width = self_out.shape
    blocks = ffn_up.shape[1] // width
    sent_x, sent_e, sent_c = deal_blocks(deal, [units, encoder, cotangent], False, "deal_in")

    up = ffn_up.reshape(own, slots, blocks, own).transpose(2, 0, 1, 3).reshape(blocks, own, width)
    late = jnp.concatenate([cross_out[None], up, ffn_down.reshape(blocks, own, width)])
    rows = jnp.concatenate([biases, norm_gain, norm_shift, ffn_bias_down[None]])
    flat = jnp.concatenate([rows.reshape(-1), ffn_bias_up])
    size = -(-flat.shape[0] // 2048) * 2048
    little = jnp.pad(flat, (0, size - flat.shape[0])).reshape(1, size // 128, 128)
    w_one, little, x, memory = first_gather(mesh, [self_qkv, self_out, cross_qkv], little, [sent_x, sent_e], 0)
    w_one = w_one.reshape(-1, width, width)
    x, memory = x.reshape(-1, width), memory.reshape(-1, width)
    flat = little.reshape(slots, size).astype(FULL)
    p = flat[:, : rows.size].reshape((slots,) + rows.shape)
    p = jnp.moveaxis(p, 0, 1).reshape(rows.shape[0], -1)
    p = jnp.pad(p, ((0, 16 - rows.shape[0]), (0, 0)))
    bias_up = flat[:, rows.size : rows.size + ffn_bias_up.size].reshape(slots, blocks, own)
    bias_up = bias_up.transpose(1, 0, 2).reshape(1, -1)

    w_two, cot, a0, qkv, mixed0, level0, x1, a1, q1, kv1, mixed1, level1 = forward(
        mesh, lengths, enc_counts, x, memory, w_one, p, late, sent_c, 1
    )
    cot = cot.reshape(-1, width)
    w_two = w_two.reshape(late.shape[0], width, width)
    (result, r, du, a2, g3, dx2, g2, grad_mixed1, inner1, bias_up_grad, bias_down_grad, bias_five, gain_two, shift_two) = feed(
        lengths, x1, mixed1, cot, w_two, p, bias_up
    )
    up_sum, down_sum, dq1, dkv1, dx1, g1, dq0, dkv0, result, bias_three, bias_two, gain_one, shift_one = back_scatter(
        mesh, lengths, enc_counts, a2, g3, du, r, qkv, q1, kv1, grad_mixed1, level1, inner1, x1, dx2, mixed0, w_one, level0, p,
        result.reshape(slots, -1, width), 2,
    )
    bias_zero = bias_one = bias_four = gain_zero = shift_zero = jnp.zeros_like(bias_two)

    bias_up_grad = bias_up_grad.reshape(blocks, slots, own).transpose(1, 0, 2).reshape(slots, -1)

    def by_owner(*lines):
        return jnp.concatenate(lines).reshape(len(lines), slots, own).transpose(1, 0, 2).reshape(slots, -1)

    terms = jnp.concatenate(
        [
            by_owner(
                bias_zero, bias_one, bias_two, bias_three, bias_four, bias_five, bias_down_grad,
                gain_zero, gain_one, gain_two, shift_zero, shift_one, shift_two,
            ),
            bias_up_grad,
        ],
        axis=1,
    )
    tiny = -(-terms.shape[1] // 1024) * 8
    terms = jnp.pad(terms, ((0, 0), (0, tiny * 128 - terms.shape[1]))).reshape(depth, 2, ring * tiny, 128)
    pairs = (mixed1, g2, a1, dq1, mixed0, g1, a0, dq0, dkv0)
    self_qkv_sum, self_out_sum, cross_qkv_sum, cross_out_sum, tiny_sums, dx, grad_memory = last_scatter(
        mesh, memory, dkv1, w_one, x, dx1, pairs, p, terms, units.shape, encoder.shape, 3
    )[:7]
    result, dx, grad_memory = deal_blocks(deal, [result, dx, grad_memory], True, "deal_out")
    flat = tiny_sums.reshape(-1)
    lines = flat[: 13 * own].reshape(13, own)
    return (
        result,
        dx,
        grad_memory,
        self_qkv_sum,
        self_out_sum,
        cross_qkv_sum,
        cross_out_sum,
        up_sum,
        down_sum,
        lines[:6],
        flat[13 * own : 13 * own + ffn_bias_up.size],
        lines[6],
        lines[7:10],
        lines[10:13],
    )


def solution(mesh):
    middle_rows = P(None, AXES, None)
    first_rows = P(AXES, None)
    last = P(None, AXES)
    weights = (middle_rows, first_rows, middle_rows, first_rows, first_rows, first_rows, last, P(AXES), P(AXES), last, last)
    return jax.shard_map(
        functools.partial(per_device, mesh),
        mesh=mesh,
        in_specs=(middle_rows,) * 3 + (P(),) * 3 + weights,
        out_specs=(middle_rows,) * 3 + weights,
        check_vma=False,
    )
```

```python
import functools

import jax
import jax.numpy as jnp
from jax import lax
from jax.experimental import pallas as pl
from jax.experimental.pallas import tpu as pltpu
from jax.sharding import PartitionSpec as P

HD = 64
EPSILON = 1e-05
SCALE = 0.125
NEGATIVE = -1e30
MESH = pl.DeviceIdType.MESH
ANY = pl.BlockSpec(memory_space=pl.ANY)
DMA = pltpu.SemaphoreType.DMA


def ring_place(f, ring):
    half = ring // 2
    upper, rest = f // half, f % half
    return upper * half + rest + upper * (half - 1 - 2 * rest)


class Place:
    def __init__(self, depth, ring):
        self.depth, self.ring, self.half = depth, ring, ring // 2
        d, f = lax.axis_index("dp"), lax.axis_index("fsdp")
        self.z, self.c, self.f = d // 2, d % 2, f
        self.at = ring_place(f, ring)
        self.right = ring_place((self.at + 1) % ring, ring)
        self.left = ring_place((self.at + ring - 1) % ring, ring)

    def greet(self):
        barrier = pltpu.get_barrier_semaphore()

        def hail(d, g):
            pl.semaphore_signal(barrier, inc=1, device_id=(d, g), device_id_type=MESH)

        for s in range(1, self.depth):
            hail((self.z + s) % self.depth * 2 + self.c, self.f)
        hail(self.z * 2 + self.c, self.right)
        hail(self.z * 2 + self.c, self.left)
        hail(self.z * 2 + 1 - self.c, self.f)
        pl.semaphore_wait(barrier, self.depth + 2)

    def index(self):
        return (self.z * 2 + self.c) * self.ring + self.f

    def peers(self):
        return 2 * self.depth * self.ring

    def peer(self, k, sign):
        dz, dc, df = k % self.depth, k // self.depth % 2, k // self.depth // 2
        z = (self.z + sign * dz + self.depth) % self.depth
        f = (self.f + sign * df + self.ring) % self.ring
        return z * 2 + (self.c + dc) % 2, f

    def greet_all(self):
        barrier = pltpu.get_barrier_semaphore()

        def hail(k):
            pl.semaphore_signal(barrier, inc=1, device_id=self.peer(k + 1, 1), device_id_type=MESH)

        loop(self.peers() - 1, hail)
        pl.semaphore_wait(barrier, self.peers() - 1)

    def to_z(self, src, dst, send, recv, s):
        return self.remote(src, dst, send, recv, (self.z + s) % self.depth * 2 + self.c, self.f)

    def to_side(self, src, dst, send, recv, way):
        return self.remote(src, dst, send, recv, self.z * 2 + self.c, (self.right, self.left)[way])

    def to_core(self, src, dst, send, recv):
        return self.remote(src, dst, send, recv, self.z * 2 + 1 - self.c, self.f)

    @staticmethod
    def remote(src, dst, send, recv, d, g):
        return pltpu.make_async_remote_copy(
            src_ref=src, dst_ref=dst, send_sem=send, recv_sem=recv,
            device_id=(d, g), device_id_type=MESH,
        )


def when(flag, run):
    if isinstance(flag, bool):
        if flag:
            run()
    else:
        pl.when(flag)(run)


def both(one, two):
    if isinstance(one, bool) and isinstance(two, bool):
        return one and two
    return jnp.logical_and(one, two)


def loop(count, run):
    def body(i, carry):
        run(i)
        return carry

    lax.fori_loop(0, count, body, 0)


class Gather:
    def __init__(self, place, count, shards, fulls, sems, ahead=2):
        self.place, self.count, self.shards, self.fulls = place, count, shards, fulls
        self.local, self.z_send, self.z_recv, self.r_send, self.r_recv, self.c_send, self.c_recv = sems
        self.ahead = min(ahead, count)

    @staticmethod
    def sems(mesh, n):
        depth, ring = mesh.shape["dp"] // 2, mesh.shape["fsdp"]
        half = ring // 2
        return [DMA((n,)), DMA((n, depth)), DMA((n, depth)), DMA((n, half, 2)), DMA((n, half, 2)), DMA((n, ring)), DMA((n, ring))]

    def chunk(self, u, zs, c, g):
        return self.fulls.at[u, zs, c, g]

    def shard(self, u):
        if callable(self.shards):
            return self.shards(u if isinstance(u, int) else 0)
        return self.shards.at[u]

    def kept(self, u):
        p = self.place
        return pltpu.make_async_copy(self.shard(u), self.chunk(u, p.z, p.c, p.f), self.local.at[u])

    def z_copy(self, u, s, incoming):
        p = self.place
        origin = (p.z + p.depth - s) % p.depth if incoming else p.z
        return p.to_z(self.shard(u), self.chunk(u, origin, p.c, p.f), self.z_send.at[u, s], self.z_recv.at[u, s], s)

    def ring_copy(self, u, t, way, incoming):
        p = self.place
        back = t - 1 + incoming
        origin = (p.at + p.ring - back) % p.ring if way == 0 else (p.at + back) % p.ring
        cut = p.depth // 2
        zs = slice(0, p.depth) if t < p.half else (slice(0, cut), slice(cut, p.depth))[way]
        piece = self.chunk(u, zs, p.c, ring_place(origin, p.ring))
        return p.to_side(piece, piece, self.r_send.at[u, t - 1, way], self.r_recv.at[u, t - 1, way], way)

    def core_copy(self, u, shift, incoming):
        p = self.place
        c = 1 - p.c if incoming else p.c
        piece = self.chunk(u, slice(0, p.depth), c, ring_place((p.at + shift) % p.ring, p.ring))
        return p.to_core(piece, piece, self.c_send.at[u, shift], self.c_recv.at[u, shift])

    def start_z(self, u):
        self.kept(u).start()
        for s in range(1, self.place.depth):
            self.z_copy(u, s, False).start()

    def start_ring(self, u, t):
        for way in range(2):
            self.ring_copy(u, t, way, 0).start()

    def start_core(self, u, t):
        half, ring = self.place.half, self.place.ring
        for shift in [0] if t == 0 else [t] if t == half else [ring - t, t]:
            self.core_copy(u, shift, False).start()

    def begin(self):
        for u in range(self.ahead):
            self.start_z(u)

    def steps(self):
        return self.count + self.place.half

    def step(self, i):
        place = self.place

        def first():
            self.kept(i).wait()
            for s in range(1, place.depth):
                self.z_copy(i, s, True).wait_recv()
            self.start_ring(i, 1)
            self.start_core(i, 0)

        def later(u, t):
            for way in range(2):
                self.ring_copy(u, t, way, 1).wait_recv()
            if t < place.half:
                self.start_ring(u, t + 1)
            self.start_core(u, t)

        when(i + self.ahead < self.count, lambda: self.start_z(i + self.ahead))
        when(i < self.count, first)
        for t in range(1, place.half + 1):
            u = i - t
            when(both(0 <= u, u < self.count), functools.partial(later, u, t))

    def finish(self):
        place = self.place

        def one(u):
            for s in range(1, place.depth):
                self.z_copy(u, s, False).wait_send()
            for t in range(1, place.half + 1):
                for way in range(2):
                    self.ring_copy(u, t, way, 0).wait_send()
            for shift in range(place.ring):
                self.core_copy(u, shift, False).wait_send()
                self.core_copy(u, shift, True).wait_recv()

        loop(self.count, one)


class Exchange:
    def __init__(self, place, arrays, steps, sems):
        self.place, self.arrays = place, arrays
        self.send, self.recv, self.local = sems
        self.each = -(-(place.peers() - 1) // steps)

    @staticmethod
    def sems(mesh, n):
        peers = 2 * (mesh.shape["dp"] // 2) * mesh.shape["fsdp"]
        return [DMA((n, peers)), DMA((n, peers)), DMA((n,))]

    def block(self, d, f):
        return d * self.place.ring + f

    def own(self, a):
        p = self.place
        src, dst = self.arrays[a]
        me = self.block(p.z * 2 + p.c, p.f)
        return pltpu.make_async_copy(src.at[me], dst.at[me], self.local.at[a])

    def copy(self, a, k, incoming):
        p = self.place
        src, dst = self.arrays[a]
        d, f = p.peer(k, 1)
        at, g = p.peer(k, -1) if incoming else (p.z * 2 + p.c, p.f)
        return p.remote(src.at[self.block(d, f)], dst.at[self.block(at, g)], self.send.at[a, k], self.recv.at[a, k], d, f)

    def begin(self):
        for a in range(len(self.arrays)):
            self.own(a).start()

    def start(self, k):
        for a in range(len(self.arrays)):
            self.copy(a, k, False).start()

    def step(self, i):
        for j in range(self.each):
            k = 1 + i * self.each + j
            when(k < self.place.peers(), functools.partial(self.start, k))

    def finish(self):
        def one(k):
            for a in range(len(self.arrays)):
                self.copy(a, k + 1, False).wait_send()
                self.copy(a, k + 1, True).wait_recv()

        loop(self.place.peers() - 1, one)
        for a in range(len(self.arrays)):
            self.own(a).wait()


class Scatter:
    def __init__(self, place, count, rows, held, put, refs, sems):
        self.place, self.count, self.rows, self.held, self.put = place, count, rows, held, put
        self.mine, self.theirs, self.rhalf, self.rfull, self.zbuf = refs
        self.c_send, self.c_recv, self.r_send, self.r_recv, self.z_send, self.z_recv = sems
        self.slots = held.shape[0]

    @staticmethod
    def refs(mesh, n, rows, cols, low):
        depth, ring = mesh.shape["dp"] // 2, mesh.shape["fsdp"]
        half, cut = ring // 2, depth // 2
        return [
            pltpu.VMEM((n, depth, ring, rows, cols), low),
            pltpu.VMEM((n, depth, ring * rows, cols), low),
            pltpu.VMEM((n, 2, cut, rows, cols), low),
            pltpu.VMEM((n, half - 1, 2, depth, rows, cols), low),
            pltpu.VMEM((n, depth - 1, rows, cols), low),
        ]

    @staticmethod
    def sems(mesh, n):
        depth, ring = mesh.shape["dp"] // 2, mesh.shape["fsdp"]
        half = ring // 2
        return [DMA((n,)), DMA((n,)), DMA((n, half, 2)), DMA((n, half, 2)), DMA((n, depth)), DMA((n, depth))]

    def core(self, u):
        p = self.place
        return p.to_core(self.held.at[u % self.slots, slice(0, p.depth), 1 - p.c], self.theirs.at[u], self.c_send.at[u], self.c_recv.at[u])

    def dest(self, t, way):
        p = self.place
        ahead = p.half - t + 1
        return ring_place((p.at + ahead) % p.ring if way == 0 else (p.at + p.ring - ahead) % p.ring, p.ring)

    def ring_copy(self, u, t, way):
        p = self.place
        g, cut = self.dest(t, way), p.depth // 2
        if t == 1:
            src = self.mine.at[u, slice(0, cut) if way == 0 else slice(cut, p.depth), g]
            dst = self.rhalf.at[u, way]
        else:
            src = self.mine.at[u, slice(0, p.depth), g]
            dst = self.rfull.at[u, t - 2, way]
        return p.to_side(src, dst, self.r_send.at[u, t - 1, way], self.r_recv.at[u, t - 1, way], way)

    def z_copy(self, u, s):
        p = self.place
        to = (p.z + s) % p.depth
        return p.to_z(self.mine.at[u, to, p.f], self.zbuf.at[u, s - 1], self.z_send.at[u, s], self.z_recv.at[u, s], s)

    def first_sum(self, u):
        p, full = self.place, jnp.float32
        self.core(u).wait_recv()

        def one(a):
            total = self.held[u % self.slots, a, p.c].astype(full) + self.theirs[u, a].astype(full)
            for g in range(p.ring):
                self.mine[u, a, g] = total[g * self.rows : (g + 1) * self.rows].astype(self.mine.dtype)

        loop(p.depth, one)
        for way in range(2):
            self.ring_copy(u, 1, way).start()

    def next_sum(self, u, t):
        p, full, mine = self.place, jnp.float32, self.mine
        for way in range(2):
            self.ring_copy(u, t, way).wait_recv()
        cut = p.depth // 2
        if t < p.half:
            for way in range(2):
                g = self.dest(t + 1, way)
                low = cut * way if t == 1 else 0
                src = self.rhalf.at[u, way] if t == 1 else self.rfull.at[u, t - 2, way]

                def one(a, g=g, low=low, src=src):
                    mine[u, low + a, g] = (mine[u, low + a, g].astype(full) + src[a].astype(full)).astype(mine.dtype)

                loop(cut if t == 1 else p.depth, one)
                self.ring_copy(u, t + 1, way).start()
        else:
            left, right = self.rfull.at[u, t - 2, 0], self.rfull.at[u, t - 2, 1]

            def one(a):
                mine[u, a, p.f] = (
                    mine[u, a, p.f].astype(full) + left[a].astype(full) + right[a].astype(full)
                ).astype(mine.dtype)

            loop(p.depth, one)
            for s in range(1, p.depth):
                self.z_copy(u, s).start()

    def last_sum(self, u):
        p, full = self.place, jnp.float32
        for s in range(1, p.depth):
            self.z_copy(u, s).wait_recv()
        total = self.mine[u, p.z, p.f].astype(full)
        for s in range(1, p.depth):
            total = total + self.zbuf[u, s - 1].astype(full)
        self.put(u, total)

    def finish(self):
        p = self.place

        def one(u):
            for t in range(1, p.half + 1):
                for way in range(2):
                    self.ring_copy(u, t, way).wait_send()
            for s in range(1, p.depth):
                self.z_copy(u, s).wait_send()

        loop(self.count, one)
        for u in range(max(0, self.count - self.slots), self.count):
            self.core(u).wait_send()

    def last_sums(self):
        for u in range(self.count):
            self.last_sum(u)

    def steps(self):
        return self.count + self.place.half // 2

    def early(self, i):
        for t in range(1, self.place.half + 1, 2):
            u = i - (t + 1) // 2
            when(both(0 <= u, u < self.count), functools.partial(self.next_sum, u, t))

    def late(self, i):
        when(i < self.count, lambda: self.first_sum(i))
        for t in range(2, self.place.half + 1, 2):
            u = i - t // 2
            when(both(0 <= u, u < self.count), functools.partial(self.next_sum, u, t))


def remote_params(ident):
    return pltpu.CompilerParams(collective_id=ident, has_side_effects=True, vmem_limit_bytes=60 * 2**20)


def take(deal_ref, sources, taken):
    def one(i):
        for src, dst in zip(sources, taken, strict=True):
            dst[i] = src[deal_ref[i]]

    loop(deal_ref.shape[0], one)


def first_gather_kernel(depth, ring, where, n_w, n_x, deal_ref, *refs):
    weights, little, sent = refs[:n_w], refs[n_w], refs[n_w + 1 : n_w + 1 + n_x]
    full, little_full, arrived = refs[n_w + 1 + n_x], refs[n_w + 2 + n_x], refs[n_w + 3 + n_x : n_w + 3 + 2 * n_x]
    taken, sems = refs[n_w + 3 + 2 * n_x : n_w + 3 + 3 * n_x], refs[n_w + 3 + 3 * n_x :]
    place = Place(depth, ring)
    place.greet_all()
    count = len(where)

    def shard(u):
        which, lead = where[u]
        return weights[which] if lead is None else weights[which].at[lead]

    small = Gather(place, 1, little, little_full, sems[:7])
    big = Gather(place, count, shard, full, sems[7:14], ahead=count)
    swap = Exchange(place, tuple(zip(taken, arrived, strict=True)), max(1, big.steps() - 5), sems[14:])
    small.begin()
    big.begin()
    take(deal_ref, sent, taken)
    swap.begin()
    for i in range(big.steps()):
        swap.step(i)
        if i < small.steps():
            small.step(i)
        big.step(i)
    small.finish()
    big.finish()
    swap.finish()


def first_gather(mesh, deal, weights, little, sent, ident):
    depth, ring = mesh.shape["dp"] // 2, mesh.shape["fsdp"]
    where = []
    for which, a in enumerate(weights):
        where += [(which, None)] if a.ndim == 2 else [(which, lead) for lead in range(a.shape[0])]
    count = len(where)

    def full(n, a):
        return jax.ShapeDtypeStruct((n, depth, 2, ring) + a.shape[-2:], a.dtype)

    same = [jax.ShapeDtypeStruct(a.shape, a.dtype) for a in sent]
    return pl.pallas_call(
        functools.partial(first_gather_kernel, depth, ring, tuple(where), len(weights), len(sent)),
        out_shape=[full(count, weights[0]), full(1, little)] + same,
        in_specs=[pl.BlockSpec(memory_space=pltpu.SMEM)] + [pl.BlockSpec(memory_space=pltpu.VMEM)] * (len(weights) + 1 + len(sent)),
        out_specs=[ANY] * (2 + len(sent)),
        scratch_shapes=[pltpu.VMEM(a.shape, a.dtype) for a in sent]
        + Gather.sems(mesh, 1)
        + Gather.sems(mesh, count)
        + Exchange.sems(mesh, len(sent)),
        compiler_params=remote_params(ident),
        cost_estimate=pl.CostEstimate(flops=60_000_000_000, bytes_accessed=2 * 33_554_432, transcendentals=0),
        name="first_gather",
    )(deal, *weights, little, *sent)


def deal_kernel(out_of, n, deal_ref, *refs):
    sources, dests, held, sem = refs[:n], refs[n : 2 * n], refs[2 * n : 3 * n], refs[3 * n]
    slots = deal_ref.shape[0]

    def load(a, i):
        return pltpu.make_async_copy(sources[a].at[i if out_of else deal_ref[i]], held[a].at[i], sem.at[0, a, i])

    def store(a, i):
        return pltpu.make_async_copy(held[a].at[i], dests[a].at[deal_ref[i] if out_of else i], sem.at[1, a, i])

    def begin(i):
        for a in range(n):
            load(a, i).start()

    def turn(i):
        for a in range(n):
            load(a, i).wait()
            store(a, i).start()

    def end(i):
        for a in range(n):
            store(a, i).wait()

    loop(slots, begin)
    loop(slots, turn)
    loop(slots, end)


def deal_blocks(deal, arrays, out_of, name):
    n = len(arrays)
    return pl.pallas_call(
        functools.partial(deal_kernel, out_of, n),
        out_shape=[jax.ShapeDtypeStruct(a.shape, a.dtype) for a in arrays],
        in_specs=[pl.BlockSpec(memory_space=pltpu.SMEM)] + [ANY] * n,
        out_specs=[ANY] * n,
        scratch_shapes=[pltpu.VMEM(a.shape, a.dtype) for a in arrays] + [DMA((2, n, deal.shape[0]))],
        compiler_params=pltpu.CompilerParams(vmem_limit_bytes=60 * 2**20),
        name=name,
    )(deal, *arrays)


NN = (((1,), (0,)), ((), ()))
NT = (((1,), (1,)), ((), ()))
TN = (((0,), (0,)), ((), ()))
LOW = jnp.bfloat16
FULL = jnp.float32
SMEM = pl.BlockSpec(memory_space=pltpu.SMEM)
VMEM = pl.BlockSpec(memory_space=pltpu.VMEM)
PAIR = 2 * HD
ROOM = 60 * 2**20


def dot(left, right, how):
    return lax.dot_general(left, right, how, preferred_element_type=FULL)


def calls(kernel, name, flops, moved, **kw):
    return pl.pallas_call(
        kernel,
        name=name,
        compiler_params=pltpu.CompilerParams(vmem_limit_bytes=ROOM),
        cost_estimate=pl.CostEstimate(flops=int(flops), bytes_accessed=int(moved), transcendentals=0),
        **kw,
    )


def whole(shape):
    return pl.BlockSpec(shape, lambda *_: (0,) * len(shape))


def normal(x):
    mean = jnp.mean(x, axis=-1, keepdims=True)
    centred = x - mean
    rstd = lax.rsqrt(jnp.mean(centred * centred, axis=-1, keepdims=True) + EPSILON)
    return centred * rstd, rstd


def normal_back(hat, rstd, grad, gain):
    scaled = grad * gain
    lean = jnp.mean(scaled, axis=-1, keepdims=True)
    tilt = jnp.mean(scaled * hat, axis=-1, keepdims=True)
    back = rstd * (scaled - lean - hat * tilt)
    return back, jnp.sum(grad * hat, axis=0, keepdims=True), jnp.sum(grad, axis=0, keepdims=True)


GAIN, SHIFT, DOWN = 6, 9, 12


def lanes(shape):
    return lax.broadcasted_iota(jnp.int32, shape, len(shape) - 1)


def rows_of(shape):
    return lax.broadcasted_iota(jnp.int32, shape, 0)


def head_mask(head):
    return jnp.where(lanes((1, PAIR)) // HD == head, 1.0, 0.0).astype(LOW)


def thirds(x):
    one = x.astype(LOW).astype(FULL)
    two = (x - one).astype(LOW).astype(FULL)
    return one, two, x - one - two


def wide_keys(k, v, n):
    count = k.shape[0]
    shut = jnp.where((lanes((count, PAIR)) == 0) & (rows_of((count, PAIR)) >= n), NEGATIVE, 0.0).astype(LOW)
    ones = jnp.ones((count, PAIR), LOW)
    return [
        (jnp.concatenate([k * head_mask(h), shut], axis=1), jnp.concatenate([v * head_mask(h), ones], axis=1))
        for h in range(2)
    ]


def attend_pair(causal, tile, h, n, q, k, v, store, l_ref):
    queries, count = q.shape[0], k.shape[0]
    first = jnp.where(lanes((queries, PAIR)) == 0, 1.0, 0.0).astype(LOW)
    wide_q = jnp.concatenate([q, first], axis=1)
    spots = lanes((tile, PAIR))
    heads = wide_keys(k, v, n)
    for i in range(queries // tile):
        at = slice(i * tile, (i + 1) * tile)
        seen = (i + 1) * tile if causal else count
        mixed = jnp.zeros((tile, PAIR), FULL)
        kept = l_ref[at]
        for head, (keys, values) in enumerate(heads):
            scores = dot(wide_q[at], keys[:seen], NT)
            if causal:
                square = (tile, tile)
                last = jnp.where(lanes(square) <= rows_of(square), scores[:, seen - tile :], NEGATIVE)
                scores = last if seen == tile else jnp.concatenate([scores[:, : seen - tile], last], axis=1)
            top = jnp.max(scores, axis=1, keepdims=True)
            weights = jnp.exp(scores - top).astype(LOW)
            sums = dot(weights, values[:seen], NN)
            total = sums[:, PAIR:]
            mixed = mixed + sums[:, :PAIR] / total
            kept = jnp.where(spots == 2 * h + head, top + jnp.log(total), kept)
        store(at, mixed.astype(LOW))
        l_ref[at] = kept


def parts_of(value, heads, spare):
    lane = lanes(value.shape)
    shown = jnp.where(lane < heads, value, 0.0)
    shown = shown + pltpu.roll(shown, heads, 1) + pltpu.roll(shown, 2 * heads, 1)
    one, two, three = thirds(-shown)
    part = jnp.where(lane < heads, one, jnp.where(lane < 2 * heads, two, three))
    return jnp.where(lane == 3 * heads, spare, part).astype(LOW)


def take_part(head, heads):
    lane = lanes((1, PAIR))
    return jnp.where((lane < 3 * heads) & (lane % heads == head), 1.0, 0.0)


def forward_kernel(
    depth, ring, count, n_ref, m_ref, x_hbm, e_hbm, w_hbm, p_ref, shard, deal_ref, sent,
    full, arrived, a0_hbm, qkv_hbm, o0_hbm, l0_hbm, x1_hbm, a1_hbm, q1_hbm, kv_hbm, o1_hbm, l1_hbm,
    x_ref, e_ref, w_ref, a_ref, qkv_ref, o_ref, l0_ref, x1_ref, q1_ref, kv_ref, l1_ref, a1_ref, lp_ref, taken,
    w_sem, in_sem, out_sem, *sems,
):
    place = Place(depth, ring)
    place.greet_all()
    me = place.index()
    gather = Gather(place, count, shard, full, sems[:7], ahead=count)
    swap = Exchange(place, ((taken, arrived),), gather.steps() - 4, sems[7:])
    gather.begin()

    def advance(i):
        swap.step(i)
        gather.step(i)

    rows, width = x_ref.shape
    tile = 256
    load_x = pltpu.make_async_copy(x_hbm, x_ref, in_sem.at[0])
    load_e = pltpu.make_async_copy(e_hbm, e_ref, in_sem.at[1])
    load_x.start()
    parts = w_ref.shape[0]
    loads = [pltpu.make_async_copy(w_hbm.at[u], w_ref.at[u], w_sem.at[u]) for u in range(parts)]
    for load in loads[:3]:
        load.start()
    load_e.start()
    for load in loads[3:]:
        load.start()
    leaving = []

    def send(src, dst):
        copy = pltpu.make_async_copy(src, dst, out_sem.at[len(leaving)])
        copy.start()
        leaving.append(copy)

    take(deal_ref, [sent], [taken])
    swap.begin()
    l0_ref[...] = jnp.zeros_like(l0_ref)
    l1_ref[...] = jnp.zeros_like(l1_ref)
    load_x.wait()
    advance(0)
    for i in range(rows // tile):
        at = slice(i * tile, (i + 1) * tile)
        hat, _ = normal(x_ref[at].astype(FULL))
        a_ref[at] = (hat * p_ref[GAIN : GAIN + 1] + p_ref[SHIFT : SHIFT + 1]).astype(LOW)
    send(a_ref, a0_hbm)
    for j in range(3):
        loads[j].wait()
        bias = (p_ref[0:1], None, p_ref[1:2])[j]

        def project(i, j=j, bias=bias):
            at = pl.ds(pl.multiple_of(i * 2 * tile, 2 * tile), 2 * tile)
            y = dot(a_ref[at], w_ref[j], NN)
            if bias is not None:
                y = y + bias
            qkv_ref[j, at] = (y * SCALE if j == 0 else y).astype(LOW)

        loop(rows // (2 * tile), project)
        send(qkv_ref.at[j], qkv_hbm.at[j])
        if j == 1:
            advance(1)

    pairs = width // PAIR

    def self_pair(h):
        cols = pl.ds(pl.multiple_of(h * PAIR, PAIR), PAIR)

        def store(at, value):
            o_ref[at, cols] = value

        attend_pair(True, tile, h, n_ref[me], qkv_ref[0, :, cols], qkv_ref[1, :, cols], qkv_ref[2, :, cols], store, l0_ref)
        when(h % 2 == 0, lambda: advance(2 + h // 2))

    loop(pairs, self_pair)
    send(o_ref, o0_hbm)
    heads = 2 * pairs
    lp_ref[0] = parts_of(l0_ref[...], heads, 1.0)
    send(lp_ref.at[0], l0_hbm)
    done = 2 + (pairs + 1) // 2
    loads[3].wait()
    loads[4].wait()

    def middle_part(i):
        at = pl.ds(pl.multiple_of(i * tile, tile), tile)
        x1 = x_ref[at].astype(FULL) + (dot(o_ref[at], w_ref[3], NN) + p_ref[2:3])
        x1_ref[at] = x1
        hat, _ = normal(x1)
        a = (hat * p_ref[GAIN + 1 : GAIN + 2] + p_ref[SHIFT + 1 : SHIFT + 2]).astype(LOW)
        a1_ref[at] = a
        q1_ref[at] = ((dot(a, w_ref[4], NN) + p_ref[3:4]) * SCALE).astype(LOW)
        when(i % 2 == 1, lambda: advance(done + i // 2))

    loop(rows // tile, middle_part)
    done = done + rows // tile // 2
    send(x1_ref, x1_hbm)
    send(a1_ref, a1_hbm)
    send(q1_ref, q1_hbm.at[0])
    load_e.wait()
    for j in range(2):
        loads[5 + j].wait()
        y = dot(e_ref[...], w_ref[5 + j], NN)
        kv_ref[j] = (y + p_ref[4:5] if j == 1 else y).astype(LOW)
    send(kv_ref, kv_hbm)
    leaving[4].wait()

    def cross_pair(h):
        cols = pl.ds(pl.multiple_of(h * PAIR, PAIR), PAIR)

        def store(at, value):
            o_ref[at, cols] = value

        attend_pair(False, tile, h, m_ref[me], q1_ref[:, cols], kv_ref[0, :, cols], kv_ref[1, :, cols], store, l1_ref)
        when(h % 2 == 0, lambda: advance(done + h // 2))

    loop(pairs, cross_pair)
    done = done + (pairs + 1) // 2
    send(o_ref, o1_hbm)
    lp_ref[1] = parts_of(l1_ref[...], heads, 1.0)
    send(lp_ref.at[1], l1_hbm)
    for i in range(done, gather.steps()):
        advance(i)
    gather.finish()
    swap.finish()
    for k, copy in enumerate(leaving):
        if k != 4:
            copy.wait()


def forward(mesh, length, enc_count, x, memory, w, p, shards, deal, sent, ident):
    depth, ring = mesh.shape["dp"] // 2, mesh.shape["fsdp"]
    count = shards.shape[0]
    rows, width = x.shape
    enc = memory.shape[0]
    low = jax.ShapeDtypeStruct((rows, width), LOW)
    level = jax.ShapeDtypeStruct((rows, PAIR), LOW)
    out_shape = [
        jax.ShapeDtypeStruct((count, depth, 2, ring) + shards.shape[1:], LOW),
        jax.ShapeDtypeStruct(sent.shape, sent.dtype),
        low,
        jax.ShapeDtypeStruct((3, rows, width), LOW),
        low,
        level,
        jax.ShapeDtypeStruct((rows, width), FULL),
        low,
        jax.ShapeDtypeStruct((1, rows, width), LOW),
        jax.ShapeDtypeStruct((2, enc, width), LOW),
        low,
        level,
    ]
    big = pltpu.VMEM((rows, width), LOW)
    return pl.pallas_call(
        functools.partial(forward_kernel, depth, ring, count),
        out_shape=out_shape,
        in_specs=[SMEM, SMEM, ANY, ANY, ANY, VMEM, VMEM, SMEM, VMEM],
        out_specs=[ANY] * len(out_shape),
        scratch_shapes=[
            big,
            pltpu.VMEM((enc, width), LOW),
            pltpu.VMEM(w.shape, LOW),
            big,
            pltpu.VMEM((3, rows, width), LOW),
            big,
            pltpu.VMEM((rows, PAIR), FULL),
            pltpu.VMEM((rows, width), FULL),
            big,
            pltpu.VMEM((2, enc, width), LOW),
            pltpu.VMEM((rows, PAIR), FULL),
            big,
            pltpu.VMEM((2, rows, PAIR), LOW),
            pltpu.VMEM(sent.shape, sent.dtype),
            DMA((w.shape[0],)),
            DMA((2,)),
            DMA((12,)),
        ]
        + Gather.sems(mesh, count)
        + Exchange.sems(mesh, 1),
        compiler_params=remote_params(ident),
        cost_estimate=pl.CostEstimate(flops=70_000_000_000, bytes_accessed=2 * 33_554_432, transcendentals=0),
        name="forward_gather",
    )(length, enc_count, x, memory, w, p, shards, deal, sent)


def back_pair(causal, tile, h, heads, n, q, k, v, grad, level, inner, acc_ref, store):
    queries, count = q.shape[0], k.shape[0]
    acc_ref[...] = jnp.zeros_like(acc_ref)
    wide_q = jnp.concatenate([q, level], axis=1)
    wide_g = jnp.concatenate([grad, inner], axis=1)
    shut = jnp.where(rows_of((count, PAIR)) >= n, NEGATIVE, 0.0)
    both_heads = []
    for head in range(2):
        mask = head_mask(head)
        mine = take_part(2 * h + head, heads)
        open_k = jnp.where(lanes((count, PAIR)) == 3 * heads, shut, mine).astype(LOW)
        open_v = jnp.broadcast_to(mine, (count, PAIR)).astype(LOW)
        wide_k = jnp.concatenate([k * mask, open_k], axis=1)
        wide_v = jnp.concatenate([v * mask, open_v], axis=1)
        both_heads.append((wide_k, wide_v, q * mask, grad * mask, k * mask))
    for i in range(count // tile):
        at = slice(i * tile, (i + 1) * tile)
        low = i * tile if causal else 0
        grad_k = jnp.zeros((tile, PAIR), FULL)
        grad_v = jnp.zeros((tile, PAIR), FULL)
        for wide_k, wide_v, q_one, g_one, k_one in both_heads:
            scores = dot(wide_k[at], wide_q[low:], NT)
            if causal:
                square = (tile, tile)
                near = jnp.where(rows_of(square) <= lanes(square), scores[:, :tile], NEGATIVE)
                scores = near if low + tile == queries else jnp.concatenate([near, scores[:, tile:]], axis=1)
            probs = jnp.exp(scores)
            slope = (probs * dot(wide_v[at], wide_g[low:], NT)).astype(LOW)
            grad_v = grad_v + dot(probs.astype(LOW), g_one[low:], NN)
            grad_k = grad_k + dot(slope, q_one[low:], NN)
            acc_ref[low:] += dot(slope, k_one[at], TN)
        store(at, grad_k.astype(LOW), grad_v.astype(LOW))


def inner_parts(grad, mixed, heads):
    width = grad.shape[1]
    product = grad.astype(FULL) * mixed.astype(FULL)
    head = (rows_of((width, PAIR)) // HD == lanes((width, PAIR))).astype(FULL).astype(LOW)
    high = product.astype(LOW)
    rest = product - high.astype(FULL)
    return parts_of(dot(high, head, NN) + dot(rest.astype(LOW), head, NN), heads, 0.0)


def unit_grad(place, held, slot, a_ref, b_ref, scale):
    depth, part = held.shape[1], held.shape[3]
    width = a_ref.shape[1]
    piece = width // 2
    for m in range(2):
        value = dot(a_ref[:, m * piece : (m + 1) * piece], b_ref[...], TN)
        if scale is not None:
            value = value * scale
        value = value.astype(LOW)
        for k in range(piece // part):
            at = m * (piece // part) + k
            held[slot, at // 2, at % 2] = value[k * part : (k + 1) * part]


def back_scatter_kernel(
    depth, ring, n_ref, m_ref, a2_hbm, g3_hbm, du_hbm, r_hbm, qkv_hbm, q1_hbm, kv_hbm, do1_hbm, l1_ref, i1_ref,
    x1_hbm, dx2_hbm, o0_hbm, w_hbm, l0_ref, p_ref, sent,
    up_out, down_out, dq1_hbm, dkv1_hbm, dx1_hbm, g1_hbm, dq_hbm, dkv_hbm, arrived, sum_q, sum_out, sum_gain, sum_shift,
    kept_ref, moving, held, q_buf, acc_ref, dq_buf, dkv_buf, dq1_ref, kv_ref, dkv1_ref, w_ref,
    x1_buf, dx2_buf, o_buf, dx1_buf, g1_buf, i0_ref, up_ref,
    in_sem, move_sem, q_sem, out_sem, tile_in, tile_out, *rest,
):
    place = Place(depth, ring)
    place.greet_all()
    me = place.index()
    blocks = du_hbm.shape[0]
    count = 2 * blocks
    rows, width = do1_hbm.shape
    pairs = width // PAIR
    tile = x1_buf.shape[1]
    tiles = rows // tile

    own = up_out.shape[0]

    def put_sum(u, total):
        if u < blocks:
            up_ref[u] = total
        else:
            down_out[(u - blocks) * own : (u - blocks + 1) * own] = total

    def place_up():
        for k in range(width // own):
            lines = [up_ref[j, :, k * own : (k + 1) * own] for j in range(blocks)]
            up_out[:, k * blocks * own : (k + 1) * blocks * own] = jnp.concatenate(lines, axis=1)

    sums = Scatter(place, count, own, held, put_sum, rest[:5], rest[5:11])
    swap = Exchange(place, ((sent, arrived),), count, rest[11:])
    slots = held.shape[0]
    load_a = pltpu.make_async_copy(a2_hbm, kept_ref, in_sem.at[0])
    load_g = pltpu.make_async_copy(g3_hbm, kept_ref, in_sem.at[1])
    load_kv = pltpu.make_async_copy(kv_hbm, kv_ref, in_sem.at[2])
    load_w = [pltpu.make_async_copy(w_hbm.at[u], w_ref.at[k], in_sem.at[3 + k]) for k, u in enumerate((4, 3))]
    send_dq1 = pltpu.make_async_copy(dq1_ref, dq1_hbm, in_sem.at[5])
    send_dkv1 = pltpu.make_async_copy(dkv1_ref, dkv1_hbm, in_sem.at[6])

    def move(u):
        source = du_hbm.at[u] if u < blocks else r_hbm.at[u - blocks]
        return pltpu.make_async_copy(source, moving, move_sem.at[0])

    def columns(h):
        return pl.ds(pl.multiple_of(h * PAIR, PAIR), PAIR)

    def fetch_cross(h):
        cols = columns(h)
        sources = [q1_hbm.at[0, :, cols], do1_hbm.at[:, cols]]
        return [pltpu.make_async_copy(s, q_buf.at[h % 2, k], q_sem.at[h % 2, k]) for k, s in enumerate(sources)]

    def fetch(h):
        cols = columns(h)
        return [pltpu.make_async_copy(qkv_hbm.at[k, :, cols], q_buf.at[h % 2, k], q_sem.at[h % 2, k]) for k in range(3)]

    def put(h):
        cols = columns(h)
        return [
            pltpu.make_async_copy(dq_buf.at[h % 2], dq_hbm.at[:, cols], out_sem.at[h % 2, 0]),
            pltpu.make_async_copy(dkv_buf.at[h % 2], dkv_hbm.at[:, :, cols], out_sem.at[h % 2, 1]),
        ]

    def load_tile(i):
        at, b = slice(i * tile, (i + 1) * tile), i % 2
        sources = ((x1_hbm, x1_buf), (dx2_hbm, dx2_buf), (o0_hbm, o_buf))
        return [pltpu.make_async_copy(s.at[at], d.at[b], tile_in.at[b, k]) for k, (s, d) in enumerate(sources)]

    def store_tile(i):
        at = slice(i * tile, (i + 1) * tile)
        targets = ((dx1_buf, dx1_hbm), (g1_buf, g1_hbm))
        return [pltpu.make_async_copy(s, d.at[at], tile_out.at[k]) for k, (s, d) in enumerate(targets)]

    def start(copies):
        for copy in copies:
            copy.start()

    def wait(copies):
        for copy in copies:
            copy.wait()

    load_a.start()
    move(0).start()
    load_kv.start()
    start(fetch_cross(0))
    swap.begin()
    start(load_w)
    for ref in (sum_q, sum_out, sum_gain, sum_shift):
        ref[...] = jnp.zeros_like(ref)
    load_a.wait()

    def weights(i):
        if i == blocks:
            load_g.wait()
        move(i).wait()
        if i >= slots:
            sums.core(i - slots).wait_send()
        if i < blocks:
            unit_grad(place, held, i % slots, kept_ref, moving, None)
            if i == blocks - 1:
                load_g.start()
        else:
            unit_grad(place, held, i % slots, moving, kept_ref, None)
        if i + 1 < count:
            move(i + 1).start()
        sums.core(i).start()

    def cross_pair(h):
        pl.when(h + 1 < pairs)(lambda: start(fetch_cross(h + 1)))
        wait(fetch_cross(h))
        b, cols = h % 2, columns(h)

        def store(at, grad_k, grad_v):
            dkv1_ref[0, at, cols] = grad_k
            dkv1_ref[1, at, cols] = grad_v

        back_pair(False, kv_ref.shape[1], h, 2 * pairs, m_ref[me], q_buf[b, 0], kv_ref[0, :, cols], kv_ref[1, :, cols],
                  q_buf[b, 1], l1_ref[...], i1_ref[...], acc_ref, store)
        dq1_ref[:, cols] = acc_ref[...].astype(LOW)

    def between(i):
        at, b = slice(i * tile, (i + 1) * tile), i % 2
        if i + 1 < tiles:
            start(load_tile(i + 1))
        wait(load_tile(i))
        dq = dq1_ref[at]
        grad = dot(dq, w_ref[0], NT) * SCALE
        hat, rstd = normal(x1_buf[b])
        back, lines, shifts = normal_back(hat, rstd, grad, p_ref[GAIN + 1 : GAIN + 2])
        dx1 = dx2_buf[b] + back
        g1 = dx1.astype(LOW)
        if i > 0:
            wait(store_tile(i - 1))
        dx1_buf[...] = dx1
        g1_buf[...] = g1
        start(store_tile(i))
        grad_mixed = dot(g1, w_ref[1], NT).astype(LOW)
        dq1_ref[at] = grad_mixed
        i0_ref[at] = inner_parts(grad_mixed, o_buf[b], 2 * pairs)
        sum_q[...] += jnp.sum(dq.astype(FULL), axis=0, keepdims=True) * SCALE
        sum_out[...] += jnp.sum(g1.astype(FULL), axis=0, keepdims=True)
        sum_gain[...] += lines
        sum_shift[...] += shifts

    def self_pair(h):
        pl.when(h + 1 < pairs)(lambda: start(fetch(h + 1)))
        wait(fetch(h))
        pl.when(h >= 2)(lambda: wait(put(h - 2)))
        b, cols = h % 2, columns(h)

        def store(at, grad_k, grad_v):
            dkv_buf[b, 0, at] = grad_k
            dkv_buf[b, 1, at] = grad_v

        back_pair(True, 256, h, 2 * pairs, n_ref[me], q_buf[b, 0], q_buf[b, 1], q_buf[b, 2], dq1_ref[:, cols],
                  l0_ref[...], i0_ref[...], acc_ref, store)
        dq_buf[b] = acc_ref[...].astype(LOW)
        start(put(h))

    def run(part, low, high):
        loop(high - low, lambda j: part(low + j))

    def work(i):
        if i < 2:
            if i == 0:
                load_kv.wait()
            run(cross_pair, i * (pairs // 2), (i + 1) * (pairs // 2))
            if i == 1:
                send_dq1.start()
                send_dkv1.start()
                start(load_tile(0))
                start(fetch(0))
                wait(load_w)
        elif i < 4:
            if i == 2:
                send_dq1.wait()
            for j in range((i - 2) * tiles // 2, (i - 1) * tiles // 2):
                between(j)
            if i == 3:
                wait(store_tile(tiles - 1))
        else:
            run(self_pair, shares[i - 4], shares[i - 3])

    steps = sums.steps()
    left = steps - 4
    shares = [pairs - ((left - k) * pairs + left - 1) // left for k in range(left + 1)]
    for i in range(steps):
        if i < count:
            weights(i)
        sums.early(i)
        work(i)
        sums.late(i)
        swap.step(i)
    for h in range(pairs - 2, pairs):
        wait(put(h))
    send_dkv1.wait()
    sums.last_sums()
    place_up()
    sums.finish()
    swap.finish()


def back_scatter(mesh, length, enc_count, a2, g3, du, r, qkv, q1, kv1, do1, level1, inner1, x1, dx2, mixed0, w, level0, p, sent, ident):
    depth, ring = mesh.shape["dp"] // 2, mesh.shape["fsdp"]
    blocks, rows, width = du.shape
    own = width // (2 * depth * ring)
    count = 2 * blocks
    enc = kv1.shape[1]
    tile = 256
    big = pltpu.VMEM((rows, width), LOW)
    low = jax.ShapeDtypeStruct((rows, width), LOW)
    line = jax.ShapeDtypeStruct((1, width), FULL)
    return pl.pallas_call(
        functools.partial(back_scatter_kernel, depth, ring),
        out_shape=[
            jax.ShapeDtypeStruct((own, blocks * width), FULL),
            jax.ShapeDtypeStruct((blocks * own, width), FULL),
            low,
            jax.ShapeDtypeStruct((2, enc, width), LOW),
            jax.ShapeDtypeStruct((rows, width), FULL),
            low,
            low,
            jax.ShapeDtypeStruct((2, rows, width), LOW),
            jax.ShapeDtypeStruct(sent.shape, sent.dtype),
            line,
            line,
            line,
            line,
        ],
        in_specs=[SMEM, SMEM] + [ANY] * 8 + [VMEM, VMEM] + [ANY] * 4 + [VMEM, VMEM, ANY],
        out_specs=[VMEM] * 2 + [ANY] * 7 + [VMEM] * 4,
        scratch_shapes=[
            big,
            big,
            pltpu.VMEM((2, depth, 2, ring * own, width), LOW),
            pltpu.VMEM((2, 3, rows, PAIR), LOW),
            pltpu.VMEM((rows, PAIR), FULL),
            pltpu.VMEM((2, rows, PAIR), LOW),
            pltpu.VMEM((2, 2, rows, PAIR), LOW),
            big,
            pltpu.VMEM((2, enc, width), LOW),
            pltpu.VMEM((2, enc, width), LOW),
            pltpu.VMEM((2, width, width), LOW),
            pltpu.VMEM((2, tile, width), FULL),
            pltpu.VMEM((2, tile, width), FULL),
            pltpu.VMEM((2, tile, width), LOW),
            pltpu.VMEM((tile, width), FULL),
            pltpu.VMEM((tile, width), LOW),
            pltpu.VMEM((rows, PAIR), LOW),
            pltpu.VMEM((blocks, own, width), FULL),
            DMA((7,)),
            DMA((1,)),
            DMA((2, 3)),
            DMA((2, 2)),
            DMA((2, 3)),
            DMA((2,)),
        ]
        + Scatter.refs(mesh, count, own, width, LOW)
        + Scatter.sems(mesh, count)
        + Exchange.sems(mesh, 1),
        compiler_params=remote_params(ident),
        cost_estimate=pl.CostEstimate(flops=90_000_000_000, bytes_accessed=2 * 33_554_432, transcendentals=0),
        name="back_scatter",
    )(length, enc_count, a2, g3, du, r, qkv, q1, kv1, do1, level1, inner1, x1, dx2, mixed0, w, level0, p, sent)


def last_scatter_kernel(
    depth, ring, e_hbm, dkv1_hbm, w_hbm, x_hbm, dx1_hbm, o1_hbm, g2_hbm, a1_hbm, dq1_hbm, o0_hbm, g1_hbm, a0_hbm, dq0_hbm,
    dkv_hbm, p_ref, two_ref, three_ref, five_ref, down_ref, gain1_ref, gain2_ref, shift1_ref, shift2_ref, up_ref,
    s_qkv, s_out, c_qkv, c_out, tiny_out, arrived, arrived_e, sent, sent_e,
    left, right, held, tiny_held, e_ref, dkv1_ref, w_ref, de_ref, x_buf, dq_buf, dkv_buf, dx1_buf, dx_buf,
    sum_q, sum_v, sum_m, sum_gain, sum_shift, left_sem, right_sem, in_sem, w_sem, tile_in, tile_out, *rest,
):
    place = Place(depth, ring)
    place.greet_all()
    made = 2
    spots = [c_qkv.at[1], c_qkv.at[2], c_qkv.at[0], c_out, s_out, s_qkv.at[0], s_qkv.at[1], s_qkv.at[2]]
    own = s_out.shape[0]

    def put_sum(u, total):
        spots[u][...] = total

    def put_tiny(u, total):
        tiny_out[u] = total

    pairs = [(a1_hbm, dq1_hbm), (o1_hbm, g2_hbm), (o0_hbm, g1_hbm), (a0_hbm, dq0_hbm), (a0_hbm, dkv_hbm.at[0]), (a0_hbm, dkv_hbm.at[1])]
    scaled = (0, 3)
    count = made + len(pairs)
    small = Scatter(place, 1, tiny_out.shape[1], tiny_held, put_tiny, rest[:5], rest[5:11])
    sums = Scatter(place, count, own, held, put_sum, rest[11:16], rest[16:22])
    slots = held.shape[0]
    rows, width = x_hbm.shape
    tile = x_buf.shape[1]
    tiles = rows // tile
    begun = 3
    swap = Exchange(place, ((sent, arrived), (sent_e, arrived_e)), count - begun, rest[22:])
    leaves = dx_buf.shape[1]

    def load(k):
        a, b = pairs[k]
        return [
            pltpu.make_async_copy(a, left.at[k % 2], left_sem.at[k % 2]),
            pltpu.make_async_copy(b, right.at[k % 2], right_sem.at[k % 2]),
        ]

    def load_tile(i):
        at, b = slice(i * tile, (i + 1) * tile), i % 2
        sources = ((x_hbm.at[at], x_buf), (dq0_hbm.at[at], dq_buf), (dkv_hbm.at[:, at], dkv_buf), (dx1_hbm.at[at], dx1_buf))
        return [pltpu.make_async_copy(s, d.at[b], tile_in.at[b, k]) for k, (s, d) in enumerate(sources)]

    def store_tile(i):
        many = tile // leaves
        return pltpu.make_async_copy(dx_buf, sent.at[i * many : (i + 1) * many], tile_out.at[0])

    def start(copies):
        for copy in copies:
            copy.start()

    def wait(copies):
        for copy in copies:
            copy.wait()

    load_e = [pltpu.make_async_copy(e_hbm, e_ref, in_sem.at[0]), pltpu.make_async_copy(dkv1_hbm, dkv1_ref, in_sem.at[1])]
    load_m = [pltpu.make_async_copy(w_hbm.at[5 + j], w_ref.at[j], w_sem.at[j]) for j in range(2)]
    load_w = [pltpu.make_async_copy(w_hbm.at[j], w_ref.at[j], w_sem.at[j]) for j in range(3)]
    send_e = pltpu.make_async_copy(de_ref, sent_e, in_sem.at[2])
    start(load_e)
    start(load_m)
    start(load_tile(0))
    for k in range(2):
        start(load(k))
    tiny_held[...] = jnp.zeros_like(tiny_held)
    for ref in (sum_q, sum_v, sum_gain, sum_shift):
        ref[...] = jnp.zeros_like(ref)
    wait(load_e)

    def weights(i):
        if i >= slots:
            sums.core(i - slots).wait_send()
        if i < made:
            unit_grad(place, held, i % slots, e_ref, dkv1_ref.at[i], None)
        else:
            k = i - made
            wait(load(k))
            unit_grad(place, held, i % slots, left.at[k % 2], right.at[k % 2], SCALE if k in scaled else None)
            if k + 2 < len(pairs):
                start(load(k + 2))
        sums.core(i).start()

    def memory_back():
        wait(load_m)
        back = dot(dkv1_ref[0], w_ref[0], NT) + dot(dkv1_ref[1], w_ref[1], NT)
        de_ref[...] = back.astype(LOW).reshape(de_ref.shape)
        send_e.start()
        start(load_w)
        sum_m[...] = jnp.sum(dkv1_ref[1].astype(FULL), axis=0, keepdims=True)

    def part(i):
        b = i % 2
        if i + 1 < tiles:
            start(load_tile(i + 1))
        wait(load_tile(i))
        if i == 0:
            wait(load_w)
        dq = dq_buf[b]
        grad = dot(dq, w_ref[0], NT) * SCALE + dot(dkv_buf[b, 0], w_ref[1], NT) + dot(dkv_buf[b, 1], w_ref[2], NT)
        hat, rstd = normal(x_buf[b].astype(FULL))
        back, lines, shifts = normal_back(hat, rstd, grad, p_ref[GAIN : GAIN + 1])
        dx = (dx1_buf[b] + back).astype(LOW)
        if i > 0:
            store_tile(i - 1).wait()
        dx_buf[...] = dx.reshape(dx_buf.shape)
        store_tile(i).start()
        sum_q[...] += jnp.sum(dq.astype(FULL), axis=0, keepdims=True) * SCALE
        sum_v[...] += jnp.sum(dkv_buf[b, 1].astype(FULL), axis=0, keepdims=True)
        sum_gain[...] += lines
        sum_shift[...] += shifts

    def place_lines():
        made_here = [sum_q, sum_v, two_ref, three_ref, sum_m, five_ref, down_ref]
        made_here += [sum_gain, gain1_ref, gain2_ref, sum_shift, shift1_ref, shift2_ref]
        made_here = [(ref, 0) for ref in made_here]
        made_here += [(up_ref, j * width) for j in range(up_ref.shape[1] // width)]
        for line, (ref, low) in enumerate(made_here):
            row, lane = line * own // 128, line * own % 128
            for k in range(width // own):
                d, g = k // ring, k % ring
                at = g * tiny_out.shape[1] + row
                tiny_held[0, d // 2, d % 2, at : at + 1, lane : lane + own] = ref[:, low + k * own : low + (k + 1) * own]

    def work(i):
        if i == 0:
            memory_back()
        elif i == 1:
            for j in range(tiles // 2):
                part(j)
        elif i == 2:
            for j in range(tiles // 2, tiles):
                part(j)
            store_tile(tiles - 1).wait()
            send_e.wait()
            swap.begin()
            place_lines()
            small.core(0).start()

    for i in range(sums.steps()):
        if i < count:
            weights(i)
        sums.early(i)
        if 0 <= i - begun < small.steps():
            small.early(i - begun)
        work(i)
        sums.late(i)
        if 0 <= i - begun < small.steps():
            small.late(i - begun)
        if i >= begun - 1:
            swap.step(i - begun + 1)
    small.last_sums()
    sums.last_sums()
    small.finish()
    sums.finish()
    swap.finish()


def last_scatter(mesh, memory, dkv1, w, x, dx1, pairs, p, lines, like, like_e, ident):
    depth, ring = mesh.shape["dp"] // 2, mesh.shape["fsdp"]
    rows, width = x.shape
    enc = memory.shape[0]
    own = width // (2 * depth * ring)
    count = 8
    tile = 256
    numbers = 13 * own + lines[-1].shape[1] * own // width
    tiny_rows = -(-numbers // 1024) * 8
    tiny = jax.ShapeDtypeStruct((depth, 2, ring * tiny_rows, 128), FULL)
    line = pltpu.VMEM((1, width), FULL)
    moved = [jax.ShapeDtypeStruct(like, LOW), jax.ShapeDtypeStruct(like_e, LOW)]
    return pl.pallas_call(
        functools.partial(last_scatter_kernel, depth, ring),
        out_shape=[
            jax.ShapeDtypeStruct((3, own, width), FULL),
            jax.ShapeDtypeStruct((own, width), FULL),
            jax.ShapeDtypeStruct((3, own, width), FULL),
            jax.ShapeDtypeStruct((own, width), FULL),
            jax.ShapeDtypeStruct((1, tiny_rows, tiny.shape[3]), FULL),
        ]
        + moved
        + moved,
        in_specs=[ANY] * (5 + len(pairs)) + [VMEM] * (1 + len(lines)),
        out_specs=[VMEM] * 5 + [ANY] * 4,
        scratch_shapes=[
            pltpu.VMEM((2, rows, width), LOW),
            pltpu.VMEM((2, rows, width), LOW),
            pltpu.VMEM((2, depth, 2, ring * own, width), LOW),
            pltpu.VMEM((1,) + tiny.shape, FULL),
            pltpu.VMEM((enc, width), LOW),
            pltpu.VMEM((2, enc, width), LOW),
            pltpu.VMEM((3, width, width), LOW),
            pltpu.VMEM(like_e, LOW),
            pltpu.VMEM((2, tile, width), LOW),
            pltpu.VMEM((2, tile, width), LOW),
            pltpu.VMEM((2, 2, tile, width), LOW),
            pltpu.VMEM((2, tile, width), FULL),
            pltpu.VMEM((tile // like[1],) + like[1:], LOW),
            line,
            line,
            line,
            line,
            line,
            DMA((2,)),
            DMA((2,)),
            DMA((3,)),
            DMA((3,)),
            DMA((2, 4)),
            DMA((1,)),
        ]
        + Scatter.refs(mesh, 1, tiny_rows, tiny.shape[3], FULL)
        + Scatter.sems(mesh, 1)
        + Scatter.refs(mesh, count, own, width, LOW)
        + Scatter.sems(mesh, count)
        + Exchange.sems(mesh, 2),
        compiler_params=remote_params(ident),
        cost_estimate=pl.CostEstimate(flops=60_000_000_000, bytes_accessed=2 * 33_554_432, transcendentals=0),
        name="last_scatter",
    )(memory, dkv1, w, x, dx1, *pairs, p, *lines)


CUBIC = 0.044715
ROOT = 0.7978845608028654


def feed_kernel(
    n_ref, x1_ref, o_ref, g_ref, w_hbm, p_ref, bu_ref,
    out_ref, r_ref, du_ref, a_ref, g3_ref, dx_ref, g2_ref, do_ref, inner_ref,
    sum_up, sum_down, sum_five, sum_gain, sum_shift,
    w_ref, slope_ref, sems,
):
    i = pl.program_id(0)
    first = i == 0
    tile, width = x1_ref.shape
    blocks = (w_hbm.shape[0] - 1) // 2
    order = [0] + [k * blocks + j + 1 for j in range(blocks) for k in range(2)]
    loads = {u: pltpu.make_async_copy(w_hbm.at[u], w_ref.at[u], sems.at[u]) for u in order}

    @pl.when(first)
    def _():
        for u in order:
            loads[u].start()
        for ref in (sum_up, sum_down, sum_five, sum_gain, sum_shift):
            ref[...] = jnp.zeros_like(ref)
        loads[0].wait()

    valid = jnp.where(i * tile + rows_of((tile, 1)) < n_ref[lax.axis_index(AXES)], 1.0, 0.0)
    x2 = x1_ref[...] + (dot(o_ref[...], w_ref[0], NN) + p_ref[5:6])
    hat, rstd = normal(x2)
    gain = p_ref[GAIN + 2 : GAIN + 3]
    a_ref[...] = (hat * gain + p_ref[SHIFT + 2 : SHIFT + 3]).astype(LOW)

    @pl.when(first)
    def _():
        for u in order[1:]:
            loads[u].wait()

    total = x2 + p_ref[DOWN : DOWN + 1]
    for j in range(blocks):
        cols = slice(j * width, (j + 1) * width)
        u = dot(a_ref[...], w_ref[1 + j], NN) + bu_ref[:, cols]
        square = u * u
        t = jnp.tanh(ROOT * (u * (1.0 + CUBIC * square)))
        half = 0.5 * (1.0 + t)
        r = (u * half).astype(LOW)
        r_ref[j] = r
        slope = half + 0.5 * u * (1.0 - t * t) * (ROOT * (1.0 + 3.0 * CUBIC * square))
        slope_ref[:, cols] = slope.astype(LOW)
        total = total + dot(r, w_ref[1 + blocks + j], NN)
    out_ref[...] = (total * valid).astype(LOW)
    grad_out = g_ref[...].astype(FULL) * valid
    g3 = grad_out.astype(LOW)
    g3_ref[...] = g3
    grad = jnp.zeros((tile, width), FULL)
    for j in range(blocks):
        cols = slice(j * width, (j + 1) * width)
        du = (dot(g3, w_ref[1 + blocks + j], NT) * slope_ref[:, cols].astype(FULL)).astype(LOW)
        du_ref[j] = du
        line = jnp.sum(du.astype(FULL), axis=0, keepdims=True)

        sum_up[:, cols] += line
        grad = grad + dot(du, w_ref[1 + j], NT)
    back, lines, shifts = normal_back(hat, rstd, grad, gain)
    dx2 = grad_out + back
    dx_ref[...] = dx2
    g2 = dx2.astype(LOW)
    g2_ref[...] = g2
    grad_mixed = dot(g2, w_ref[0], NT).astype(LOW)
    do_ref[...] = grad_mixed
    inner_ref[...] = inner_parts(grad_mixed, o_ref[...], width // HD)
    sum_down[...] += jnp.sum(g3.astype(FULL), axis=0, keepdims=True)
    sum_five[...] += jnp.sum(g2.astype(FULL), axis=0, keepdims=True)
    sum_gain[...] += lines
    sum_shift[...] += shifts


def feed(length, x1, mixed, cotangent, w, p, bias_up, tile=256):
    rows, width = x1.shape
    blocks = (w.shape[0] - 1) // 2
    inner = blocks * width
    part = pl.BlockSpec((tile, width), lambda i: (i, 0))
    broad = pl.BlockSpec((blocks, tile, width), lambda i: (0, i, 0))
    thin = pl.BlockSpec((tile, PAIR), lambda i: (i, 0))
    low = jax.ShapeDtypeStruct((rows, width), LOW)
    wide = jax.ShapeDtypeStruct((blocks, rows, width), LOW)
    line = jax.ShapeDtypeStruct((1, width), FULL)
    return calls(
        feed_kernel,
        "feed",
        2 * rows * width * (4 * inner + 2 * width),
        2 * rows * (9 * width + 2 * inner) + 4 * inner * width,
        grid=(rows // tile,),
        in_specs=[SMEM, part, part, part, ANY, whole(p.shape), whole(bias_up.shape)],
        out_specs=[part, broad, broad, part, part, part, part, part, thin, whole((1, inner))] + [whole((1, width))] * 4,
        out_shape=[low, wide, wide, low, low, jax.ShapeDtypeStruct((rows, width), FULL), low, low,
                   jax.ShapeDtypeStruct((rows, PAIR), LOW), jax.ShapeDtypeStruct((1, inner), FULL), line, line, line, line],
        scratch_shapes=[pltpu.VMEM(w.shape, LOW), pltpu.VMEM((tile, inner), LOW), DMA((w.shape[0],))],
    )(length, x1, mixed, cotangent, w, p, bias_up)


AXES = ("dp", "fsdp")


def per_device(
    mesh,
    units,
    encoder,
    cotangent,
    deal,
    lengths,
    enc_counts,
    self_qkv,
    self_out,
    cross_qkv,
    cross_out,
    ffn_up,
    ffn_down,
    biases,
    ffn_bias_up,
    ffn_bias_down,
    norm_gain,
    norm_shift,
):
    slots = deal.shape[0]
    depth, ring = mesh.shape["dp"] // 2, mesh.shape["fsdp"]
    own, width = self_out.shape
    blocks = ffn_up.shape[1] // width
    up = ffn_up.reshape(own, slots, blocks, own).transpose(2, 0, 1, 3).reshape(blocks, own, width)
    late = jnp.concatenate([cross_out[None], up, ffn_down.reshape(blocks, own, width)])
    rows = jnp.concatenate([biases, norm_gain, norm_shift, ffn_bias_down[None]])
    flat = jnp.concatenate([rows.reshape(-1), ffn_bias_up])
    size = -(-flat.shape[0] // 2048) * 2048
    little = jnp.pad(flat, (0, size - flat.shape[0])).reshape(1, size // 128, 128)
    w_one, little, x, memory = first_gather(mesh, deal, [self_qkv, self_out, cross_qkv], little, [units, encoder], 0)
    w_one = w_one.reshape(-1, width, width)
    x, memory = x.reshape(-1, width), memory.reshape(-1, width)
    flat = little.reshape(slots, size).astype(FULL)
    p = flat[:, : rows.size].reshape((slots,) + rows.shape)
    p = jnp.moveaxis(p, 0, 1).reshape(rows.shape[0], -1)
    p = jnp.pad(p, ((0, 16 - rows.shape[0]), (0, 0)))
    bias_up = flat[:, rows.size : rows.size + ffn_bias_up.size].reshape(slots, blocks, own)
    bias_up = bias_up.transpose(1, 0, 2).reshape(1, -1)

    w_two, cot, a0, qkv, mixed0, level0, x1, a1, q1, kv1, mixed1, level1 = forward(
        mesh, lengths, enc_counts, x, memory, w_one, p, late, deal, cotangent, 1
    )
    cot = cot.reshape(-1, width)
    w_two = w_two.reshape(late.shape[0], width, width)
    (result, r, du, a2, g3, dx2, g2, grad_mixed1, inner1, bias_up_grad, bias_down_grad, bias_five, gain_two, shift_two) = feed(
        lengths, x1, mixed1, cot, w_two, p, bias_up
    )
    up_sum, down_sum, dq1, dkv1, dx1, g1, dq0, dkv0, result, bias_three, bias_two, gain_one, shift_one = back_scatter(
        mesh, lengths, enc_counts, a2, g3, du, r, qkv, q1, kv1, grad_mixed1, level1, inner1, x1, dx2, mixed0, w_one, level0, p,
        result.reshape(slots, -1, width), 2,
    )
    lines = (bias_two, bias_three, bias_five, bias_down_grad, gain_one, gain_two, shift_one, shift_two, bias_up_grad)
    pairs = (mixed1, g2, a1, dq1, mixed0, g1, a0, dq0, dkv0)
    self_qkv_sum, self_out_sum, cross_qkv_sum, cross_out_sum, tiny_sums, dx, grad_memory = last_scatter(
        mesh, memory, dkv1, w_one, x, dx1, pairs, p, lines, units.shape, encoder.shape, 3
    )[:7]
    result, dx, grad_memory = deal_blocks(deal, [result, dx, grad_memory], True, "deal_out")
    flat = tiny_sums.reshape(-1)
    lines = flat[: 13 * own].reshape(13, own)
    return (
        result,
        dx,
        grad_memory,
        self_qkv_sum,
        self_out_sum,
        cross_qkv_sum,
        cross_out_sum,
        up_sum,
        down_sum,
        lines[:6],
        flat[13 * own : 13 * own + ffn_bias_up.size],
        lines[6],
        lines[7:10],
        lines[10:13],
    )


def solution(mesh):
    middle_rows = P(None, AXES, None)
    first_rows = P(AXES, None)
    last = P(None, AXES)
    weights = (middle_rows, first_rows, middle_rows, first_rows, first_rows, first_rows, last, P(AXES), P(AXES), last, last)
    return jax.shard_map(
        functools.partial(per_device, mesh),
        mesh=mesh,
        in_specs=(middle_rows,) * 3 + (P(),) * 3 + weights,
        out_specs=(middle_rows,) * 3 + weights,
        check_vma=False,
    )
```
